32 devices in a mesh: seq: 4 (over y, x), res: 8 (over z, core).
Axes of the slice: x: 2, y: 2, z: 4, core: 2. Of those that a mesh axis runs over, the one named last changes fastest.
Arguments:
- alignment: bfloat16 [256, 64, 256], P(('seq', 'res')), may hold values from -6 to 6
- layer_norm_gain: float32 [256], replicated, may hold values from 0.1 to 1.9
- layer_norm_bias: float32 [256], replicated, may hold values from -0.6 to 0.6
- left_projection_weight: bfloat16 [256, 32], replicated, may hold values from -0.375 to 0.375
- left_bias: float32 [32], replicated, may hold values from -0.6 to 0.6
- right_projection_weight: bfloat16 [256, 32], replicated, may hold values from -0.375 to 0.375
- right_bias: float32 [32], replicated, may hold values from -0.6 to 0.6
- out_weight: bfloat16 [1024, 128], replicated, may hold values from -6 to 6
- out_bias: float32 [128], replicated, may hold values from -3 to 3
Outputs:
- pair_update: bfloat16 [64, 64, 128], P('res', 'seq')
The draws below stay inside these ranges and needn't reach their ends.
All inputs are finite; a program needn't handle non-finite values.
Results may differ from the reference program's by a relative error of at most 0.022.
Values may be sent and summed in bfloat16 or wider, within the bound.
No kernel may reach another device: no remote copies, remote signals or barrier semaphores. Data moves between devices by JAX's collectives and lax.ppermute only.
A program may use at most 64 MiB of HBM per device.

```python
import jax
import jax.numpy as jnp
from jax import lax

ALIGN_CHANNELS = 256
OUTER_CHANNELS = 32
PAIR_CH = 128
SEQ_DEV = 64
RES_DEV = 8
SEQUENCE_COUNT = 256
RESIDUE_COUNT = 64
N_SEQ = 4
N_RES = 8


def shard_levels(stream_key, shape, split, low, high):
    factor_of, own = 1.0, jax.random.fold_in(stream_key, 6)
    for axis_at, shards_of in split:
        draws = jnp.exp(jax.random.uniform(jax.random.fold_in(own, axis_at), (shards_of,), jnp.float32, low / len(split), high / len(split)))
        factor_of = factor_of * jnp.repeat(draws, shape[axis_at] // shards_of).reshape([-1 if axis == axis_at else 1 for axis in range(len(shape))])
    return factor_of


def noise(rng, extent, deviation, limit, cuts=(), kind=jnp.bfloat16):
    drawn = jax.random.normal(rng, extent, jnp.float32) * deviation
    if len(cuts) > 0:
        drawn = shard_levels(rng, extent, cuts, -0.22, 0.18) * drawn
    return jnp.clip(drawn, min=-limit, max=limit).astype(kind)


def setup_inputs(seed: int = 0) -> dict:
    keys = jax.random.split(jax.random.key(seed), 10)
    alignment = noise(keys[0], (SEQUENCE_COUNT, RESIDUE_COUNT, ALIGN_CHANNELS), 1.0, 6.0, ((0, 32),))
    layer_norm_gain = jnp.clip(1.0 + 0.18 * jax.random.normal(keys[1], (ALIGN_CHANNELS,), jnp.float32), 0.1, 1.9)
    layer_norm_bias = noise(keys[2], (ALIGN_CHANNELS,), 0.1, 0.6, (), jnp.float32)
    left_projection_weight = noise(keys[3], (ALIGN_CHANNELS, OUTER_CHANNELS), ALIGN_CHANNELS ** -0.5, 0.375)
    left_bias = noise(keys[4], (OUTER_CHANNELS,), 0.1, 0.6, (), jnp.float32)
    right_projection_weight = noise(keys[5], (ALIGN_CHANNELS, OUTER_CHANNELS), ALIGN_CHANNELS ** -0.5, 0.375)
    right_bias = noise(keys[6], (OUTER_CHANNELS,), 0.1, 0.6, (), jnp.float32)
    out_weight = noise(keys[7], (OUTER_CHANNELS * OUTER_CHANNELS, PAIR_CH), 1.0, 6.0)
    out_bias = noise(keys[8], (PAIR_CH,), 0.5, 3.0, (), jnp.float32)
    return {"alignment": alignment, "layer_norm_gain": layer_norm_gain, "layer_norm_bias": layer_norm_bias, "left_projection_weight": left_projection_weight, "left_bias": left_bias, "right_projection_weight": right_projection_weight, "right_bias": right_bias, "out_weight": out_weight, "out_bias": out_bias}


def normalize_project(alignment, layer_norm_gain, layer_norm_bias, weight, bias):
    values = alignment.astype(jnp.float32)
    centre = lax.optimization_barrier(jnp.mean(values, axis=-1, keepdims=True))
    spread = lax.optimization_barrier(jnp.mean((values - centre) ** 2, axis=-1, keepdims=True))
    normed = ((values - centre) * lax.rsqrt(spread + 1e-05) * layer_norm_gain + layer_norm_bias).astype(jnp.bfloat16)
    flat = normed.reshape(-1, normed.shape[-1])
    result = jnp.dot(flat, weight, preferred_element_type=jnp.float32) + bias
    return result.astype(jnp.bfloat16).reshape(normed.shape[:-1] + (weight.shape[1],))

def reference(alignment, layer_norm_gain, layer_norm_bias, left_projection_weight, left_bias, right_projection_weight, right_bias, out_weight, out_bias):
    left_proj = normalize_project(alignment, layer_norm_gain, layer_norm_bias, left_projection_weight, left_bias)
    right_proj = normalize_project(alignment, layer_norm_gain, layer_norm_bias, right_projection_weight, right_bias)
    seq_total = alignment.shape[0]
    res_total = alignment.shape[1]
    hidden_width = left_projection_weight.shape[1]
    left_groups = left_proj.reshape(N_SEQ, SEQ_DEV, res_total, hidden_width)
    right_groups = right_proj.reshape(N_SEQ, SEQ_DEV, res_total, hidden_width)

    def one_block(block_index):
        left_rows = lax.dynamic_slice_in_dim(left_groups, (block_index * RES_DEV).astype(jnp.int32), RES_DEV, 2)

        def add_group(running, pair_in):
            left_part, right_part = pair_in
            outer_block = jnp.einsum('sic,sjd->ijcd', left_part.astype(jnp.float32), right_part.astype(jnp.float32)) / float(seq_total)
            outer_block = outer_block.astype(jnp.bfloat16).reshape(RES_DEV * res_total, hidden_width * hidden_width)
            term_block = jnp.dot(outer_block, out_weight, preferred_element_type=jnp.float32)
            return (running + term_block.reshape(RES_DEV, res_total, -1), None)
        start_value = jnp.zeros((RES_DEV, res_total, out_weight.shape[1]), jnp.float32)
        running, unused = lax.scan(add_group, start_value, (left_rows, right_groups))
        return (running + out_bias).astype(jnp.bfloat16)
    blocks = lax.map(one_block, jnp.arange(N_RES, dtype=jnp.int32))
    return blocks.reshape(res_total, res_total, out_weight.shape[1])
```

```python
import functools

import jax
import jax.numpy as jnp
from jax import lax
from jax.experimental import pallas as pl
from jax.experimental.pallas import tpu as pltpu
from jax.sharding import PartitionSpec as P

LANES = 128


def project_kernel(
    seq_count,
    res_count,
    align_ref,
    gain_ref,
    offset_ref,
    left_w_ref,
    left_b_ref,
    right_w_ref,
    right_b_ref,
    send_ref,
    proj_ref,
):
    rows, res_total, chan = align_ref.shape
    hidden = left_w_ref.shape[0]
    values = align_ref[...].astype(jnp.float32).reshape(rows * res_total, chan)
    centred = values - jnp.mean(values, axis=-1, keepdims=True)
    spread = jnp.mean(centred * centred, axis=-1, keepdims=True)
    normed = centred * lax.rsqrt(spread + 1e-05) * gain_ref[...] + offset_ref[...]
    weights = jnp.concatenate([left_w_ref[...], right_w_ref[...]], axis=0)
    biases = jnp.concatenate([left_b_ref[...], right_b_ref[...]], axis=1)
    proj_ref[:, : 2 * hidden] = (
        lax.dot_general(
            normed.astype(jnp.bfloat16),
            weights,
            (((1,), (1,)), ((), ())),
            preferred_element_type=jnp.float32,
        )
        + biases
    )
    tiles = [proj_ref[pl.ds(r, rows, stride=res_total), :][:, : 2 * hidden] for r in range(res_total)]
    row_block = res_total // res_count
    col_block = res_total // seq_count
    left = [
        jnp.concatenate([t[:, :hidden] for t in tiles[a * row_block : (a + 1) * row_block]], axis=1)
        for a in range(res_count)
    ]
    right = [
        jnp.concatenate([t[:, hidden:] for t in tiles[b * col_block : (b + 1) * col_block]], axis=1)
        for b in range(seq_count)
    ]
    pieces = [
        jnp.concatenate([left[a], right[b]], axis=1)
        for b in range(seq_count)
        for a in range(res_count)
    ]
    group = max(1, 16 // rows)
    for start in range(0, len(pieces), group):
        block = jnp.concatenate(pieces[start : start + group], axis=0)
        send_ref[pl.ds(start * rows, group * rows), :] = block.astype(jnp.bfloat16)


def pair_kernel(hidden, row_block, col_block, recv_ref, weight_ref, bias_ref, out_ref, outer_ref, term_ref):
    seq_total = recv_ref.shape[0]
    left = recv_ref[:, : row_block * hidden]
    right = recv_ref[:, row_block * hidden :]
    outer = lax.dot_general(
        left, right, (((0,), (0,)), ((), ())), preferred_element_type=jnp.float32
    )
    for g in range(outer_ref.shape[0]):
        outer_ref[g] = outer[:, g * LANES : (g + 1) * LANES]
    per_group = LANES // hidden
    terms = []
    for g in range(outer_ref.shape[0]):
        slabs = [outer_ref[g, pl.ds(c, row_block, stride=hidden), :] for c in range(hidden)]
        for j in range(per_group):
            flat = jnp.concatenate([s[:, j * hidden : (j + 1) * hidden] for s in slabs], axis=1)
            terms.append(flat)
    flat = jnp.concatenate(terms, axis=0).astype(jnp.bfloat16)
    term = jnp.dot(flat, weight_ref[...], preferred_element_type=jnp.float32)
    term_ref[...] = term * (1.0 / float(seq_total)) + bias_ref[...]
    for i in range(row_block):
        out_ref[i] = term_ref[pl.ds(i, col_block, stride=row_block), :].astype(jnp.bfloat16)


def body(
    alignment,
    layer_norm_gain,
    layer_norm_bias,
    left_projection_weight,
    left_bias,
    right_projection_weight,
    right_bias,
    out_weight,
    out_bias,
):
    res_count = lax.axis_size("res")
    seq_count = lax.axis_size("seq")
    rows, res_total, chan = alignment.shape
    hidden = left_projection_weight.shape[1]
    pair_width = out_weight.shape[1]
    row_block = res_total // res_count
    col_block = res_total // seq_count
    device_count = seq_count * res_count
    width = (row_block + col_block) * hidden
    vmem = pl.BlockSpec(memory_space=pltpu.VMEM)
    send = pl.pallas_call(
        functools.partial(project_kernel, seq_count, res_count),
        out_shape=jax.ShapeDtypeStruct((device_count * rows, width), jnp.bfloat16),
        in_specs=[vmem] * 7,
        out_specs=vmem,
        scratch_shapes=[pltpu.VMEM((rows * res_total, LANES), jnp.float32)],
        compiler_params=pltpu.CompilerParams(vmem_limit_bytes=32 * 1024 * 1024),
    )(
        alignment,
        layer_norm_gain.reshape(1, chan),
        layer_norm_bias.reshape(1, chan),
        left_projection_weight.T,
        left_bias.reshape(1, hidden),
        right_projection_weight.T,
        right_bias.reshape(1, hidden),
    )
    recv = lax.all_to_all(send, ("seq", "res"), split_axis=0, concat_axis=0, tiled=True)
    return pl.pallas_call(
        functools.partial(pair_kernel, hidden, row_block, col_block),
        out_shape=jax.ShapeDtypeStruct((row_block, col_block, pair_width), jnp.bfloat16),
        in_specs=[vmem] * 3,
        out_specs=vmem,
        scratch_shapes=[
            pltpu.VMEM((col_block * hidden // LANES, row_block * hidden, LANES), jnp.float32),
            pltpu.VMEM((row_block * col_block, pair_width), jnp.float32),
        ],
        compiler_params=pltpu.CompilerParams(vmem_limit_bytes=32 * 1024 * 1024),
    )(recv, out_weight, out_bias.reshape(1, pair_width))


def solution(mesh):
    in_specs = (P(("seq", "res"), None, None), P(), P(), P(), P(), P(), P(), P(), P())
    out_specs = P("res", "seq", None)
    return jax.shard_map(body, mesh=mesh, in_specs=in_specs, out_specs=out_specs, check_vma=False)
```

```python
import functools

import jax
import jax.numpy as jnp
from jax import lax
from jax.experimental import pallas as pl
from jax.experimental.pallas import tpu as pltpu
from jax.sharding import PartitionSpec as P

LANES = 128


def project_kernel(
    seq_count,
    res_count,
    align_hbm,
    gain_hbm,
    offset_hbm,
    left_w_hbm,
    left_b_hbm,
    right_w_hbm,
    right_b_hbm,
    send_ref,
    align_ref,
    gain_ref,
    offset_ref,
    left_w_ref,
    left_b_ref,
    right_w_ref,
    right_b_ref,
    proj_ref,
    sems,
):
    copies = [
        pltpu.make_async_copy(source, target, sems.at[n])
        for n, (source, target) in enumerate(
            [
                (align_hbm, align_ref),
                (gain_hbm, gain_ref),
                (offset_hbm, offset_ref),
                (left_w_hbm, left_w_ref),
                (left_b_hbm, left_b_ref),
                (right_w_hbm, right_w_ref),
                (right_b_hbm, right_b_ref),
            ]
        )
    ]
    for copy in copies:
        copy.start()
    for copy in copies:
        copy.wait()
    rows, res_total, chan = align_ref.shape
    hidden = left_w_ref.shape[0]
    values = align_ref[...].astype(jnp.float32).reshape(rows * res_total, chan)
    centred = values - jnp.mean(values, axis=-1, keepdims=True)
    spread = jnp.mean(centred * centred, axis=-1, keepdims=True)
    normed = centred * lax.rsqrt(spread + 1e-05) * gain_ref[...] + offset_ref[...]
    weights = jnp.concatenate([left_w_ref[...], right_w_ref[...]], axis=0)
    biases = jnp.concatenate([left_b_ref[...], right_b_ref[...]], axis=1)
    proj_ref[:, : 2 * hidden] = (
        lax.dot_general(
            normed.astype(jnp.bfloat16),
            weights,
            (((1,), (1,)), ((), ())),
            preferred_element_type=jnp.float32,
        )
        + biases
    )
    tiles = [proj_ref[pl.ds(r, rows, stride=res_total), :][:, : 2 * hidden] for r in range(res_total)]
    row_block = res_total // res_count
    col_block = res_total // seq_count
    left = [
        jnp.concatenate([t[:, :hidden] for t in tiles[a * row_block : (a + 1) * row_block]], axis=1)
        for a in range(res_count)
    ]
    right = [
        jnp.concatenate([t[:, hidden:] for t in tiles[b * col_block : (b + 1) * col_block]], axis=1)
        for b in range(seq_count)
    ]
    pieces = [
        jnp.concatenate([left[a], right[b]], axis=1)
        for b in range(seq_count)
        for a in range(res_count)
    ]
    group = max(1, 16 // rows)
    for start in range(0, len(pieces), group):
        block = jnp.concatenate(pieces[start : start + group], axis=0)
        send_ref[pl.ds(start * rows, group * rows), :] = block.astype(jnp.bfloat16)


def pair_kernel(
    hidden,
    row_block,
    col_block,
    recv_ref,
    weight_ref,
    bias_hbm,
    out_ref,
    bias_ref,
    outer_ref,
    term_ref,
    sem,
):
    bias_copy = pltpu.make_async_copy(bias_hbm, bias_ref, sem)
    bias_copy.start()
    seq_total = recv_ref.shape[0]
    left = recv_ref[:, : row_block * hidden]
    right = recv_ref[:, row_block * hidden :]
    outer = lax.dot_general(
        left, right, (((0,), (0,)), ((), ())), preferred_element_type=jnp.float32
    )
    for g in range(outer_ref.shape[0]):
        outer_ref[g] = outer[:, g * LANES : (g + 1) * LANES]
    per_group = LANES // hidden
    terms = []
    for g in range(outer_ref.shape[0]):
        slabs = [outer_ref[g, pl.ds(c, row_block, stride=hidden), :] for c in range(hidden)]
        for j in range(per_group):
            flat = jnp.concatenate([s[:, j * hidden : (j + 1) * hidden] for s in slabs], axis=1)
            terms.append(flat)
    flat = jnp.concatenate(terms, axis=0).astype(jnp.bfloat16)
    term = jnp.dot(flat, weight_ref[...], preferred_element_type=jnp.float32)
    bias_copy.wait()
    term_ref[...] = term * (1.0 / float(seq_total)) + bias_ref[...]
    for i in range(row_block):
        out_ref[i] = term_ref[pl.ds(i, col_block, stride=row_block), :].astype(jnp.bfloat16)


def in_hbm(array):
    return pltpu.with_memory_space_constraint(array, pltpu.HBM)


def body(
    alignment,
    layer_norm_gain,
    layer_norm_bias,
    left_projection_weight,
    left_bias,
    right_projection_weight,
    right_bias,
    out_weight,
    out_bias,
):
    res_count = lax.axis_size("res")
    seq_count = lax.axis_size("seq")
    rows, res_total, chan = alignment.shape
    hidden = left_projection_weight.shape[1]
    pair_width = out_weight.shape[1]
    row_block = res_total // res_count
    col_block = res_total // seq_count
    device_count = seq_count * res_count
    width = (row_block + col_block) * hidden
    vmem = pl.BlockSpec(memory_space=pltpu.VMEM)
    hbm = pl.BlockSpec(memory_space=pltpu.HBM)
    send = pl.pallas_call(
        functools.partial(project_kernel, seq_count, res_count),
        out_shape=jax.ShapeDtypeStruct((device_count * rows, width), jnp.bfloat16),
        in_specs=[hbm] * 7,
        out_specs=vmem,
        scratch_shapes=[
            pltpu.VMEM((rows, res_total, chan), jnp.bfloat16),
            pltpu.VMEM((1, chan), jnp.float32),
            pltpu.VMEM((1, chan), jnp.float32),
            pltpu.VMEM((hidden, chan), jnp.bfloat16),
            pltpu.VMEM((1, hidden), jnp.float32),
            pltpu.VMEM((hidden, chan), jnp.bfloat16),
            pltpu.VMEM((1, hidden), jnp.float32),
            pltpu.VMEM((rows * res_total, LANES), jnp.float32),
            pltpu.SemaphoreType.DMA((7,)),
        ],
        compiler_params=pltpu.CompilerParams(vmem_limit_bytes=32 * 1024 * 1024),
    )(
        in_hbm(alignment),
        in_hbm(layer_norm_gain.reshape(1, chan)),
        in_hbm(layer_norm_bias.reshape(1, chan)),
        in_hbm(left_projection_weight.T),
        in_hbm(left_bias.reshape(1, hidden)),
        in_hbm(right_projection_weight.T),
        in_hbm(right_bias.reshape(1, hidden)),
    )
    recv = lax.all_to_all(send, ("seq", "res"), split_axis=0, concat_axis=0, tiled=True)
    return pl.pallas_call(
        functools.partial(pair_kernel, hidden, row_block, col_block),
        out_shape=jax.ShapeDtypeStruct((row_block, col_block, pair_width), jnp.bfloat16),
        in_specs=[vmem, vmem, hbm],
        out_specs=vmem,
        scratch_shapes=[
            pltpu.VMEM((1, pair_width), jnp.float32),
            pltpu.VMEM((col_block * hidden // LANES, row_block * hidden, LANES), jnp.float32),
            pltpu.VMEM((row_block * col_block, pair_width), jnp.float32),
            pltpu.SemaphoreType.DMA,
        ],
        compiler_params=pltpu.CompilerParams(vmem_limit_bytes=32 * 1024 * 1024),
    )(recv, out_weight, in_hbm(out_bias.reshape(1, pair_width)))


def solution(mesh):
    in_specs = (P(("seq", "res"), None, None), P(), P(), P(), P(), P(), P(), P(), P())
    out_specs = P("res", "seq", None)
    return jax.shard_map(body, mesh=mesh, in_specs=in_specs, out_specs=out_specs, check_vma=False)
```

```python
import functools

import jax
import jax.numpy as jnp
from jax import lax
from jax.experimental import pallas as pl
from jax.experimental.pallas import tpu as pltpu
from jax.sharding import PartitionSpec as P

LANES = 128


def project_kernel(
    seq_count,
    res_count,
    align_hbm,
    gain_hbm,
    offset_hbm,
    left_w_hbm,
    left_b_hbm,
    right_w_hbm,
    right_b_hbm,
    out_b_hbm,
    *refs,
):
    out_b_ref, *send_refs = refs[: 1 + seq_count * res_count]
    (
        align_ref,
        gain_ref,
        offset_ref,
        left_w_ref,
        left_b_ref,
        right_w_ref,
        right_b_ref,
        proj_ref,
        left_ref,
        right_ref,
        sems,
    ) = refs[1 + seq_count * res_count :]
    copies = [
        pltpu.make_async_copy(source, target, sems.at[n])
        for n, (source, target) in enumerate(
            [
                (align_hbm, align_ref),
                (gain_hbm, gain_ref),
                (offset_hbm, offset_ref),
                (left_w_hbm, left_w_ref),
                (left_b_hbm, left_b_ref),
                (right_w_hbm, right_w_ref),
                (right_b_hbm, right_b_ref),
                (out_b_hbm, out_b_ref),
            ]
        )
    ]
    for copy in copies:
        copy.start()
    for copy in copies:
        copy.wait()
    rows, res_total, chan = align_ref.shape
    hidden = left_w_ref.shape[0]
    values = align_ref[...].astype(jnp.float32).reshape(rows * res_total, chan)
    centred = values - jnp.mean(values, axis=-1, keepdims=True)
    spread = jnp.mean(centred * centred, axis=-1, keepdims=True)
    normed = centred * lax.rsqrt(spread + 1e-05) * gain_ref[...] + offset_ref[...]
    weights = jnp.concatenate([left_w_ref[...], right_w_ref[...]], axis=0)
    biases = jnp.concatenate([left_b_ref[...], right_b_ref[...]], axis=1)
    proj_ref[:, : 2 * hidden] = (
        lax.dot_general(
            normed.astype(jnp.bfloat16),
            weights,
            (((1,), (1,)), ((), ())),
            preferred_element_type=jnp.float32,
        )
        + biases
    )
    tiles = [proj_ref[pl.ds(r, rows, stride=res_total), :][:, : 2 * hidden] for r in range(res_total)]
    row_block = res_total // res_count
    col_block = res_total // seq_count
    for a in range(res_count):
        left_ref[a] = jnp.concatenate(
            [t[:, :hidden] for t in tiles[a * row_block : (a + 1) * row_block]], axis=1
        )
    for b in range(seq_count):
        right_ref[b] = jnp.concatenate(
            [t[:, hidden:] for t in tiles[b * col_block : (b + 1) * col_block]], axis=1
        )
    seq_at = lax.axis_index("seq")
    res_at = lax.axis_index("res")
    split = row_block * hidden
    for k, send_ref in enumerate(send_refs):
        send_ref[:, :split] = left_ref[res_at ^ (k % res_count)].astype(jnp.bfloat16)
        send_ref[:, split:] = right_ref[seq_at ^ (k // res_count)].astype(jnp.bfloat16)


def pair_kernel(hidden, row_block, col_block, weight_ref, bias_ref, *refs):
    *recv_refs, out_ref, outer_ref, term_ref = refs
    recv = jnp.concatenate([ref[...] for ref in recv_refs], axis=0)
    seq_total = recv.shape[0]
    left = recv[:, : row_block * hidden]
    right = recv[:, row_block * hidden :]
    outer = lax.dot_general(
        left, right, (((0,), (0,)), ((), ())), preferred_element_type=jnp.float32
    )
    for g in range(outer_ref.shape[0]):
        outer_ref[g] = outer[:, g * LANES : (g + 1) * LANES]
    per_group = LANES // hidden
    terms = []
    for g in range(outer_ref.shape[0]):
        slabs = [outer_ref[g, pl.ds(c, row_block, stride=hidden), :] for c in range(hidden)]
        for j in range(per_group):
            flat = jnp.concatenate([s[:, j * hidden : (j + 1) * hidden] for s in slabs], axis=1)
            terms.append(flat)
    flat = jnp.concatenate(terms, axis=0).astype(jnp.bfloat16)
    term = jnp.dot(flat, weight_ref[...], preferred_element_type=jnp.float32)
    term_ref[...] = term * (1.0 / float(seq_total)) + bias_ref[...]
    for i in range(row_block):
        out_ref[i] = term_ref[pl.ds(i, col_block, stride=row_block), :].astype(jnp.bfloat16)


def in_hbm(array):
    return pltpu.with_memory_space_constraint(array, pltpu.HBM)


def body(
    alignment,
    layer_norm_gain,
    layer_norm_bias,
    left_projection_weight,
    left_bias,
    right_projection_weight,
    right_bias,
    out_weight,
    out_bias,
):
    res_count = lax.axis_size("res")
    seq_count = lax.axis_size("seq")
    rows, res_total, chan = alignment.shape
    hidden = left_projection_weight.shape[1]
    pair_width = out_weight.shape[1]
    row_block = res_total // res_count
    col_block = res_total // seq_count
    device_count = seq_count * res_count
    width = (row_block + col_block) * hidden
    vmem = pl.BlockSpec(memory_space=pltpu.VMEM)
    hbm = pl.BlockSpec(memory_space=pltpu.HBM)
    params = pltpu.CompilerParams(vmem_limit_bytes=32 * 1024 * 1024)
    bias_row, *sends = pl.pallas_call(
        functools.partial(project_kernel, seq_count, res_count),
        out_shape=[jax.ShapeDtypeStruct((1, pair_width), jnp.float32)]
        + [jax.ShapeDtypeStruct((rows, width), jnp.bfloat16)] * device_count,
        in_specs=[hbm] * 8,
        out_specs=[vmem] * (1 + device_count),
        scratch_shapes=[
            pltpu.VMEM((rows, res_total, chan), jnp.bfloat16),
            pltpu.VMEM((1, chan), jnp.float32),
            pltpu.VMEM((1, chan), jnp.float32),
            pltpu.VMEM((hidden, chan), jnp.bfloat16),
            pltpu.VMEM((1, hidden), jnp.float32),
            pltpu.VMEM((hidden, chan), jnp.bfloat16),
            pltpu.VMEM((1, hidden), jnp.float32),
            pltpu.VMEM((rows * res_total, LANES), jnp.float32),
            pltpu.VMEM((res_count, rows, row_block * hidden), jnp.float32),
            pltpu.VMEM((seq_count, rows, col_block * hidden), jnp.float32),
            pltpu.SemaphoreType.DMA((8,)),
        ],
        compiler_params=params,
    )(
        in_hbm(alignment),
        in_hbm(layer_norm_gain.reshape(1, chan)),
        in_hbm(layer_norm_bias.reshape(1, chan)),
        in_hbm(left_projection_weight.T),
        in_hbm(left_bias.reshape(1, hidden)),
        in_hbm(right_projection_weight.T),
        in_hbm(right_bias.reshape(1, hidden)),
        in_hbm(out_bias.reshape(1, pair_width)),
    )
    if device_count <= 32:
        recvs = [sends[0]]
        for k in range(1, device_count):
            pairs = [(n, n ^ k) for n in range(device_count)]
            recvs.append(lax.ppermute(sends[k], ("seq", "res"), pairs))
    else:
        relative = jnp.stack(sends)
        order = jnp.arange(device_count) ^ lax.axis_index(("seq", "res"))
        stacked = lax.all_to_all(relative[order], ("seq", "res"), split_axis=0, concat_axis=0, tiled=True)
        recvs = [stacked.reshape(device_count * rows, width)]
    return pl.pallas_call(
        functools.partial(pair_kernel, hidden, row_block, col_block),
        out_shape=jax.ShapeDtypeStruct((row_block, col_block, pair_width), jnp.bfloat16),
        in_specs=[vmem] * (2 + len(recvs)),
        out_specs=vmem,
        scratch_shapes=[
            pltpu.VMEM((col_block * hidden // LANES, row_block * hidden, LANES), jnp.float32),
            pltpu.VMEM((row_block * col_block, pair_width), jnp.float32),
        ],
        compiler_params=params,
    )(out_weight, bias_row, *recvs)


def solution(mesh):
    in_specs = (P(("seq", "res"), None, None), P(), P(), P(), P(), P(), P(), P(), P())
    out_specs = P("res", "seq", None)
    return jax.shard_map(body, mesh=mesh, in_specs=in_specs, out_specs=out_specs, check_vma=False)
```

```python
import functools

import jax
import jax.numpy as jnp
from jax import lax
from jax.experimental import pallas as pl
from jax.experimental.pallas import tpu as pltpu
from jax.sharding import Mesh
from jax.sharding import PartitionSpec as P

LANES = 128


def project_kernel(
    seq_count,
    half_count,
    rest_count,
    align_hbm,
    gain_hbm,
    offset_hbm,
    left_w_hbm,
    left_b_hbm,
    right_w_hbm,
    right_b_hbm,
    out_b_hbm,
    send_ref,
    out_b_ref,
    align_ref,
    gain_ref,
    offset_ref,
    left_w_ref,
    left_b_ref,
    right_w_ref,
    right_b_ref,
    proj_ref,
    sems,
):
    copies = [
        pltpu.make_async_copy(source, target, sems.at[n])
        for n, (source, target) in enumerate(
            [
                (align_hbm, align_ref),
                (gain_hbm, gain_ref),
                (offset_hbm, offset_ref),
                (left_w_hbm, left_w_ref),
                (left_b_hbm, left_b_ref),
                (right_w_hbm, right_w_ref),
                (right_b_hbm, right_b_ref),
                (out_b_hbm, out_b_ref),
            ]
        )
    ]
    for copy in copies:
        copy.start()
    for copy in copies:
        copy.wait()
    rows, res_total, chan = align_ref.shape
    hidden = left_w_ref.shape[0]
    values = align_ref[...].astype(jnp.float32).reshape(rows * res_total, chan)
    centred = values - jnp.mean(values, axis=-1, keepdims=True)
    spread = jnp.mean(centred * centred, axis=-1, keepdims=True)
    normed = centred * lax.rsqrt(spread + 1e-05) * gain_ref[...] + offset_ref[...]
    weights = jnp.concatenate([left_w_ref[...], right_w_ref[...]], axis=0)
    biases = jnp.concatenate([left_b_ref[...], right_b_ref[...]], axis=1)
    proj_ref[:, : 2 * hidden] = (
        lax.dot_general(
            normed.astype(jnp.bfloat16),
            weights,
            (((1,), (1,)), ((), ())),
            preferred_element_type=jnp.float32,
        )
        + biases
    )
    tiles = [proj_ref[pl.ds(r, rows, stride=res_total), :][:, : 2 * hidden] for r in range(res_total)]
    row_block = res_total // (half_count * rest_count)
    col_block = res_total // seq_count
    left = [
        jnp.concatenate([t[:, :hidden] for t in tiles[a * row_block : (a + 1) * row_block]], axis=1)
        for a in range(half_count * rest_count)
    ]
    right = [
        jnp.concatenate([t[:, hidden:] for t in tiles[b * col_block : (b + 1) * col_block]], axis=1)
        for b in range(seq_count)
    ]
    pieces = [
        jnp.concatenate([left[h * rest_count + a] for h in range(half_count)] + [right[b]], axis=1)
        for b in range(seq_count)
        for a in range(rest_count)
    ]
    group = max(1, 16 // rows)
    for start in range(0, len(pieces), group):
        block = jnp.concatenate(pieces[start : start + group], axis=0)
        send_ref[pl.ds(start * rows, group * rows), :] = block.astype(jnp.bfloat16)


def pair_kernel(
    hidden, row_block, col_block, recv_ref, weight_ref, mine_ref, theirs_ref, outer_ref, term_ref
):
    seq_total = 2 * recv_ref.shape[0]
    left = recv_ref[:, : 2 * row_block * hidden]
    right = recv_ref[:, 2 * row_block * hidden :]
    outer = lax.dot_general(
        left, right, (((0,), (0,)), ((), ())), preferred_element_type=jnp.float32
    )
    for g in range(outer_ref.shape[0]):
        outer_ref[g] = outer[:, g * LANES : (g + 1) * LANES]
    per_group = LANES // hidden
    terms = []
    for h in range(2):
        for g in range(outer_ref.shape[0]):
            slabs = [
                outer_ref[g, pl.ds(h * row_block * hidden + c, row_block, stride=hidden), :]
                for c in range(hidden)
            ]
            for j in range(per_group):
                flat = jnp.concatenate([s[:, j * hidden : (j + 1) * hidden] for s in slabs], axis=1)
                terms.append(flat)
    flat = jnp.concatenate(terms, axis=0).astype(jnp.bfloat16)
    term = jnp.dot(flat, weight_ref[...], preferred_element_type=jnp.float32)
    term = term * (1.0 / float(seq_total))
    pairs = row_block * col_block
    term_ref[0] = term[:pairs]
    term_ref[1] = term[pairs:]
    half = lax.axis_index("half")
    mine_ref[...] = term_ref[half]
    theirs_ref[...] = term_ref[1 - half].astype(jnp.bfloat16)


def add_kernel(mine_ref, came_ref, bias_ref, out_ref, term_ref):
    row_block, col_block, _ = out_ref.shape
    term_ref[...] = mine_ref[...] + came_ref[...].astype(jnp.float32) + bias_ref[...]
    for i in range(row_block):
        out_ref[i] = term_ref[pl.ds(i, col_block, stride=row_block), :].astype(jnp.bfloat16)


def in_hbm(array):
    return pltpu.with_memory_space_constraint(array, pltpu.HBM)


def body(
    alignment,
    layer_norm_gain,
    layer_norm_bias,
    left_projection_weight,
    left_bias,
    right_projection_weight,
    right_bias,
    out_weight,
    out_bias,
):
    seq_count = lax.axis_size("seq")
    half_count = lax.axis_size("half")
    rest_count = lax.axis_size("rest")
    rows, res_total, chan = alignment.shape
    hidden = left_projection_weight.shape[1]
    pair_width = out_weight.shape[1]
    row_block = res_total // (half_count * rest_count)
    col_block = res_total // seq_count
    peers = seq_count * rest_count
    width = (half_count * row_block + col_block) * hidden
    pairs = row_block * col_block
    vmem = pl.BlockSpec(memory_space=pltpu.VMEM)
    hbm = pl.BlockSpec(memory_space=pltpu.HBM)
    params = pltpu.CompilerParams(vmem_limit_bytes=32 * 1024 * 1024)
    send, bias_row = pl.pallas_call(
        functools.partial(project_kernel, seq_count, half_count, rest_count),
        out_shape=[
            jax.ShapeDtypeStruct((peers * rows, width), jnp.bfloat16),
            jax.ShapeDtypeStruct((1, pair_width), jnp.float32),
        ],
        in_specs=[hbm] * 8,
        out_specs=[vmem] * 2,
        scratch_shapes=[
            pltpu.VMEM((rows, res_total, chan), jnp.bfloat16),
            pltpu.VMEM((1, chan), jnp.float32),
            pltpu.VMEM((1, chan), jnp.float32),
            pltpu.VMEM((hidden, chan), jnp.bfloat16),
            pltpu.VMEM((1, hidden), jnp.float32),
            pltpu.VMEM((hidden, chan), jnp.bfloat16),
            pltpu.VMEM((1, hidden), jnp.float32),
            pltpu.VMEM((rows * res_total, LANES), jnp.float32),
            pltpu.SemaphoreType.DMA((8,)),
        ],
        compiler_params=params,
    )(
        in_hbm(alignment),
        in_hbm(layer_norm_gain.reshape(1, chan)),
        in_hbm(layer_norm_bias.reshape(1, chan)),
        in_hbm(left_projection_weight.T),
        in_hbm(left_bias.reshape(1, hidden)),
        in_hbm(right_projection_weight.T),
        in_hbm(right_bias.reshape(1, hidden)),
        in_hbm(out_bias.reshape(1, pair_width)),
    )
    recv = lax.all_to_all(send, ("seq", "rest"), split_axis=0, concat_axis=0, tiled=True)
    mine, theirs = pl.pallas_call(
        functools.partial(pair_kernel, hidden, row_block, col_block),
        out_shape=[
            jax.ShapeDtypeStruct((pairs, pair_width), jnp.float32),
            jax.ShapeDtypeStruct((pairs, pair_width), jnp.bfloat16),
        ],
        in_specs=[vmem] * 2,
        out_specs=[vmem] * 2,
        scratch_shapes=[
            pltpu.VMEM((col_block * hidden // LANES, 2 * row_block * hidden, LANES), jnp.float32),
            pltpu.VMEM((2, pairs, pair_width), jnp.float32),
        ],
        compiler_params=params,
    )(recv, out_weight)
    came = lax.ppermute(theirs, "half", [(0, 1), (1, 0)])
    return pl.pallas_call(
        add_kernel,
        out_shape=jax.ShapeDtypeStruct((row_block, col_block, pair_width), jnp.bfloat16),
        in_specs=[vmem] * 3,
        out_specs=vmem,
        scratch_shapes=[pltpu.VMEM((pairs, pair_width), jnp.float32)],
        compiler_params=params,
    )(mine, came, bias_row)


def solution(mesh):
    seq_count, res_count = mesh.devices.shape
    split = Mesh(mesh.devices.reshape(seq_count, 2, res_count // 2), ("seq", "half", "rest"))
    in_specs = (P(("seq", "half", "rest"), None, None), P(), P(), P(), P(), P(), P(), P(), P())
    out_specs = P(("half", "rest"), "seq", None)
    return jax.shard_map(body, mesh=split, in_specs=in_specs, out_specs=out_specs, check_vma=False)
```

```python
import functools

import jax
import jax.numpy as jnp
from jax import lax
from jax.experimental import pallas as pl
from jax.experimental.pallas import tpu as pltpu
from jax.sharding import Mesh
from jax.sharding import PartitionSpec as P

LANES = 128


def project_kernel(
    seq_count,
    core_count,
    rest_count,
    align_hbm,
    gain_hbm,
    offset_hbm,
    left_w_hbm,
    left_b_hbm,
    right_w_hbm,
    right_b_hbm,
    out_b_hbm,
    send_ref,
    out_b_ref,
    align_ref,
    gain_ref,
    offset_ref,
    left_w_ref,
    left_b_ref,
    right_w_ref,
    right_b_ref,
    proj_ref,
    sems,
):
    copies = [
        pltpu.make_async_copy(source, target, sems.at[n])
        for n, (source, target) in enumerate(
            [
                (align_hbm, align_ref),
                (gain_hbm, gain_ref),
                (offset_hbm, offset_ref),
                (left_w_hbm, left_w_ref),
                (left_b_hbm, left_b_ref),
                (right_w_hbm, right_w_ref),
                (right_b_hbm, right_b_ref),
                (out_b_hbm, out_b_ref),
            ]
        )
    ]
    for copy in copies:
        copy.start()
    for copy in copies:
        copy.wait()
    rows, res_total, chan = align_ref.shape
    hidden = left_w_ref.shape[0]
    values = align_ref[...].astype(jnp.float32).reshape(rows * res_total, chan)
    centred = values - jnp.mean(values, axis=-1, keepdims=True)
    spread = jnp.mean(centred * centred, axis=-1, keepdims=True)
    normed = centred * lax.rsqrt(spread + 1e-05) * gain_ref[...] + offset_ref[...]
    weights = jnp.concatenate([left_w_ref[...], right_w_ref[...]], axis=0)
    biases = jnp.concatenate([left_b_ref[...], right_b_ref[...]], axis=1)
    proj_ref[:, : 2 * hidden] = (
        lax.dot_general(
            normed.astype(jnp.bfloat16),
            weights,
            (((1,), (1,)), ((), ())),
            preferred_element_type=jnp.float32,
        )
        + biases
    )
    tiles = [proj_ref[pl.ds(r, rows, stride=res_total), :][:, : 2 * hidden] for r in range(res_total)]
    row_block = res_total // (core_count * rest_count)
    col_block = res_total // seq_count
    left = [
        jnp.concatenate([t[:, :hidden] for t in tiles[a * row_block : (a + 1) * row_block]], axis=1)
        for a in range(core_count * rest_count)
    ]
    right = [
        jnp.concatenate([t[:, hidden:] for t in tiles[b * col_block : (b + 1) * col_block]], axis=1)
        for b in range(seq_count)
    ]
    pieces = [
        jnp.concatenate([left[a * core_count + k] for k in range(core_count)] + [right[b]], axis=1)
        for b in range(seq_count)
        for a in range(rest_count)
    ]
    group = max(1, 16 // rows)
    for start in range(0, len(pieces), group):
        block = jnp.concatenate(pieces[start : start + group], axis=0)
        send_ref[pl.ds(start * rows, group * rows), :] = block.astype(jnp.bfloat16)


def pair_kernel(own, hidden, row_block, col_block, recv_ref, weight_ref, out_ref, outer_ref):
    core = lax.axis_index("core")
    seq_total = 2 * recv_ref.shape[0]
    split = row_block * hidden
    start = pl.multiple_of((core if own else 1 - core) * split, split)
    left = recv_ref[:, pl.ds(start, split)]
    right = recv_ref[:, 2 * split :]
    outer = lax.dot_general(
        left, right, (((0,), (0,)), ((), ())), preferred_element_type=jnp.float32
    )
    for g in range(outer_ref.shape[0]):
        outer_ref[g] = outer[:, g * LANES : (g + 1) * LANES]
    per_group = LANES // hidden
    terms = []
    for g in range(outer_ref.shape[0]):
        slabs = [outer_ref[g, pl.ds(c, row_block, stride=hidden), :] for c in range(hidden)]
        for j in range(per_group):
            flat = jnp.concatenate([s[:, j * hidden : (j + 1) * hidden] for s in slabs], axis=1)
            terms.append(flat)
    flat = jnp.concatenate(terms, axis=0).astype(jnp.bfloat16)
    term = jnp.dot(flat, weight_ref[...], preferred_element_type=jnp.float32)
    out_ref[...] = (term * (1.0 / float(seq_total))).astype(out_ref.dtype)


def add_kernel(mine_ref, came_ref, bias_ref, out_ref, term_ref):
    row_block, col_block, _ = out_ref.shape
    term_ref[...] = mine_ref[...] + came_ref[...].astype(jnp.float32) + bias_ref[...]
    for i in range(row_block):
        out_ref[i] = term_ref[pl.ds(i, col_block, stride=row_block), :].astype(jnp.bfloat16)


def in_hbm(array):
    return pltpu.with_memory_space_constraint(array, pltpu.HBM)


def body(
    alignment,
    layer_norm_gain,
    layer_norm_bias,
    left_projection_weight,
    left_bias,
    right_projection_weight,
    right_bias,
    out_weight,
    out_bias,
):
    seq_count = lax.axis_size("seq")
    core_count = lax.axis_size("core")
    rest_count = lax.axis_size("rest")
    rows, res_total, chan = alignment.shape
    hidden = left_projection_weight.shape[1]
    pair_width = out_weight.shape[1]
    row_block = res_total // (core_count * rest_count)
    col_block = res_total // seq_count
    peers = seq_count * rest_count
    width = (core_count * row_block + col_block) * hidden
    pairs = row_block * col_block
    vmem = pl.BlockSpec(memory_space=pltpu.VMEM)
    hbm = pl.BlockSpec(memory_space=pltpu.HBM)
    params = pltpu.CompilerParams(vmem_limit_bytes=32 * 1024 * 1024)
    send, bias_row = pl.pallas_call(
        functools.partial(project_kernel, seq_count, core_count, rest_count),
        out_shape=[
            jax.ShapeDtypeStruct((peers * rows, width), jnp.bfloat16),
            jax.ShapeDtypeStruct((1, pair_width), jnp.float32),
        ],
        in_specs=[hbm] * 8,
        out_specs=[vmem] * 2,
        scratch_shapes=[
            pltpu.VMEM((rows, res_total, chan), jnp.bfloat16),
            pltpu.VMEM((1, chan), jnp.float32),
            pltpu.VMEM((1, chan), jnp.float32),
            pltpu.VMEM((hidden, chan), jnp.bfloat16),
            pltpu.VMEM((1, hidden), jnp.float32),
            pltpu.VMEM((hidden, chan), jnp.bfloat16),
            pltpu.VMEM((1, hidden), jnp.float32),
            pltpu.VMEM((rows * res_total, LANES), jnp.float32),
            pltpu.SemaphoreType.DMA((8,)),
        ],
        compiler_params=params,
    )(
        in_hbm(alignment),
        in_hbm(layer_norm_gain.reshape(1, chan)),
        in_hbm(layer_norm_bias.reshape(1, chan)),
        in_hbm(left_projection_weight.T),
        in_hbm(left_bias.reshape(1, hidden)),
        in_hbm(right_projection_weight.T),
        in_hbm(right_bias.reshape(1, hidden)),
        in_hbm(out_bias.reshape(1, pair_width)),
    )
    recv = lax.all_to_all(send, ("seq", "rest"), split_axis=0, concat_axis=0, tiled=True)
    outer_values = pairs * hidden * hidden

    def pair_block(own, dtype):
        return pl.pallas_call(
            functools.partial(pair_kernel, own, hidden, row_block, col_block),
            out_shape=jax.ShapeDtypeStruct((pairs, pair_width), dtype),
            in_specs=[vmem] * 2,
            out_specs=vmem,
            scratch_shapes=[
                pltpu.VMEM((col_block * hidden // LANES, row_block * hidden, LANES), jnp.float32)
            ],
            compiler_params=params,
            cost_estimate=pl.CostEstimate(
                flops=2 * outer_values * (recv.shape[0] + pair_width),
                bytes_accessed=2 * (recv.size + out_weight.size),
                transcendentals=0,
            ),
        )(recv, out_weight)

    theirs = pair_block(False, jnp.bfloat16)
    came = lax.ppermute(theirs, "core", [(0, 1), (1, 0)])
    mine = pair_block(True, jnp.float32)
    return pl.pallas_call(
        add_kernel,
        out_shape=jax.ShapeDtypeStruct((row_block, col_block, pair_width), jnp.bfloat16),
        in_specs=[vmem] * 3,
        out_specs=vmem,
        scratch_shapes=[pltpu.VMEM((pairs, pair_width), jnp.float32)],
        compiler_params=params,
    )(mine, came, bias_row)


def solution(mesh):
    seq_count, res_count = mesh.devices.shape
    split = Mesh(mesh.devices.reshape(seq_count, res_count // 2, 2), ("seq", "rest", "core"))
    in_specs = (P(("seq", "rest", "core"), None, None), P(), P(), P(), P(), P(), P(), P(), P())
    out_specs = P(("rest", "core"), "seq", None)
    return jax.shard_map(body, mesh=split, in_specs=in_specs, out_specs=out_specs, check_vma=False)
```

```python
import functools

import jax
import jax.numpy as jnp
from jax import lax
from jax.experimental import pallas as pl
from jax.experimental.pallas import tpu as pltpu
from jax.sharding import Mesh
from jax.sharding import PartitionSpec as P

LANES = 128


def mirror(at, rest_count):
    pair = 2 - rest_count % 2
    return (rest_count // pair - 1 - at // pair) * pair + at % pair


def project_kernel(
    seq_count,
    half_count,
    rest_count,
    align_hbm,
    gain_hbm,
    offset_hbm,
    left_w_hbm,
    left_b_hbm,
    right_w_hbm,
    right_b_hbm,
    out_b_hbm,
    send_ref,
    out_b_ref,
    align_ref,
    gain_ref,
    offset_ref,
    left_w_ref,
    left_b_ref,
    right_w_ref,
    right_b_ref,
    proj_ref,
    left_ref,
    sems,
):
    copies = [
        pltpu.make_async_copy(source, target, sems.at[n])
        for n, (source, target) in enumerate(
            [
                (align_hbm, align_ref),
                (gain_hbm, gain_ref),
                (offset_hbm, offset_ref),
                (left_w_hbm, left_w_ref),
                (left_b_hbm, left_b_ref),
                (right_w_hbm, right_w_ref),
                (right_b_hbm, right_b_ref),
                (out_b_hbm, out_b_ref),
            ]
        )
    ]
    for copy in copies:
        copy.start()
    for copy in copies:
        copy.wait()
    rows, res_total, chan = align_ref.shape
    hidden = left_w_ref.shape[0]
    values = align_ref[...].astype(jnp.float32).reshape(rows * res_total, chan)
    centred = values - jnp.mean(values, axis=-1, keepdims=True)
    spread = jnp.mean(centred * centred, axis=-1, keepdims=True)
    normed = centred * lax.rsqrt(spread + 1e-05) * gain_ref[...] + offset_ref[...]
    weights = jnp.concatenate([left_w_ref[...], right_w_ref[...]], axis=0)
    biases = jnp.concatenate([left_b_ref[...], right_b_ref[...]], axis=1)
    proj_ref[:, : 2 * hidden] = (
        lax.dot_general(
            normed.astype(jnp.bfloat16),
            weights,
            (((1,), (1,)), ((), ())),
            preferred_element_type=jnp.float32,
        )
        + biases
    )
    tiles = [proj_ref[pl.ds(r, rows, stride=res_total), :][:, : 2 * hidden] for r in range(res_total)]
    row_block = res_total // (half_count * rest_count)
    col_block = res_total // seq_count
    for a in range(half_count * rest_count):
        left_ref[a] = jnp.concatenate(
            [t[:, :hidden] for t in tiles[a * row_block : (a + 1) * row_block]], axis=1
        )
    right = [
        jnp.concatenate([t[:, hidden:] for t in tiles[b * col_block : (b + 1) * col_block]], axis=1)
        for b in range(seq_count)
    ]
    half = lax.axis_index("half")
    own = [left_ref[half * rest_count + a] for a in range(rest_count)]
    other = [left_ref[(1 - half) * rest_count + mirror(a, rest_count)] for a in range(rest_count)]
    pieces = [
        jnp.concatenate([own[a], other[a], right[b]], axis=1)
        for b in range(seq_count)
        for a in range(rest_count)
    ]
    group = max(1, 16 // rows)
    for start in range(0, len(pieces), group):
        block = jnp.concatenate(pieces[start : start + group], axis=0)
        send_ref[pl.ds(start * rows, group * rows), :] = block.astype(jnp.bfloat16)


def pair_kernel(own, hidden, row_block, col_block, recv_ref, weight_ref, out_ref, outer_ref):
    seq_total = 2 * recv_ref.shape[0]
    split = row_block * hidden
    left = recv_ref[:, :split] if own else recv_ref[:, split : 2 * split]
    right = recv_ref[:, 2 * split :]
    outer = lax.dot_general(
        left, right, (((0,), (0,)), ((), ())), preferred_element_type=jnp.float32
    )
    for g in range(outer_ref.shape[0]):
        outer_ref[g] = outer[:, g * LANES : (g + 1) * LANES]
    per_group = LANES // hidden
    terms = []
    for g in range(outer_ref.shape[0]):
        slabs = [outer_ref[g, pl.ds(c, row_block, stride=hidden), :] for c in range(hidden)]
        for j in range(per_group):
            flat = jnp.concatenate([s[:, j * hidden : (j + 1) * hidden] for s in slabs], axis=1)
            terms.append(flat)
    flat = jnp.concatenate(terms, axis=0).astype(jnp.bfloat16)
    term = jnp.dot(flat, weight_ref[...], preferred_element_type=jnp.float32)
    out_ref[...] = (term * (1.0 / float(seq_total))).astype(out_ref.dtype)


def add_kernel(mine_ref, came_ref, bias_ref, out_ref, term_ref):
    row_block, col_block, _ = out_ref.shape
    term_ref[...] = mine_ref[...] + came_ref[...].astype(jnp.float32) + bias_ref[...]
    for i in range(row_block):
        out_ref[i] = term_ref[pl.ds(i, col_block, stride=row_block), :].astype(jnp.bfloat16)


def in_hbm(array):
    return pltpu.with_memory_space_constraint(array, pltpu.HBM)


def body(
    alignment,
    layer_norm_gain,
    layer_norm_bias,
    left_projection_weight,
    left_bias,
    right_projection_weight,
    right_bias,
    out_weight,
    out_bias,
):
    seq_count = lax.axis_size("seq")
    half_count = lax.axis_size("half")
    rest_count = lax.axis_size("rest")
    rows, res_total, chan = alignment.shape
    hidden = left_projection_weight.shape[1]
    pair_width = out_weight.shape[1]
    row_block = res_total // (half_count * rest_count)
    col_block = res_total // seq_count
    peers = seq_count * rest_count
    width = (half_count * row_block + col_block) * hidden
    pairs = row_block * col_block
    vmem = pl.BlockSpec(memory_space=pltpu.VMEM)
    hbm = pl.BlockSpec(memory_space=pltpu.HBM)
    params = pltpu.CompilerParams(vmem_limit_bytes=32 * 1024 * 1024)
    send, bias_row = pl.pallas_call(
        functools.partial(project_kernel, seq_count, half_count, rest_count),
        out_shape=[
            jax.ShapeDtypeStruct((peers * rows, width), jnp.bfloat16),
            jax.ShapeDtypeStruct((1, pair_width), jnp.float32),
        ],
        in_specs=[hbm] * 8,
        out_specs=[vmem] * 2,
        scratch_shapes=[
            pltpu.VMEM((rows, res_total, chan), jnp.bfloat16),
            pltpu.VMEM((1, chan), jnp.float32),
            pltpu.VMEM((1, chan), jnp.float32),
            pltpu.VMEM((hidden, chan), jnp.bfloat16),
            pltpu.VMEM((1, hidden), jnp.float32),
            pltpu.VMEM((hidden, chan), jnp.bfloat16),
            pltpu.VMEM((1, hidden), jnp.float32),
            pltpu.VMEM((rows * res_total, LANES), jnp.float32),
            pltpu.VMEM((half_count * rest_count, rows, row_block * hidden), jnp.float32),
            pltpu.SemaphoreType.DMA((8,)),
        ],
        compiler_params=params,
    )(
        in_hbm(alignment),
        in_hbm(layer_norm_gain.reshape(1, chan)),
        in_hbm(layer_norm_bias.reshape(1, chan)),
        in_hbm(left_projection_weight.T),
        in_hbm(left_bias.reshape(1, hidden)),
        in_hbm(right_projection_weight.T),
        in_hbm(right_bias.reshape(1, hidden)),
        in_hbm(out_bias.reshape(1, pair_width)),
    )
    recv = lax.all_to_all(send, ("seq", "rest"), split_axis=0, concat_axis=0, tiled=True)
    outer_values = pairs * hidden * hidden

    def pair_block(own, dtype):
        return pl.pallas_call(
            functools.partial(pair_kernel, own, hidden, row_block, col_block),
            out_shape=jax.ShapeDtypeStruct((pairs, pair_width), dtype),
            in_specs=[vmem] * 2,
            out_specs=vmem,
            scratch_shapes=[
                pltpu.VMEM((col_block * hidden // LANES, row_block * hidden, LANES), jnp.float32)
            ],
            compiler_params=params,
            cost_estimate=pl.CostEstimate(
                flops=2 * outer_values * (recv.shape[0] + pair_width),
                bytes_accessed=2 * (recv.size + out_weight.size),
                transcendentals=0,
            ),
        )(recv, out_weight)

    theirs = pair_block(False, jnp.bfloat16)
    swap = [
        (h * rest_count + q, (1 - h) * rest_count + mirror(q, rest_count))
        for h in range(half_count)
        for q in range(rest_count)
    ]
    came = lax.ppermute(theirs, ("half", "rest"), swap)
    mine = pair_block(True, jnp.float32)
    return pl.pallas_call(
        add_kernel,
        out_shape=jax.ShapeDtypeStruct((row_block, col_block, pair_width), jnp.bfloat16),
        in_specs=[vmem] * 3,
        out_specs=vmem,
        scratch_shapes=[pltpu.VMEM((pairs, pair_width), jnp.float32)],
        compiler_params=params,
    )(mine, came, bias_row)


def solution(mesh):
    seq_count, res_count = mesh.devices.shape
    split = Mesh(mesh.devices.reshape(seq_count, 2, res_count // 2), ("seq", "half", "rest"))
    in_specs = (P(("seq", "half", "rest"), None, None), P(), P(), P(), P(), P(), P(), P(), P())
    out_specs = P(("half", "rest"), "seq", None)
    return jax.shard_map(body, mesh=split, in_specs=in_specs, out_specs=out_specs, check_vma=False)
```

```python
import functools

import jax
import jax.numpy as jnp
from jax import lax
from jax.experimental import pallas as pl
from jax.experimental.pallas import tpu as pltpu
from jax.sharding import Mesh
from jax.sharding import PartitionSpec as P

LANES = 128


def partner(rest_count):
    ring = list(range(1, rest_count, 2)) + list(range(0, rest_count, 2))[::-1]
    step = dict(zip(ring, ring[1:] + ring[:1]))
    return [step[at] for at in range(rest_count)]


def project_kernel(
    seq_count,
    half_count,
    rest_count,
    align_hbm,
    gain_hbm,
    offset_hbm,
    left_w_hbm,
    left_b_hbm,
    right_w_hbm,
    right_b_hbm,
    out_b_hbm,
    send_ref,
    out_b_ref,
    align_ref,
    gain_ref,
    offset_ref,
    left_w_ref,
    left_b_ref,
    right_w_ref,
    right_b_ref,
    proj_ref,
    left_ref,
    sems,
):
    rows, res_total, chan = align_ref.shape
    hidden = left_w_ref.shape[0]
    step = max(1, rows // 4)
    cuts = [pl.ds(at, step) for at in range(0, rows, step)]
    small = [
        pltpu.make_async_copy(source, target, sems.at[len(cuts) + n])
        for n, (source, target) in enumerate(
            [
                (left_w_hbm, left_w_ref),
                (right_w_hbm, right_w_ref),
                (gain_hbm, gain_ref),
                (offset_hbm, offset_ref),
                (left_b_hbm, left_b_ref),
                (right_b_hbm, right_b_ref),
                (out_b_hbm, out_b_ref),
            ]
        )
    ]
    large = [
        pltpu.make_async_copy(align_hbm.at[cut], align_ref.at[cut], sems.at[n])
        for n, cut in enumerate(cuts)
    ]
    for copy in large[:1] + small + large[1:]:
        copy.start()
    for copy in small:
        copy.wait()
    weights = jnp.concatenate([left_w_ref[...], right_w_ref[...]], axis=0)
    biases = jnp.concatenate([left_b_ref[...], right_b_ref[...]], axis=1)
    for n, cut in enumerate(cuts):
        large[n].wait()
        values = align_ref[cut].astype(jnp.float32).reshape(step * res_total, chan)
        centred = values - jnp.mean(values, axis=-1, keepdims=True)
        spread = jnp.mean(centred * centred, axis=-1, keepdims=True)
        normed = centred * lax.rsqrt(spread + 1e-05) * gain_ref[...] + offset_ref[...]
        proj_ref[pl.ds(n * step * res_total, step * res_total), : 2 * hidden] = (
            lax.dot_general(
                normed.astype(jnp.bfloat16),
                weights,
                (((1,), (1,)), ((), ())),
                preferred_element_type=jnp.float32,
            )
            + biases
        )
    tiles = [proj_ref[pl.ds(r, rows, stride=res_total), :][:, : 2 * hidden] for r in range(res_total)]
    row_block = res_total // (half_count * rest_count)
    col_block = res_total // seq_count
    for a in range(half_count * rest_count):
        left_ref[a] = jnp.concatenate(
            [t[:, :hidden] for t in tiles[a * row_block : (a + 1) * row_block]], axis=1
        )
    right = [
        jnp.concatenate([t[:, hidden:] for t in tiles[b * col_block : (b + 1) * col_block]], axis=1)
        for b in range(seq_count)
    ]
    half = lax.axis_index("half")
    own = [left_ref[half * rest_count + a] for a in range(rest_count)]
    up = partner(rest_count)
    other = [
        left_ref[jnp.where(half == 0, rest_count + up[a], up.index(a))] for a in range(rest_count)
    ]
    pieces = [
        jnp.concatenate([own[a], other[a], right[b]], axis=1)
        for b in range(seq_count)
        for a in range(rest_count)
    ]
    group = max(1, 16 // rows)
    for start in range(0, len(pieces), group):
        block = jnp.concatenate(pieces[start : start + group], axis=0)
        send_ref[pl.ds(start * rows, group * rows), :] = block.astype(jnp.bfloat16)


def pair_kernel(own, hidden, row_block, col_block, recv_ref, weight_ref, out_ref, outer_ref):
    seq_total = 2 * recv_ref.shape[0]
    split = row_block * hidden
    left = recv_ref[:, :split] if own else recv_ref[:, split : 2 * split]
    right = recv_ref[:, 2 * split :]
    outer = lax.dot_general(
        left, right, (((0,), (0,)), ((), ())), preferred_element_type=jnp.float32
    )
    for g in range(outer_ref.shape[0]):
        outer_ref[g] = outer[:, g * LANES : (g + 1) * LANES]
    per_group = LANES // hidden
    terms = []
    for g in range(outer_ref.shape[0]):
        slabs = [outer_ref[g, pl.ds(c, row_block, stride=hidden), :] for c in range(hidden)]
        for j in range(per_group):
            flat = jnp.concatenate([s[:, j * hidden : (j + 1) * hidden] for s in slabs], axis=1)
            terms.append(flat)
    flat = jnp.concatenate(terms, axis=0).astype(jnp.bfloat16)
    term = jnp.dot(flat, weight_ref[...], preferred_element_type=jnp.float32)
    out_ref[...] = (term * (1.0 / float(seq_total))).astype(out_ref.dtype)


def add_kernel(mine_ref, came_ref, bias_ref, out_ref, term_ref):
    row_block, col_block, _ = out_ref.shape
    term_ref[...] = mine_ref[...] + came_ref[...].astype(jnp.float32) + bias_ref[...]
    for i in range(row_block):
        out_ref[i] = term_ref[pl.ds(i, col_block, stride=row_block), :].astype(jnp.bfloat16)


def in_hbm(array):
    return pltpu.with_memory_space_constraint(array, pltpu.HBM)


def body(
    alignment,
    layer_norm_gain,
    layer_norm_bias,
    left_projection_weight,
    left_bias,
    right_projection_weight,
    right_bias,
    out_weight,
    out_bias,
):
    seq_count = lax.axis_size("seq")
    half_count = lax.axis_size("half")
    rest_count = lax.axis_size("rest")
    rows, res_total, chan = alignment.shape
    hidden = left_projection_weight.shape[1]
    pair_width = out_weight.shape[1]
    row_block = res_total // (half_count * rest_count)
    col_block = res_total // seq_count
    peers = seq_count * rest_count
    width = (half_count * row_block + col_block) * hidden
    pairs = row_block * col_block
    vmem = pl.BlockSpec(memory_space=pltpu.VMEM)
    hbm = pl.BlockSpec(memory_space=pltpu.HBM)
    params = pltpu.CompilerParams(vmem_limit_bytes=32 * 1024 * 1024)
    send, bias_row = pl.pallas_call(
        functools.partial(project_kernel, seq_count, half_count, rest_count),
        out_shape=[
            jax.ShapeDtypeStruct((peers * rows, width), jnp.bfloat16),
            jax.ShapeDtypeStruct((1, pair_width), jnp.float32),
        ],
        in_specs=[hbm] * 8,
        out_specs=[vmem] * 2,
        scratch_shapes=[
            pltpu.VMEM((rows, res_total, chan), jnp.bfloat16),
            pltpu.VMEM((1, chan), jnp.float32),
            pltpu.VMEM((1, chan), jnp.float32),
            pltpu.VMEM((hidden, chan), jnp.bfloat16),
            pltpu.VMEM((1, hidden), jnp.float32),
            pltpu.VMEM((hidden, chan), jnp.bfloat16),
            pltpu.VMEM((1, hidden), jnp.float32),
            pltpu.VMEM((rows * res_total, LANES), jnp.float32),
            pltpu.VMEM((half_count * rest_count, rows, row_block * hidden), jnp.float32),
            pltpu.SemaphoreType.DMA((7 + rows // max(1, rows // 4),)),
        ],
        compiler_params=params,
    )(
        in_hbm(alignment),
        in_hbm(layer_norm_gain.reshape(1, chan)),
        in_hbm(layer_norm_bias.reshape(1, chan)),
        in_hbm(left_projection_weight.T),
        in_hbm(left_bias.reshape(1, hidden)),
        in_hbm(right_projection_weight.T),
        in_hbm(right_bias.reshape(1, hidden)),
        in_hbm(out_bias.reshape(1, pair_width)),
    )
    recv = lax.all_to_all(send, ("seq", "rest"), split_axis=0, concat_axis=0, tiled=True)
    outer_values = pairs * hidden * hidden

    def pair_block(own, dtype):
        return pl.pallas_call(
            functools.partial(pair_kernel, own, hidden, row_block, col_block),
            out_shape=jax.ShapeDtypeStruct((pairs, pair_width), dtype),
            in_specs=[vmem] * 2,
            out_specs=vmem,
            scratch_shapes=[
                pltpu.VMEM((col_block * hidden // LANES, row_block * hidden, LANES), jnp.float32)
            ],
            compiler_params=params,
            cost_estimate=pl.CostEstimate(
                flops=2 * outer_values * (recv.shape[0] + pair_width),
                bytes_accessed=2 * (recv.size + out_weight.size),
                transcendentals=0,
            ),
        )(recv, out_weight)

    theirs = pair_block(False, jnp.bfloat16)
    across = [(low, rest_count + high) for low, high in enumerate(partner(rest_count))]
    swap = across + [(high, low) for low, high in across]
    came = lax.ppermute(theirs, ("half", "rest"), swap)
    mine = pair_block(True, jnp.float32)
    return pl.pallas_call(
        add_kernel,
        out_shape=jax.ShapeDtypeStruct((row_block, col_block, pair_width), jnp.bfloat16),
        in_specs=[vmem] * 3,
        out_specs=vmem,
        scratch_shapes=[pltpu.VMEM((pairs, pair_width), jnp.float32)],
        compiler_params=params,
    )(mine, came, bias_row)


def solution(mesh):
    seq_count, res_count = mesh.devices.shape
    split = Mesh(mesh.devices.reshape(seq_count, 2, res_count // 2), ("seq", "half", "rest"))
    in_specs = (P(("seq", "half", "rest"), None, None), P(), P(), P(), P(), P(), P(), P(), P())
    out_specs = P(("half", "rest"), "seq", None)
    return jax.shard_map(body, mesh=split, in_specs=in_specs, out_specs=out_specs, check_vma=False)
```

```python
import functools

import jax
import jax.numpy as jnp
from jax import lax
from jax.experimental import pallas as pl
from jax.experimental.pallas import tpu as pltpu
from jax.sharding import Mesh
from jax.sharding import PartitionSpec as P

LANES = 128


def peer_order(seq_count, rest_count):
    return [(b, a) for b in range(seq_count) for a in range(rest_count)][::-1]


def project_kernel(
    seq_count,
    half_count,
    rest_count,
    align_hbm,
    gain_hbm,
    offset_hbm,
    left_w_hbm,
    left_b_hbm,
    right_w_hbm,
    right_b_hbm,
    out_b_hbm,
    send_ref,
    out_b_ref,
    align_ref,
    gain_ref,
    offset_ref,
    left_w_ref,
    left_b_ref,
    right_w_ref,
    right_b_ref,
    proj_ref,
    left_ref,
    sems,
):
    copies = [
        pltpu.make_async_copy(source, target, sems.at[n])
        for n, (source, target) in enumerate(
            [
                (align_hbm, align_ref),
                (gain_hbm, gain_ref),
                (offset_hbm, offset_ref),
                (left_w_hbm, left_w_ref),
                (left_b_hbm, left_b_ref),
                (right_w_hbm, right_w_ref),
                (right_b_hbm, right_b_ref),
                (out_b_hbm, out_b_ref),
            ]
        )
    ]
    for copy in copies:
        copy.start()
    for copy in copies:
        copy.wait()
    rows, res_total, chan = align_ref.shape
    hidden = left_w_ref.shape[0]
    values = align_ref[...].astype(jnp.float32).reshape(rows * res_total, chan)
    centred = values - jnp.mean(values, axis=-1, keepdims=True)
    spread = jnp.mean(centred * centred, axis=-1, keepdims=True)
    normed = centred * lax.rsqrt(spread + 1e-05) * gain_ref[...] + offset_ref[...]
    weights = jnp.concatenate([left_w_ref[...], right_w_ref[...]], axis=0)
    biases = jnp.concatenate([left_b_ref[...], right_b_ref[...]], axis=1)
    proj_ref[:, : 2 * hidden] = (
        lax.dot_general(
            normed.astype(jnp.bfloat16),
            weights,
            (((1,), (1,)), ((), ())),
            preferred_element_type=jnp.float32,
        )
        + biases
    )
    tiles = [proj_ref[pl.ds(r, rows, stride=res_total), :][:, : 2 * hidden] for r in range(res_total)]
    row_block = res_total // (half_count * rest_count)
    col_block = res_total // seq_count
    for a in range(half_count * rest_count):
        left_ref[a] = jnp.concatenate(
            [t[:, :hidden] for t in tiles[a * row_block : (a + 1) * row_block]], axis=1
        )
    right = [
        jnp.concatenate([t[:, hidden:] for t in tiles[b * col_block : (b + 1) * col_block]], axis=1)
        for b in range(seq_count)
    ]
    half = lax.axis_index("half")
    own = [left_ref[half * rest_count + a] for a in range(rest_count)]
    other = [left_ref[(1 - half) * rest_count + a] for a in range(rest_count)]
    pieces = [
        jnp.concatenate([own[a], other[a], right[b]], axis=1)
        for b, a in peer_order(seq_count, rest_count)
    ]
    group = max(1, 16 // rows)
    for start in range(0, len(pieces), group):
        block = jnp.concatenate(pieces[start : start + group], axis=0)
        send_ref[pl.ds(start * rows, group * rows), :] = block.astype(jnp.bfloat16)


def pair_kernel(own, hidden, row_block, col_block, recv_ref, weight_ref, out_ref, outer_ref):
    seq_total = 2 * recv_ref.shape[0]
    split = row_block * hidden
    left = recv_ref[:, :split] if own else recv_ref[:, split : 2 * split]
    right = recv_ref[:, 2 * split :]
    outer = lax.dot_general(
        left, right, (((0,), (0,)), ((), ())), preferred_element_type=jnp.float32
    )
    for g in range(outer_ref.shape[0]):
        outer_ref[g] = outer[:, g * LANES : (g + 1) * LANES]
    per_group = LANES // hidden
    terms = []
    for g in range(outer_ref.shape[0]):
        slabs = [outer_ref[g, pl.ds(c, row_block, stride=hidden), :] for c in range(hidden)]
        for j in range(per_group):
            flat = jnp.concatenate([s[:, j * hidden : (j + 1) * hidden] for s in slabs], axis=1)
            terms.append(flat)
    flat = jnp.concatenate(terms, axis=0).astype(jnp.bfloat16)
    term = jnp.dot(flat, weight_ref[...], preferred_element_type=jnp.float32)
    out_ref[...] = (term * (1.0 / float(seq_total))).astype(out_ref.dtype)


def add_kernel(mine_ref, came_ref, bias_ref, out_ref, term_ref):
    row_block, col_block, _ = out_ref.shape
    term_ref[...] = mine_ref[...] + came_ref[...].astype(jnp.float32) + bias_ref[...]
    for i in range(row_block):
        out_ref[i] = term_ref[pl.ds(i, col_block, stride=row_block), :].astype(jnp.bfloat16)


def in_hbm(array):
    return pltpu.with_memory_space_constraint(array, pltpu.HBM)


def body(
    alignment,
    layer_norm_gain,
    layer_norm_bias,
    left_projection_weight,
    left_bias,
    right_projection_weight,
    right_bias,
    out_weight,
    out_bias,
):
    seq_count = lax.axis_size("seq")
    half_count = lax.axis_size("half")
    rest_count = lax.axis_size("rest")
    rows, res_total, chan = alignment.shape
    hidden = left_projection_weight.shape[1]
    pair_width = out_weight.shape[1]
    row_block = res_total // (half_count * rest_count)
    col_block = res_total // seq_count
    peers = seq_count * rest_count
    width = (half_count * row_block + col_block) * hidden
    pairs = row_block * col_block
    vmem = pl.BlockSpec(memory_space=pltpu.VMEM)
    hbm = pl.BlockSpec(memory_space=pltpu.HBM)
    params = pltpu.CompilerParams(vmem_limit_bytes=32 * 1024 * 1024)
    send, bias_row = pl.pallas_call(
        functools.partial(project_kernel, seq_count, half_count, rest_count),
        out_shape=[
            jax.ShapeDtypeStruct((peers * rows, width), jnp.bfloat16),
            jax.ShapeDtypeStruct((1, pair_width), jnp.float32),
        ],
        in_specs=[hbm] * 8,
        out_specs=[vmem] * 2,
        scratch_shapes=[
            pltpu.VMEM((rows, res_total, chan), jnp.bfloat16),
            pltpu.VMEM((1, chan), jnp.float32),
            pltpu.VMEM((1, chan), jnp.float32),
            pltpu.VMEM((hidden, chan), jnp.bfloat16),
            pltpu.VMEM((1, hidden), jnp.float32),
            pltpu.VMEM((hidden, chan), jnp.bfloat16),
            pltpu.VMEM((1, hidden), jnp.float32),
            pltpu.VMEM((rows * res_total, LANES), jnp.float32),
            pltpu.VMEM((half_count * rest_count, rows, row_block * hidden), jnp.float32),
            pltpu.SemaphoreType.DMA((8,)),
        ],
        compiler_params=params,
    )(
        in_hbm(alignment),
        in_hbm(layer_norm_gain.reshape(1, chan)),
        in_hbm(layer_norm_bias.reshape(1, chan)),
        in_hbm(left_projection_weight.T),
        in_hbm(left_bias.reshape(1, hidden)),
        in_hbm(right_projection_weight.T),
        in_hbm(right_bias.reshape(1, hidden)),
        in_hbm(out_bias.reshape(1, pair_width)),
    )
    groups = [
        [(b * half_count + h) * rest_count + a for b, a in peer_order(seq_count, rest_count)]
        for h in range(half_count)
    ]
    recv = lax.all_to_all(
        send,
        ("seq", "half", "rest"),
        split_axis=0,
        concat_axis=0,
        tiled=True,
        axis_index_groups=groups,
    )
    outer_values = pairs * hidden * hidden

    def pair_block(own, dtype):
        return pl.pallas_call(
            functools.partial(pair_kernel, own, hidden, row_block, col_block),
            out_shape=jax.ShapeDtypeStruct((pairs, pair_width), dtype),
            in_specs=[vmem] * 2,
            out_specs=vmem,
            scratch_shapes=[
                pltpu.VMEM((col_block * hidden // LANES, row_block * hidden, LANES), jnp.float32)
            ],
            compiler_params=params,
            cost_estimate=pl.CostEstimate(
                flops=2 * outer_values * (recv.shape[0] + pair_width),
                bytes_accessed=2 * (recv.size + out_weight.size),
                transcendentals=0,
            ),
        )(recv, out_weight)

    theirs = pair_block(False, jnp.bfloat16)
    came = lax.ppermute(theirs, "half", [(0, 1), (1, 0)])
    mine = pair_block(True, jnp.float32)
    return pl.pallas_call(
        add_kernel,
        out_shape=jax.ShapeDtypeStruct((row_block, col_block, pair_width), jnp.bfloat16),
        in_specs=[vmem] * 3,
        out_specs=vmem,
        scratch_shapes=[pltpu.VMEM((pairs, pair_width), jnp.float32)],
        compiler_params=params,
    )(mine, came, bias_row)


def solution(mesh):
    seq_count, res_count = mesh.devices.shape
    split = Mesh(mesh.devices.reshape(seq_count, 2, res_count // 2), ("seq", "half", "rest"))
    in_specs = (P(("seq", "half", "rest"), None, None), P(), P(), P(), P(), P(), P(), P(), P())
    out_specs = P(("half", "rest"), "seq", None)
    return jax.shard_map(body, mesh=split, in_specs=in_specs, out_specs=out_specs, check_vma=False)
```

```python
import functools

import jax
import jax.numpy as jnp
from jax import lax
from jax.experimental import pallas as pl
from jax.experimental.pallas import tpu as pltpu
from jax.sharding import Mesh
from jax.sharding import PartitionSpec as P

LANES = 128


def peer_order(seq_count, rest_count):
    peers = [(b, a) for b in range(seq_count) for a in range(rest_count)]
    return peers[-1:] + peers[:-1]


def project_kernel(
    seq_count,
    half_count,
    rest_count,
    align_hbm,
    gain_hbm,
    offset_hbm,
    left_w_hbm,
    left_b_hbm,
    right_w_hbm,
    right_b_hbm,
    out_b_hbm,
    send_ref,
    out_b_ref,
    align_ref,
    gain_ref,
    offset_ref,
    left_w_ref,
    left_b_ref,
    right_w_ref,
    right_b_ref,
    proj_ref,
    left_ref,
    sems,
):
    copies = [
        pltpu.make_async_copy(source, target, sems.at[n])
        for n, (source, target) in enumerate(
            [
                (align_hbm, align_ref),
                (gain_hbm, gain_ref),
                (offset_hbm, offset_ref),
                (left_w_hbm, left_w_ref),
                (left_b_hbm, left_b_ref),
                (right_w_hbm, right_w_ref),
                (right_b_hbm, right_b_ref),
                (out_b_hbm, out_b_ref),
            ]
        )
    ]
    for copy in copies:
        copy.start()
    for copy in copies:
        copy.wait()
    rows, res_total, chan = align_ref.shape
    hidden = left_w_ref.shape[0]
    values = align_ref[...].astype(jnp.float32).reshape(rows * res_total, chan)
    centred = values - jnp.mean(values, axis=-1, keepdims=True)
    spread = jnp.mean(centred * centred, axis=-1, keepdims=True)
    normed = centred * lax.rsqrt(spread + 1e-05) * gain_ref[...] + offset_ref[...]
    weights = jnp.concatenate([left_w_ref[...], right_w_ref[...]], axis=0)
    biases = jnp.concatenate([left_b_ref[...], right_b_ref[...]], axis=1)
    proj_ref[:, : 2 * hidden] = (
        lax.dot_general(
            normed.astype(jnp.bfloat16),
            weights,
            (((1,), (1,)), ((), ())),
            preferred_element_type=jnp.float32,
        )
        + biases
    )
    tiles = [proj_ref[pl.ds(r, rows, stride=res_total), :][:, : 2 * hidden] for r in range(res_total)]
    row_block = res_total // (half_count * rest_count)
    col_block = res_total // seq_count
    for a in range(half_count * rest_count):
        left_ref[a] = jnp.concatenate(
            [t[:, :hidden] for t in tiles[a * row_block : (a + 1) * row_block]], axis=1
        )
    right = [
        jnp.concatenate([t[:, hidden:] for t in tiles[b * col_block : (b + 1) * col_block]], axis=1)
        for b in range(seq_count)
    ]
    half = lax.axis_index("half")
    own = [left_ref[half * rest_count + a] for a in range(rest_count)]
    other = [left_ref[(1 - half) * rest_count + a] for a in range(rest_count)]
    pieces = [
        jnp.concatenate([own[a], other[a], right[b]], axis=1)
        for b, a in peer_order(seq_count, rest_count)
    ]
    group = max(1, 16 // rows)
    for start in range(0, len(pieces), group):
        block = jnp.concatenate(pieces[start : start + group], axis=0)
        send_ref[pl.ds(start * rows, group * rows), :] = block.astype(jnp.bfloat16)


def pair_kernel(own, hidden, row_block, col_block, recv_ref, weight_ref, out_ref, outer_ref):
    seq_total = 2 * recv_ref.shape[0]
    split = row_block * hidden
    left = recv_ref[:, :split] if own else recv_ref[:, split : 2 * split]
    right = recv_ref[:, 2 * split :]
    outer = lax.dot_general(
        left, right, (((0,), (0,)), ((), ())), preferred_element_type=jnp.float32
    )
    for g in range(outer_ref.shape[0]):
        outer_ref[g] = outer[:, g * LANES : (g + 1) * LANES]
    per_group = LANES // hidden
    terms = []
    for g in range(outer_ref.shape[0]):
        slabs = [outer_ref[g, pl.ds(c, row_block, stride=hidden), :] for c in range(hidden)]
        for j in range(per_group):
            flat = jnp.concatenate([s[:, j * hidden : (j + 1) * hidden] for s in slabs], axis=1)
            terms.append(flat)
    flat = jnp.concatenate(terms, axis=0).astype(jnp.bfloat16)
    term = jnp.dot(flat, weight_ref[...], preferred_element_type=jnp.float32)
    out_ref[...] = (term * (1.0 / float(seq_total))).astype(out_ref.dtype)


def add_kernel(mine_ref, came_ref, bias_ref, out_ref, term_ref):
    row_block, col_block, _ = out_ref.shape
    term_ref[...] = mine_ref[...] + came_ref[...].astype(jnp.float32) + bias_ref[...]
    for i in range(row_block):
        out_ref[i] = term_ref[pl.ds(i, col_block, stride=row_block), :].astype(jnp.bfloat16)


def in_hbm(array):
    return pltpu.with_memory_space_constraint(array, pltpu.HBM)


def body(
    alignment,
    layer_norm_gain,
    layer_norm_bias,
    left_projection_weight,
    left_bias,
    right_projection_weight,
    right_bias,
    out_weight,
    out_bias,
):
    seq_count = lax.axis_size("seq")
    half_count = lax.axis_size("half")
    rest_count = lax.axis_size("rest")
    rows, res_total, chan = alignment.shape
    hidden = left_projection_weight.shape[1]
    pair_width = out_weight.shape[1]
    row_block = res_total // (half_count * rest_count)
    col_block = res_total // seq_count
    peers = seq_count * rest_count
    width = (half_count * row_block + col_block) * hidden
    pairs = row_block * col_block
    vmem = pl.BlockSpec(memory_space=pltpu.VMEM)
    hbm = pl.BlockSpec(memory_space=pltpu.HBM)
    params = pltpu.CompilerParams(vmem_limit_bytes=32 * 1024 * 1024)
    send, bias_row = pl.pallas_call(
        functools.partial(project_kernel, seq_count, half_count, rest_count),
        out_shape=[
            jax.ShapeDtypeStruct((peers * rows, width), jnp.bfloat16),
            jax.ShapeDtypeStruct((1, pair_width), jnp.float32),
        ],
        in_specs=[hbm] * 8,
        out_specs=[vmem] * 2,
        scratch_shapes=[
            pltpu.VMEM((rows, res_total, chan), jnp.bfloat16),
            pltpu.VMEM((1, chan), jnp.float32),
            pltpu.VMEM((1, chan), jnp.float32),
            pltpu.VMEM((hidden, chan), jnp.bfloat16),
            pltpu.VMEM((1, hidden), jnp.float32),
            pltpu.VMEM((hidden, chan), jnp.bfloat16),
            pltpu.VMEM((1, hidden), jnp.float32),
            pltpu.VMEM((rows * res_total, LANES), jnp.float32),
            pltpu.VMEM((half_count * rest_count, rows, row_block * hidden), jnp.float32),
            pltpu.SemaphoreType.DMA((8,)),
        ],
        compiler_params=params,
    )(
        in_hbm(alignment),
        in_hbm(layer_norm_gain.reshape(1, chan)),
        in_hbm(layer_norm_bias.reshape(1, chan)),
        in_hbm(left_projection_weight.T),
        in_hbm(left_bias.reshape(1, hidden)),
        in_hbm(right_projection_weight.T),
        in_hbm(right_bias.reshape(1, hidden)),
        in_hbm(out_bias.reshape(1, pair_width)),
    )
    groups = [
        [(b * half_count + h) * rest_count + a for b, a in peer_order(seq_count, rest_count)]
        for h in range(half_count)
    ]
    recv = lax.all_to_all(
        send,
        ("seq", "half", "rest"),
        split_axis=0,
        concat_axis=0,
        tiled=True,
        axis_index_groups=groups,
    )
    outer_values = pairs * hidden * hidden

    def pair_block(own, dtype):
        return pl.pallas_call(
            functools.partial(pair_kernel, own, hidden, row_block, col_block),
            out_shape=jax.ShapeDtypeStruct((pairs, pair_width), dtype),
            in_specs=[vmem] * 2,
            out_specs=vmem,
            scratch_shapes=[
                pltpu.VMEM((col_block * hidden // LANES, row_block * hidden, LANES), jnp.float32)
            ],
            compiler_params=params,
            cost_estimate=pl.CostEstimate(
                flops=2 * outer_values * (recv.shape[0] + pair_width),
                bytes_accessed=2 * (recv.size + out_weight.size),
                transcendentals=0,
            ),
        )(recv, out_weight)

    theirs = pair_block(False, jnp.bfloat16)
    came = lax.ppermute(theirs, "half", [(0, 1), (1, 0)])
    mine = pair_block(True, jnp.float32)
    return pl.pallas_call(
        add_kernel,
        out_shape=jax.ShapeDtypeStruct((row_block, col_block, pair_width), jnp.bfloat16),
        in_specs=[vmem] * 3,
        out_specs=vmem,
        scratch_shapes=[pltpu.VMEM((pairs, pair_width), jnp.float32)],
        compiler_params=params,
    )(mine, came, bias_row)


def solution(mesh):
    seq_count, res_count = mesh.devices.shape
    split = Mesh(mesh.devices.reshape(seq_count, 2, res_count // 2), ("seq", "half", "rest"))
    in_specs = (P(("seq", "half", "rest"), None, None), P(), P(), P(), P(), P(), P(), P(), P())
    out_specs = P(("half", "rest"), "seq", None)
    return jax.shard_map(body, mesh=split, in_specs=in_specs, out_specs=out_specs, check_vma=False)
```

```python
import functools

import jax
import jax.numpy as jnp
from jax import lax
from jax.experimental import pallas as pl
from jax.experimental.pallas import tpu as pltpu
from jax.sharding import Mesh
from jax.sharding import PartitionSpec as P

LANES = 128


def peer_order(seq_count, rest_count):
    peers = [(b, a) for b in range(seq_count) for a in range(rest_count)]
    return peers[-1:] + peers[:-1]


def project_kernel(
    seq_count,
    half_count,
    rest_count,
    align_hbm,
    gain_hbm,
    offset_hbm,
    left_w_hbm,
    left_b_hbm,
    right_w_hbm,
    right_b_hbm,
    out_b_hbm,
    send_ref,
    out_b_ref,
    align_ref,
    gain_ref,
    offset_ref,
    left_w_ref,
    left_b_ref,
    right_w_ref,
    right_b_ref,
    proj_ref,
    left_ref,
    sems,
):
    step = max(1, align_ref.shape[0] // 4)
    cuts = [pl.ds(at, step) for at in range(0, align_ref.shape[0], step)]
    copies = [
        pltpu.make_async_copy(source, target, sems.at[n])
        for n, (source, target) in enumerate(
            [(align_hbm.at[cut], align_ref.at[cut]) for cut in cuts]
            + [
                (gain_hbm, gain_ref),
                (offset_hbm, offset_ref),
                (left_w_hbm, left_w_ref),
                (left_b_hbm, left_b_ref),
                (right_w_hbm, right_w_ref),
                (right_b_hbm, right_b_ref),
                (out_b_hbm, out_b_ref),
            ]
        )
    ]
    for copy in copies:
        copy.start()
    for copy in copies:
        copy.wait()
    rows, res_total, chan = align_ref.shape
    hidden = left_w_ref.shape[0]
    values = align_ref[...].astype(jnp.float32).reshape(rows * res_total, chan)
    centred = values - jnp.mean(values, axis=-1, keepdims=True)
    spread = jnp.mean(centred * centred, axis=-1, keepdims=True)
    normed = centred * lax.rsqrt(spread + 1e-05) * gain_ref[...] + offset_ref[...]
    weights = jnp.concatenate([left_w_ref[...], right_w_ref[...]], axis=0)
    biases = jnp.concatenate([left_b_ref[...], right_b_ref[...]], axis=1)
    proj_ref[:, : 2 * hidden] = (
        lax.dot_general(
            normed.astype(jnp.bfloat16),
            weights,
            (((1,), (1,)), ((), ())),
            preferred_element_type=jnp.float32,
        )
        + biases
    )
    tiles = [proj_ref[pl.ds(r, rows, stride=res_total), :][:, : 2 * hidden] for r in range(res_total)]
    row_block = res_total // (half_count * rest_count)
    col_block = res_total // seq_count
    for a in range(half_count * rest_count):
        left_ref[a] = jnp.concatenate(
            [t[:, :hidden] for t in tiles[a * row_block : (a + 1) * row_block]], axis=1
        )
    order = column_order(col_block, LANES // hidden)
    right = [
        jnp.concatenate([tiles[b * col_block + j][:, hidden:] for j in order], axis=1)
        for b in range(seq_count)
    ]
    half = lax.axis_index("half")
    own = [left_ref[half * rest_count + a] for a in range(rest_count)]
    other = [left_ref[(1 - half) * rest_count + a] for a in range(rest_count)]
    pieces = [
        jnp.concatenate([own[a], other[a], right[b]], axis=1)
        for b, a in peer_order(seq_count, rest_count)
    ]
    group = max(1, 16 // rows)
    for start in range(0, len(pieces), group):
        block = jnp.concatenate(pieces[start : start + group], axis=0)
        send_ref[pl.ds(start * rows, group * rows), :] = block.astype(jnp.bfloat16)


def pair_kernel(own, hidden, row_block, col_block, recv_ref, weight_ref, out_ref, left_ref):
    seqs = recv_ref.shape[0]
    split = row_block * hidden
    left = recv_ref[:, :split] if own else recv_ref[:, split : 2 * split]
    right = recv_ref[:, 2 * split :]
    turned = left.astype(jnp.float32).T
    parts = left_ref.shape[0]
    for n in range(parts):
        left_ref[n] = turned[:, n * LANES : (n + 1) * LANES]
    left = jnp.concatenate(
        [
            jnp.concatenate(
                [left_ref[n, pl.ds(c, row_block, stride=hidden), :] for n in range(parts)], axis=1
            )
            for c in range(hidden)
        ],
        axis=0,
    ).astype(jnp.bfloat16)
    outer = jnp.dot(left, right, preferred_element_type=jnp.float32)
    per_group = LANES // hidden
    lane_block = lax.broadcasted_iota(jnp.int32, (2 * row_block, LANES), 1) // hidden
    rows = []
    for g in range(0, col_block // per_group, 2):
        lines = [[] for _ in range(per_group)]
        for c in range(0, hidden, per_group):
            rolled = []
            for k in range(per_group):
                at = (c + k) * row_block
                tile = jnp.concatenate(
                    [
                        outer[at : at + row_block, (g + h) * LANES : (g + h + 1) * LANES]
                        for h in range(2)
                    ],
                    axis=0,
                )
                rolled.append(roll_blocks(tile.astype(jnp.bfloat16), k, hidden))
            for j in range(per_group):
                mixed = rolled[(per_group - 1 - j) % per_group]
                for p in range(per_group - 1):
                    mixed = jnp.where(lane_block == p, rolled[(p - j) % per_group], mixed)
                lines[j].append(roll_blocks(mixed, -j, hidden))
        rows += [jnp.concatenate(line, axis=1) for line in lines]
    flat = jnp.concatenate(rows, axis=0)
    term = jnp.dot(flat, weight_ref[...], preferred_element_type=jnp.float32)
    out_ref[...] = (term * (1.0 / float(2 * seqs))).astype(out_ref.dtype)


def roll_blocks(tile, count, hidden):
    shift = count * hidden % LANES
    return pltpu.roll(tile, shift, 1) if shift else tile


def column_order(col_block, per_group):
    double = 2 * per_group
    return [
        double * (p // double) + 2 * (p % per_group) + (p // per_group) % 2 for p in range(col_block)
    ]


def add_kernel(mine_ref, came_ref, bias_ref, out_ref, term_ref):
    row_block, col_block, _ = out_ref.shape
    term_ref[...] = mine_ref[...] + came_ref[...].astype(jnp.float32) + bias_ref[...]
    for i in range(row_block):
        out_ref[i] = term_ref[pl.ds(i, col_block, stride=row_block), :].astype(jnp.bfloat16)


def in_hbm(array):
    return pltpu.with_memory_space_constraint(array, pltpu.HBM)


def body(
    alignment,
    layer_norm_gain,
    layer_norm_bias,
    left_projection_weight,
    left_bias,
    right_projection_weight,
    right_bias,
    out_weight,
    out_bias,
):
    seq_count = lax.axis_size("seq")
    half_count = lax.axis_size("half")
    rest_count = lax.axis_size("rest")
    rows, res_total, chan = alignment.shape
    hidden = left_projection_weight.shape[1]
    pair_width = out_weight.shape[1]
    row_block = res_total // (half_count * rest_count)
    col_block = res_total // seq_count
    peers = seq_count * rest_count
    width = (half_count * row_block + col_block) * hidden
    pairs = row_block * col_block
    vmem = pl.BlockSpec(memory_space=pltpu.VMEM)
    hbm = pl.BlockSpec(memory_space=pltpu.HBM)
    params = pltpu.CompilerParams(vmem_limit_bytes=32 * 1024 * 1024)
    send, bias_row = pl.pallas_call(
        functools.partial(project_kernel, seq_count, half_count, rest_count),
        out_shape=[
            jax.ShapeDtypeStruct((peers * rows, width), jnp.bfloat16),
            jax.ShapeDtypeStruct((1, pair_width), jnp.float32),
        ],
        in_specs=[hbm] * 8,
        out_specs=[vmem] * 2,
        scratch_shapes=[
            pltpu.VMEM((rows, res_total, chan), jnp.bfloat16),
            pltpu.VMEM((1, chan), jnp.float32),
            pltpu.VMEM((1, chan), jnp.float32),
            pltpu.VMEM((hidden, chan), jnp.bfloat16),
            pltpu.VMEM((1, hidden), jnp.float32),
            pltpu.VMEM((hidden, chan), jnp.bfloat16),
            pltpu.VMEM((1, hidden), jnp.float32),
            pltpu.VMEM((rows * res_total, LANES), jnp.float32),
            pltpu.VMEM((half_count * rest_count, rows, row_block * hidden), jnp.float32),
            pltpu.SemaphoreType.DMA((7 + rows // max(1, rows // 4),)),
        ],
        compiler_params=params,
    )(
        in_hbm(alignment),
        in_hbm(layer_norm_gain.reshape(1, chan)),
        in_hbm(layer_norm_bias.reshape(1, chan)),
        in_hbm(left_projection_weight.T),
        in_hbm(left_bias.reshape(1, hidden)),
        in_hbm(right_projection_weight.T),
        in_hbm(right_bias.reshape(1, hidden)),
        in_hbm(out_bias.reshape(1, pair_width)),
    )
    groups = [
        [(b * half_count + h) * rest_count + a for b, a in peer_order(seq_count, rest_count)]
        for h in range(half_count)
    ]
    recv = lax.all_to_all(
        send,
        ("seq", "half", "rest"),
        split_axis=0,
        concat_axis=0,
        tiled=True,
        axis_index_groups=groups,
    )
    outer_values = pairs * hidden * hidden

    def pair_block(own, dtype):
        return pl.pallas_call(
            functools.partial(pair_kernel, own, hidden, row_block, col_block),
            out_shape=jax.ShapeDtypeStruct((pairs, pair_width), dtype),
            in_specs=[vmem] * 2,
            out_specs=vmem,
            scratch_shapes=[
                pltpu.VMEM((recv.shape[0] // LANES, row_block * hidden, LANES), jnp.float32)
            ],
            compiler_params=params,
            cost_estimate=pl.CostEstimate(
                flops=2 * outer_values * (recv.shape[0] + pair_width),
                bytes_accessed=2 * (recv.size + out_weight.size),
                transcendentals=0,
            ),
        )(recv, out_weight)

    theirs = pair_block(False, jnp.bfloat16)
    came = lax.ppermute(theirs, "half", [(0, 1), (1, 0)])
    mine = pair_block(True, jnp.float32)
    return pl.pallas_call(
        add_kernel,
        out_shape=jax.ShapeDtypeStruct((row_block, col_block, pair_width), jnp.bfloat16),
        in_specs=[vmem] * 3,
        out_specs=vmem,
        scratch_shapes=[pltpu.VMEM((pairs, pair_width), jnp.float32)],
        compiler_params=params,
    )(mine, came, bias_row)


def solution(mesh):
    seq_count, res_count = mesh.devices.shape
    split = Mesh(mesh.devices.reshape(seq_count, 2, res_count // 2), ("seq", "half", "rest"))
    in_specs = (P(("seq", "half", "rest"), None, None), P(), P(), P(), P(), P(), P(), P(), P())
    out_specs = P(("half", "rest"), "seq", None)
    return jax.shard_map(body, mesh=split, in_specs=in_specs, out_specs=out_specs, check_vma=False)
```

```python
import functools

import jax
import jax.numpy as jnp
from jax import lax
from jax.experimental import pallas as pl
from jax.experimental.pallas import tpu as pltpu
from jax.sharding import Mesh
from jax.sharding import PartitionSpec as P

LANES = 128


def peer_order(seq_count, rest_count):
    peers = [(b, a) for b in range(seq_count) for a in range(rest_count)]
    return peers[-1:] + peers[:-1]


def project_kernel(
    seq_count,
    half_count,
    rest_count,
    align_hbm,
    gain_hbm,
    offset_hbm,
    left_w_hbm,
    left_b_hbm,
    right_w_hbm,
    right_b_hbm,
    out_b_hbm,
    send_ref,
    out_b_ref,
    align_ref,
    gain_ref,
    offset_ref,
    left_w_ref,
    left_b_ref,
    right_w_ref,
    right_b_ref,
    proj_ref,
    left_ref,
    sems,
):
    rows, res_total, chan = align_ref.shape
    hidden = left_w_ref.shape[0]
    align, left_w, right_w, gain, offset, left_b, right_b, out_b = [
        pltpu.make_async_copy(source, target, sems.at[n])
        for n, (source, target) in enumerate(
            [
                (align_hbm, align_ref),
                (left_w_hbm, left_w_ref),
                (right_w_hbm, right_w_ref),
                (gain_hbm, gain_ref),
                (offset_hbm, offset_ref),
                (left_b_hbm, left_b_ref),
                (right_b_hbm, right_b_ref),
                (out_b_hbm, out_b_ref),
            ]
        )
    ]
    for copy in (align, left_w, right_w, gain, offset, left_b, right_b, out_b):
        copy.start()
    align.wait()
    values = align_ref[...].astype(jnp.float32).reshape(rows * res_total, chan)
    centred = values - jnp.mean(values, axis=-1, keepdims=True)
    spread = jnp.mean(centred * centred, axis=-1, keepdims=True)
    scaled = centred * lax.rsqrt(spread + 1e-05)
    for copy in (left_w, right_w, gain, offset):
        copy.wait()
    normed = (scaled * gain_ref[...] + offset_ref[...]).astype(jnp.bfloat16)
    repeats = LANES // hidden
    weights = jnp.concatenate([left_w_ref[...]] * repeats + [right_w_ref[...]] * repeats, axis=0)
    both = lax.dot_general(
        normed, weights, (((1,), (1,)), ((), ())), preferred_element_type=jnp.float32
    )
    for copy in (left_b, right_b, out_b):
        copy.wait()
    proj_ref[0] = both[:, :LANES] + jnp.concatenate([left_b_ref[...]] * repeats, axis=1)
    proj_ref[1] = both[:, LANES:] + jnp.concatenate([right_b_ref[...]] * repeats, axis=1)
    lane_block = lax.broadcasted_iota(jnp.int32, (rows, LANES), 1) // hidden

    def lined_up(side, residues):
        tiles = [proj_ref[side, pl.ds(r, rows, stride=res_total), :] for r in residues]
        lines = []
        for at in range(0, len(tiles), repeats):
            line = tiles[at]
            for p in range(1, repeats):
                line = jnp.where(lane_block == p, tiles[at + p], line)
            lines.append(line)
        return jnp.concatenate(lines, axis=1)

    row_block = res_total // (half_count * rest_count)
    col_block = res_total // seq_count
    order = column_order(col_block, repeats)
    for a in range(half_count * rest_count):
        left_ref[a] = lined_up(0, [a * row_block + i for i in range(row_block)])
    right = [lined_up(1, [b * col_block + j for j in order]) for b in range(seq_count)]
    half = lax.axis_index("half")
    own = [left_ref[half * rest_count + a] for a in range(rest_count)]
    other = [left_ref[(1 - half) * rest_count + a] for a in range(rest_count)]
    pieces = [
        jnp.concatenate([own[a], other[a], right[b]], axis=1)
        for b, a in peer_order(seq_count, rest_count)
    ]
    group = max(1, 16 // rows)
    for start in range(0, len(pieces), group):
        block = jnp.concatenate(pieces[start : start + group], axis=0)
        send_ref[pl.ds(start * rows, group * rows), :] = block.astype(jnp.bfloat16)


def pair_kernel(own, hidden, row_block, col_block, recv_ref, weight_ref, out_ref, left_ref):
    seqs = recv_ref.shape[0]
    split = row_block * hidden
    left = recv_ref[:, :split] if own else recv_ref[:, split : 2 * split]
    right = recv_ref[:, 2 * split :]
    turned = left.astype(jnp.float32).T
    parts = left_ref.shape[0]
    for n in range(parts):
        left_ref[n] = turned[:, n * LANES : (n + 1) * LANES]
    left = jnp.concatenate(
        [
            jnp.concatenate(
                [left_ref[n, pl.ds(c, row_block, stride=hidden), :] for n in range(parts)], axis=1
            )
            for c in range(hidden)
        ],
        axis=0,
    ).astype(jnp.bfloat16)
    outer = jnp.dot(left, right, preferred_element_type=jnp.float32)
    per_group = LANES // hidden
    lane_block = lax.broadcasted_iota(jnp.int32, (2 * row_block, LANES), 1) // hidden
    rows = []
    for g in range(0, col_block // per_group, 2):
        lines = [[] for _ in range(per_group)]
        for c in range(0, hidden, per_group):
            rolled = []
            for k in range(per_group):
                at = (c + k) * row_block
                tile = jnp.concatenate(
                    [
                        outer[at : at + row_block, (g + h) * LANES : (g + h + 1) * LANES]
                        for h in range(2)
                    ],
                    axis=0,
                )
                rolled.append(roll_blocks(tile.astype(jnp.bfloat16), k, hidden))
            for j in range(per_group):
                mixed = rolled[(per_group - 1 - j) % per_group]
                for p in range(per_group - 1):
                    mixed = jnp.where(lane_block == p, rolled[(p - j) % per_group], mixed)
                lines[j].append(roll_blocks(mixed, -j, hidden))
        rows += [jnp.concatenate(line, axis=1) for line in lines]
    flat = jnp.concatenate(rows, axis=0)
    term = jnp.dot(flat, weight_ref[...], preferred_element_type=jnp.float32)
    out_ref[...] = (term * (1.0 / float(2 * seqs))).astype(out_ref.dtype)


def roll_blocks(tile, count, hidden):
    shift = count * hidden % LANES
    return pltpu.roll(tile, shift, 1) if shift else tile


def column_order(col_block, per_group):
    double = 2 * per_group
    return [
        double * (p // double) + 2 * (p % per_group) + (p // per_group) % 2 for p in range(col_block)
    ]


def add_kernel(mine_ref, came_ref, bias_ref, out_ref, term_ref):
    row_block, col_block, _ = out_ref.shape
    term_ref[...] = mine_ref[...] + came_ref[...].astype(jnp.float32) + bias_ref[...]
    for i in range(row_block):
        out_ref[i] = term_ref[pl.ds(i, col_block, stride=row_block), :].astype(jnp.bfloat16)


def in_hbm(array):
    return pltpu.with_memory_space_constraint(array, pltpu.HBM)


def body(
    alignment,
    layer_norm_gain,
    layer_norm_bias,
    left_projection_weight,
    left_bias,
    right_projection_weight,
    right_bias,
    out_weight,
    out_bias,
):
    seq_count = lax.axis_size("seq")
    half_count = lax.axis_size("half")
    rest_count = lax.axis_size("rest")
    rows, res_total, chan = alignment.shape
    hidden = left_projection_weight.shape[1]
    pair_width = out_weight.shape[1]
    row_block = res_total // (half_count * rest_count)
    col_block = res_total // seq_count
    peers = seq_count * rest_count
    width = (half_count * row_block + col_block) * hidden
    pairs = row_block * col_block
    vmem = pl.BlockSpec(memory_space=pltpu.VMEM)
    hbm = pl.BlockSpec(memory_space=pltpu.HBM)
    params = pltpu.CompilerParams(vmem_limit_bytes=32 * 1024 * 1024)
    send, bias_row = pl.pallas_call(
        functools.partial(project_kernel, seq_count, half_count, rest_count),
        out_shape=[
            jax.ShapeDtypeStruct((peers * rows, width), jnp.bfloat16),
            jax.ShapeDtypeStruct((1, pair_width), jnp.float32),
        ],
        in_specs=[hbm] * 8,
        out_specs=[vmem] * 2,
        scratch_shapes=[
            pltpu.VMEM((rows, res_total, chan), jnp.bfloat16),
            pltpu.VMEM((1, chan), jnp.float32),
            pltpu.VMEM((1, chan), jnp.float32),
            pltpu.VMEM((hidden, chan), jnp.bfloat16),
            pltpu.VMEM((1, hidden), jnp.float32),
            pltpu.VMEM((hidden, chan), jnp.bfloat16),
            pltpu.VMEM((1, hidden), jnp.float32),
            pltpu.VMEM((2, rows * res_total, LANES), jnp.float32),
            pltpu.VMEM((half_count * rest_count, rows, row_block * hidden), jnp.float32),
            pltpu.SemaphoreType.DMA((8,)),
        ],
        compiler_params=params,
    )(
        in_hbm(alignment),
        in_hbm(layer_norm_gain.reshape(1, chan)),
        in_hbm(layer_norm_bias.reshape(1, chan)),
        in_hbm(left_projection_weight.T),
        in_hbm(left_bias.reshape(1, hidden)),
        in_hbm(right_projection_weight.T),
        in_hbm(right_bias.reshape(1, hidden)),
        in_hbm(out_bias.reshape(1, pair_width)),
    )
    groups = [
        [(b * half_count + h) * rest_count + a for b, a in peer_order(seq_count, rest_count)]
        for h in range(half_count)
    ]
    recv = lax.all_to_all(
        send,
        ("seq", "half", "rest"),
        split_axis=0,
        concat_axis=0,
        tiled=True,
        axis_index_groups=groups,
    )
    outer_values = pairs * hidden * hidden

    def pair_block(own, dtype):
        return pl.pallas_call(
            functools.partial(pair_kernel, own, hidden, row_block, col_block),
            out_shape=jax.ShapeDtypeStruct((pairs, pair_width), dtype),
            in_specs=[vmem] * 2,
            out_specs=vmem,
            scratch_shapes=[
                pltpu.VMEM((recv.shape[0] // LANES, row_block * hidden, LANES), jnp.float32)
            ],
            compiler_params=params,
            cost_estimate=pl.CostEstimate(
                flops=2 * outer_values * (recv.shape[0] + pair_width),
                bytes_accessed=2 * (recv.size + out_weight.size),
                transcendentals=0,
            ),
        )(recv, out_weight)

    theirs = pair_block(False, jnp.bfloat16)
    came = lax.ppermute(theirs, "half", [(0, 1), (1, 0)])
    mine = pair_block(True, jnp.float32)
    return pl.pallas_call(
        add_kernel,
        out_shape=jax.ShapeDtypeStruct((row_block, col_block, pair_width), jnp.bfloat16),
        in_specs=[vmem] * 3,
        out_specs=vmem,
        scratch_shapes=[pltpu.VMEM((pairs, pair_width), jnp.float32)],
        compiler_params=params,
    )(mine, came, bias_row)


def solution(mesh):
    seq_count, res_count = mesh.devices.shape
    split = Mesh(mesh.devices.reshape(seq_count, 2, res_count // 2), ("seq", "half", "rest"))
    in_specs = (P(("seq", "half", "rest"), None, None), P(), P(), P(), P(), P(), P(), P(), P())
    out_specs = P(("half", "rest"), "seq", None)
    return jax.shard_map(body, mesh=split, in_specs=in_specs, out_specs=out_specs, check_vma=False)
```

```python
import functools

import jax
import jax.numpy as jnp
from jax import lax
from jax.experimental import pallas as pl
from jax.experimental.pallas import tpu as pltpu
from jax.sharding import Mesh
from jax.sharding import PartitionSpec as P

LANES = 128


def peer_order(seq_count, rest_count):
    peers = [(b, a) for a in range(rest_count) for b in range(seq_count)]
    return peers[-1:] + peers[:-1]


def project_kernel(
    seq_count,
    half_count,
    rest_count,
    align_hbm,
    gain_hbm,
    offset_hbm,
    left_w_hbm,
    left_b_hbm,
    right_w_hbm,
    right_b_hbm,
    out_b_hbm,
    send_ref,
    out_b_ref,
    align_ref,
    gain_ref,
    offset_ref,
    left_w_ref,
    left_b_ref,
    right_w_ref,
    right_b_ref,
    proj_ref,
    left_ref,
    sems,
):
    copies = [
        pltpu.make_async_copy(source, target, sems.at[n])
        for n, (source, target) in enumerate(
            [
                (align_hbm, align_ref),
                (left_w_hbm, left_w_ref),
                (right_w_hbm, right_w_ref),
                (gain_hbm, gain_ref),
                (offset_hbm, offset_ref),
                (left_b_hbm, left_b_ref),
                (right_b_hbm, right_b_ref),
                (out_b_hbm, out_b_ref),
            ]
        )
    ]
    for copy in copies:
        copy.start()
    for copy in copies:
        copy.wait()
    rows, res_total, chan = align_ref.shape
    hidden = left_w_ref.shape[0]
    weights = jnp.concatenate([left_w_ref[...], right_w_ref[...]], axis=0)
    scaled = (weights.astype(jnp.float32) * gain_ref[...]).astype(jnp.bfloat16)
    inner = (((1,), (1,)), ((), ()))
    raw = align_ref[...].reshape(rows * res_total, chan)
    product = lax.dot_general(raw, scaled, inner, preferred_element_type=jnp.float32)
    ones = jnp.ones((8, chan), jnp.bfloat16)
    sums = lax.dot_general(ones, scaled, inner, preferred_element_type=jnp.float32)[:1]
    offset = jnp.broadcast_to(offset_ref[...], (8, chan))
    high = offset.astype(jnp.bfloat16)
    low = (offset - high.astype(jnp.float32)).astype(jnp.bfloat16)
    shift = (
        lax.dot_general(high, weights, inner, preferred_element_type=jnp.float32)
        + lax.dot_general(low, weights, inner, preferred_element_type=jnp.float32)
    )[:1] + jnp.concatenate([left_b_ref[...], right_b_ref[...]], axis=1)
    values = raw.astype(jnp.float32)
    centre = jnp.mean(values, axis=-1, keepdims=True)
    centred = values - centre
    spread = jnp.mean(centred * centred, axis=-1, keepdims=True)
    proj_ref[:, : 2 * hidden] = (product - centre * sums) * lax.rsqrt(spread + 1e-05) + shift
    tiles = [proj_ref[pl.ds(r, rows, stride=res_total), :][:, : 2 * hidden] for r in range(res_total)]
    row_block = res_total // (half_count * rest_count)
    col_block = res_total // seq_count
    for a in range(half_count * rest_count):
        left_ref[a] = jnp.concatenate(
            [t[:, :hidden] for t in tiles[a * row_block : (a + 1) * row_block]], axis=1
        )
    order = column_order(col_block, LANES // hidden)
    right = [
        jnp.concatenate([tiles[b * col_block + j][:, hidden:] for j in order], axis=1)
        for b in range(seq_count)
    ]
    half = lax.axis_index("half")
    own = [left_ref[half * rest_count + a] for a in range(rest_count)]
    other = [left_ref[(1 - half) * rest_count + a] for a in range(rest_count)]
    pieces = [
        jnp.concatenate([own[a], other[a], right[b]], axis=1)
        for b, a in peer_order(seq_count, rest_count)
    ]
    group = max(1, 16 // rows)
    for start in range(0, len(pieces), group):
        block = jnp.concatenate(pieces[start : start + group], axis=0)
        send_ref[pl.ds(start * rows, group * rows), :] = block.astype(jnp.bfloat16)


def pair_kernel(own, hidden, row_block, col_block, recv_ref, weight_ref, out_ref, left_ref):
    seqs = recv_ref.shape[0]
    split = row_block * hidden
    left = recv_ref[:, :split] if own else recv_ref[:, split : 2 * split]
    right = recv_ref[:, 2 * split :]
    turned = left.astype(jnp.float32).T
    parts = left_ref.shape[0]
    for n in range(parts):
        left_ref[n] = turned[:, n * LANES : (n + 1) * LANES]
    left = jnp.concatenate(
        [
            jnp.concatenate(
                [left_ref[n, pl.ds(c, row_block, stride=hidden), :] for n in range(parts)], axis=1
            )
            for c in range(hidden)
        ],
        axis=0,
    ).astype(jnp.bfloat16)
    outer = jnp.dot(left, right, preferred_element_type=jnp.float32)
    per_group = LANES // hidden
    lane_block = lax.broadcasted_iota(jnp.int32, (2 * row_block, LANES), 1) // hidden
    rows = []
    for g in range(0, col_block // per_group, 2):
        lines = [[] for _ in range(per_group)]
        for c in range(0, hidden, per_group):
            rolled = []
            for k in range(per_group):
                at = (c + k) * row_block
                tile = jnp.concatenate(
                    [
                        outer[at : at + row_block, (g + h) * LANES : (g + h + 1) * LANES]
                        for h in range(2)
                    ],
                    axis=0,
                )
                rolled.append(roll_blocks(tile.astype(jnp.bfloat16), k, hidden))
            for j in range(per_group):
                mixed = rolled[(per_group - 1 - j) % per_group]
                for p in range(per_group - 1):
                    mixed = jnp.where(lane_block == p, rolled[(p - j) % per_group], mixed)
                lines[j].append(roll_blocks(mixed, -j, hidden))
        rows += [jnp.concatenate(line, axis=1) for line in lines]
    flat = jnp.concatenate(rows, axis=0)
    term = jnp.dot(flat, weight_ref[...], preferred_element_type=jnp.float32)
    out_ref[...] = (term * (1.0 / float(2 * seqs))).astype(out_ref.dtype)


def roll_blocks(tile, count, hidden):
    shift = count * hidden % LANES
    return pltpu.roll(tile, shift, 1) if shift else tile


def column_order(col_block, per_group):
    double = 2 * per_group
    return [
        double * (p // double) + 2 * (p % per_group) + (p // per_group) % 2 for p in range(col_block)
    ]


def add_kernel(mine_ref, came_ref, bias_ref, out_ref, term_ref):
    row_block, col_block, _ = out_ref.shape
    term_ref[...] = mine_ref[...] + came_ref[...].astype(jnp.float32) + bias_ref[...]
    for i in range(row_block):
        out_ref[i] = term_ref[pl.ds(i, col_block, stride=row_block), :].astype(jnp.bfloat16)


def in_hbm(array):
    return pltpu.with_memory_space_constraint(array, pltpu.HBM)


def body(
    alignment,
    layer_norm_gain,
    layer_norm_bias,
    left_projection_weight,
    left_bias,
    right_projection_weight,
    right_bias,
    out_weight,
    out_bias,
):
    seq_count = lax.axis_size("seq")
    half_count = lax.axis_size("half")
    rest_count = lax.axis_size("rest")
    rows, res_total, chan = alignment.shape
    hidden = left_projection_weight.shape[1]
    pair_width = out_weight.shape[1]
    row_block = res_total // (half_count * rest_count)
    col_block = res_total // seq_count
    peers = seq_count * rest_count
    width = (half_count * row_block + col_block) * hidden
    pairs = row_block * col_block
    vmem = pl.BlockSpec(memory_space=pltpu.VMEM)
    hbm = pl.BlockSpec(memory_space=pltpu.HBM)
    params = pltpu.CompilerParams(vmem_limit_bytes=32 * 1024 * 1024)
    send, bias_row = pl.pallas_call(
        functools.partial(project_kernel, seq_count, half_count, rest_count),
        out_shape=[
            jax.ShapeDtypeStruct((peers * rows, width), jnp.bfloat16),
            jax.ShapeDtypeStruct((1, pair_width), jnp.float32),
        ],
        in_specs=[hbm] * 8,
        out_specs=[vmem] * 2,
        scratch_shapes=[
            pltpu.VMEM((rows, res_total, chan), jnp.bfloat16),
            pltpu.VMEM((1, chan), jnp.float32),
            pltpu.VMEM((1, chan), jnp.float32),
            pltpu.VMEM((hidden, chan), jnp.bfloat16),
            pltpu.VMEM((1, hidden), jnp.float32),
            pltpu.VMEM((hidden, chan), jnp.bfloat16),
            pltpu.VMEM((1, hidden), jnp.float32),
            pltpu.VMEM((rows * res_total, LANES), jnp.float32),
            pltpu.VMEM((half_count * rest_count, rows, row_block * hidden), jnp.float32),
            pltpu.SemaphoreType.DMA((8,)),
        ],
        compiler_params=params,
    )(
        in_hbm(alignment),
        in_hbm(layer_norm_gain.reshape(1, chan)),
        in_hbm(layer_norm_bias.reshape(1, chan)),
        in_hbm(left_projection_weight.T),
        in_hbm(left_bias.reshape(1, hidden)),
        in_hbm(right_projection_weight.T),
        in_hbm(right_bias.reshape(1, hidden)),
        in_hbm(out_bias.reshape(1, pair_width)),
    )
    groups = [
        [(b * half_count + h) * rest_count + a for b, a in peer_order(seq_count, rest_count)]
        for h in range(half_count)
    ]
    recv = lax.all_to_all(
        send,
        ("seq", "half", "rest"),
        split_axis=0,
        concat_axis=0,
        tiled=True,
        axis_index_groups=groups,
    )
    outer_values = pairs * hidden * hidden

    def pair_block(own, dtype):
        return pl.pallas_call(
            functools.partial(pair_kernel, own, hidden, row_block, col_block),
            out_shape=jax.ShapeDtypeStruct((pairs, pair_width), dtype),
            in_specs=[vmem] * 2,
            out_specs=vmem,
            scratch_shapes=[
                pltpu.VMEM((recv.shape[0] // LANES, row_block * hidden, LANES), jnp.float32)
            ],
            compiler_params=params,
            cost_estimate=pl.CostEstimate(
                flops=2 * outer_values * (recv.shape[0] + pair_width),
                bytes_accessed=2 * (recv.size + out_weight.size),
                transcendentals=0,
            ),
        )(recv, out_weight)

    theirs = pair_block(False, jnp.bfloat16)
    came = lax.ppermute(theirs, "half", [(0, 1), (1, 0)])
    mine = pair_block(True, jnp.float32)
    return pl.pallas_call(
        add_kernel,
        out_shape=jax.ShapeDtypeStruct((row_block, col_block, pair_width), jnp.bfloat16),
        in_specs=[vmem] * 3,
        out_specs=vmem,
        scratch_shapes=[pltpu.VMEM((pairs, pair_width), jnp.float32)],
        compiler_params=params,
    )(mine, came, bias_row)


def solution(mesh):
    seq_count, res_count = mesh.devices.shape
    split = Mesh(mesh.devices.reshape(seq_count, 2, res_count // 2), ("seq", "half", "rest"))
    in_specs = (P(("seq", "half", "rest"), None, None), P(), P(), P(), P(), P(), P(), P(), P())
    out_specs = P(("half", "rest"), "seq", None)
    return jax.shard_map(body, mesh=split, in_specs=in_specs, out_specs=out_specs, check_vma=False)
```

```python
import functools

import jax
import jax.numpy as jnp
from jax import lax
from jax.experimental import pallas as pl
from jax.experimental.pallas import tpu as pltpu
from jax.sharding import Mesh
from jax.sharding import PartitionSpec as P

LANES = 128


def peer_order(seq_count, rest_count):
    peers = [(b, a) for b in range(seq_count) for a in range(rest_count)]
    return peers[-1:] + peers[:-1]


def partner(at, rest_count):
    return at ^ 1 if rest_count % 2 == 0 else at


def project_kernel(
    seq_count,
    half_count,
    rest_count,
    align_hbm,
    gain_hbm,
    offset_hbm,
    left_w_hbm,
    left_b_hbm,
    right_w_hbm,
    right_b_hbm,
    out_b_hbm,
    send_ref,
    out_b_ref,
    align_ref,
    gain_ref,
    offset_ref,
    left_w_ref,
    left_b_ref,
    right_w_ref,
    right_b_ref,
    proj_ref,
    left_ref,
    sems,
):
    step = max(1, align_ref.shape[0] // 4)
    cuts = [pl.ds(at, step) for at in range(0, align_ref.shape[0], step)]
    copies = [
        pltpu.make_async_copy(source, target, sems.at[n])
        for n, (source, target) in enumerate(
            [(align_hbm.at[cut], align_ref.at[cut]) for cut in cuts]
            + [
                (gain_hbm, gain_ref),
                (offset_hbm, offset_ref),
                (left_w_hbm, left_w_ref),
                (left_b_hbm, left_b_ref),
                (right_w_hbm, right_w_ref),
                (right_b_hbm, right_b_ref),
                (out_b_hbm, out_b_ref),
            ]
        )
    ]
    for n, copy in enumerate(copies):
        copy.start(priority=n % 2)
    for copy in copies:
        copy.wait()
    rows, res_total, chan = align_ref.shape
    hidden = left_w_ref.shape[0]
    values = align_ref[...].astype(jnp.float32).reshape(rows * res_total, chan)
    centred = values - jnp.mean(values, axis=-1, keepdims=True)
    spread = jnp.mean(centred * centred, axis=-1, keepdims=True)
    normed = centred * lax.rsqrt(spread + 1e-05) * gain_ref[...] + offset_ref[...]
    weights = jnp.concatenate([left_w_ref[...], right_w_ref[...]], axis=0)
    biases = jnp.concatenate([left_b_ref[...], right_b_ref[...]], axis=1)
    proj_ref[:, : 2 * hidden] = (
        lax.dot_general(
            normed.astype(jnp.bfloat16),
            weights,
            (((1,), (1,)), ((), ())),
            preferred_element_type=jnp.float32,
        )
        + biases
    )
    tiles = [proj_ref[pl.ds(r, rows, stride=res_total), :][:, : 2 * hidden] for r in range(res_total)]
    row_block = res_total // (half_count * rest_count)
    col_block = res_total // seq_count
    for a in range(half_count * rest_count):
        left_ref[a] = jnp.concatenate(
            [t[:, :hidden] for t in tiles[a * row_block : (a + 1) * row_block]], axis=1
        )
    order = column_order(col_block, LANES // hidden)
    right = [
        jnp.concatenate([tiles[b * col_block + j][:, hidden:] for j in order], axis=1)
        for b in range(seq_count)
    ]
    half = lax.axis_index("half")
    own = [left_ref[half * rest_count + a] for a in range(rest_count)]
    other = [left_ref[(1 - half) * rest_count + partner(a, rest_count)] for a in range(rest_count)]
    pieces = [
        jnp.concatenate([own[a], other[a], right[b]], axis=1)
        for b, a in peer_order(seq_count, rest_count)
    ]
    group = max(1, 16 // rows)
    for start in range(0, len(pieces), group):
        block = jnp.concatenate(pieces[start : start + group], axis=0)
        send_ref[pl.ds(start * rows, group * rows), :] = block.astype(jnp.bfloat16)


def pair_kernel(own, hidden, row_block, col_block, recv_ref, weight_ref, out_ref, left_ref):
    seqs = recv_ref.shape[0]
    split = row_block * hidden
    left = recv_ref[:, :split] if own else recv_ref[:, split : 2 * split]
    right = recv_ref[:, 2 * split :]
    turned = left.astype(jnp.float32).T
    parts = left_ref.shape[0]
    for n in range(parts):
        left_ref[n] = turned[:, n * LANES : (n + 1) * LANES]
    left = jnp.concatenate(
        [
            jnp.concatenate(
                [left_ref[n, pl.ds(c, row_block, stride=hidden), :] for n in range(parts)], axis=1
            )
            for c in range(hidden)
        ],
        axis=0,
    ).astype(jnp.bfloat16)
    outer = jnp.dot(left, right, preferred_element_type=jnp.float32)
    per_group = LANES // hidden
    lane_block = lax.broadcasted_iota(jnp.int32, (2 * row_block, LANES), 1) // hidden
    rows = []
    for g in range(0, col_block // per_group, 2):
        lines = [[] for _ in range(per_group)]
        for c in range(0, hidden, per_group):
            rolled = []
            for k in range(per_group):
                at = (c + k) * row_block
                tile = jnp.concatenate(
                    [
                        outer[at : at + row_block, (g + h) * LANES : (g + h + 1) * LANES]
                        for h in range(2)
                    ],
                    axis=0,
                )
                rolled.append(roll_blocks(tile.astype(jnp.bfloat16), k, hidden))
            for j in range(per_group):
                mixed = rolled[(per_group - 1 - j) % per_group]
                for p in range(per_group - 1):
                    mixed = jnp.where(lane_block == p, rolled[(p - j) % per_group], mixed)
                lines[j].append(roll_blocks(mixed, -j, hidden))
        rows += [jnp.concatenate(line, axis=1) for line in lines]
    flat = jnp.concatenate(rows, axis=0)
    term = jnp.dot(flat, weight_ref[...], preferred_element_type=jnp.float32)
    out_ref[...] = (term * (1.0 / float(2 * seqs))).astype(out_ref.dtype)


def roll_blocks(tile, count, hidden):
    shift = count * hidden % LANES
    return pltpu.roll(tile, shift, 1) if shift else tile


def column_order(col_block, per_group):
    double = 2 * per_group
    return [
        double * (p // double) + 2 * (p % per_group) + (p // per_group) % 2 for p in range(col_block)
    ]


def add_kernel(mine_ref, came_ref, bias_ref, out_ref, term_ref):
    row_block, col_block, _ = out_ref.shape
    term_ref[...] = mine_ref[...] + came_ref[...].astype(jnp.float32) + bias_ref[...]
    for i in range(row_block):
        out_ref[i] = term_ref[pl.ds(i, col_block, stride=row_block), :].astype(jnp.bfloat16)


def in_hbm(array):
    return pltpu.with_memory_space_constraint(array, pltpu.HBM)


def body(
    alignment,
    layer_norm_gain,
    layer_norm_bias,
    left_projection_weight,
    left_bias,
    right_projection_weight,
    right_bias,
    out_weight,
    out_bias,
):
    seq_count = lax.axis_size("seq")
    half_count = lax.axis_size("half")
    rest_count = lax.axis_size("rest")
    rows, res_total, chan = alignment.shape
    hidden = left_projection_weight.shape[1]
    pair_width = out_weight.shape[1]
    row_block = res_total // (half_count * rest_count)
    col_block = res_total // seq_count
    peers = seq_count * rest_count
    width = (half_count * row_block + col_block) * hidden
    pairs = row_block * col_block
    vmem = pl.BlockSpec(memory_space=pltpu.VMEM)
    hbm = pl.BlockSpec(memory_space=pltpu.HBM)
    params = pltpu.CompilerParams(vmem_limit_bytes=32 * 1024 * 1024)
    send, bias_row = pl.pallas_call(
        functools.partial(project_kernel, seq_count, half_count, rest_count),
        out_shape=[
            jax.ShapeDtypeStruct((peers * rows, width), jnp.bfloat16),
            jax.ShapeDtypeStruct((1, pair_width), jnp.float32),
        ],
        in_specs=[hbm] * 8,
        out_specs=[vmem] * 2,
        scratch_shapes=[
            pltpu.VMEM((rows, res_total, chan), jnp.bfloat16),
            pltpu.VMEM((1, chan), jnp.float32),
            pltpu.VMEM((1, chan), jnp.float32),
            pltpu.VMEM((hidden, chan), jnp.bfloat16),
            pltpu.VMEM((1, hidden), jnp.float32),
            pltpu.VMEM((hidden, chan), jnp.bfloat16),
            pltpu.VMEM((1, hidden), jnp.float32),
            pltpu.VMEM((rows * res_total, LANES), jnp.float32),
            pltpu.VMEM((half_count * rest_count, rows, row_block * hidden), jnp.float32),
            pltpu.SemaphoreType.DMA((7 + rows // max(1, rows // 4),)),
        ],
        compiler_params=params,
    )(
        in_hbm(alignment),
        in_hbm(layer_norm_gain.reshape(1, chan)),
        in_hbm(layer_norm_bias.reshape(1, chan)),
        in_hbm(left_projection_weight.T),
        in_hbm(left_bias.reshape(1, hidden)),
        in_hbm(right_projection_weight.T),
        in_hbm(right_bias.reshape(1, hidden)),
        in_hbm(out_bias.reshape(1, pair_width)),
    )
    groups = [
        [(b * half_count + h) * rest_count + a for b, a in peer_order(seq_count, rest_count)]
        for h in range(half_count)
    ]
    recv = lax.all_to_all(
        send,
        ("seq", "half", "rest"),
        split_axis=0,
        concat_axis=0,
        tiled=True,
        axis_index_groups=groups,
    )
    outer_values = pairs * hidden * hidden

    def pair_block(own, dtype):
        return pl.pallas_call(
            functools.partial(pair_kernel, own, hidden, row_block, col_block),
            out_shape=jax.ShapeDtypeStruct((pairs, pair_width), dtype),
            in_specs=[vmem] * 2,
            out_specs=vmem,
            scratch_shapes=[
                pltpu.VMEM((recv.shape[0] // LANES, row_block * hidden, LANES), jnp.float32)
            ],
            compiler_params=params,
            cost_estimate=pl.CostEstimate(
                flops=2 * outer_values * (recv.shape[0] + pair_width),
                bytes_accessed=2 * (recv.size + out_weight.size),
                transcendentals=0,
            ),
        )(recv, out_weight)

    theirs = pair_block(False, jnp.bfloat16)
    swap = [
        (h * rest_count + q, (1 - h) * rest_count + partner(q, rest_count))
        for h in range(half_count)
        for q in range(rest_count)
    ]
    came = lax.ppermute(theirs, ("half", "rest"), swap)
    mine = pair_block(True, jnp.float32)
    return pl.pallas_call(
        add_kernel,
        out_shape=jax.ShapeDtypeStruct((row_block, col_block, pair_width), jnp.bfloat16),
        in_specs=[vmem] * 3,
        out_specs=vmem,
        scratch_shapes=[pltpu.VMEM((pairs, pair_width), jnp.float32)],
        compiler_params=params,
    )(mine, came, bias_row)


def solution(mesh):
    seq_count, res_count = mesh.devices.shape
    split = Mesh(mesh.devices.reshape(seq_count, 2, res_count // 2), ("seq", "half", "rest"))
    in_specs = (P(("seq", "half", "rest"), None, None), P(), P(), P(), P(), P(), P(), P(), P())
    out_specs = P(("half", "rest"), "seq", None)
    return jax.shard_map(body, mesh=split, in_specs=in_specs, out_specs=out_specs, check_vma=False)
```

```python
import functools

import jax
import jax.numpy as jnp
from jax import lax
from jax.experimental import pallas as pl
from jax.experimental.pallas import tpu as pltpu
from jax.sharding import Mesh
from jax.sharding import PartitionSpec as P

LANES = 128


def peer_order(seq_count, rest_count):
    peers = [(b, a) for a in range(rest_count) for b in range(seq_count)]
    return peers[-1:] + peers[:-1]


def partner(at, rest_count):
    return at ^ 1 if rest_count % 2 == 0 else at


def project_kernel(
    seq_count,
    half_count,
    rest_count,
    align_hbm,
    gain_hbm,
    offset_hbm,
    left_w_hbm,
    left_b_hbm,
    right_w_hbm,
    right_b_hbm,
    out_b_hbm,
    send_ref,
    out_b_ref,
    align_ref,
    gain_ref,
    offset_ref,
    left_w_ref,
    left_b_ref,
    right_w_ref,
    right_b_ref,
    proj_ref,
    left_ref,
    sems,
):
    copies = [
        pltpu.make_async_copy(source, target, sems.at[n])
        for n, (source, target) in enumerate(
            [
                (align_hbm, align_ref),
                (gain_hbm, gain_ref),
                (offset_hbm, offset_ref),
                (left_w_hbm, left_w_ref),
                (left_b_hbm, left_b_ref),
                (right_w_hbm, right_w_ref),
                (right_b_hbm, right_b_ref),
                (out_b_hbm, out_b_ref),
            ]
        )
    ]
    for copy in copies:
        copy.start()
    for copy in copies:
        copy.wait()
    rows, res_total, chan = align_ref.shape
    hidden = left_w_ref.shape[0]
    values = align_ref[...].astype(jnp.float32).reshape(rows * res_total, chan)
    centred = values - jnp.mean(values, axis=-1, keepdims=True)
    spread = jnp.mean(centred * centred, axis=-1, keepdims=True)
    normed = centred * lax.rsqrt(spread + 1e-05) * gain_ref[...] + offset_ref[...]
    weights = jnp.concatenate([left_w_ref[...], right_w_ref[...]], axis=0)
    biases = jnp.concatenate([left_b_ref[...], right_b_ref[...]], axis=1)
    proj_ref[:, : 2 * hidden] = (
        lax.dot_general(
            normed.astype(jnp.bfloat16),
            weights,
            (((1,), (1,)), ((), ())),
            preferred_element_type=jnp.float32,
        )
        + biases
    )
    tiles = [proj_ref[pl.ds(r, rows, stride=res_total), :][:, : 2 * hidden] for r in range(res_total)]
    row_block = res_total // (half_count * rest_count)
    col_block = res_total // seq_count
    for a in range(half_count * rest_count):
        left_ref[a] = jnp.concatenate(
            [t[:, :hidden] for t in tiles[a * row_block : (a + 1) * row_block]], axis=1
        )
    order = column_order(col_block, LANES // hidden)
    right = [
        jnp.concatenate([tiles[b * col_block + j][:, hidden:] for j in order], axis=1)
        for b in range(seq_count)
    ]
    half = lax.axis_index("half")
    own = [left_ref[half * rest_count + a] for a in range(rest_count)]
    other = [left_ref[(1 - half) * rest_count + partner(a, rest_count)] for a in range(rest_count)]
    pieces = [
        jnp.concatenate([own[a], other[a], right[b]], axis=1)
        for b, a in peer_order(seq_count, rest_count)
    ]
    group = max(1, 16 // rows)
    for start in range(0, len(pieces), group):
        block = jnp.concatenate(pieces[start : start + group], axis=0)
        send_ref[pl.ds(start * rows, group * rows), :] = block.astype(jnp.bfloat16)


def pair_kernel(own, hidden, row_block, col_block, recv_ref, weight_ref, out_ref, left_ref):
    seqs = recv_ref.shape[0]
    split = row_block * hidden
    left = recv_ref[:, :split] if own else recv_ref[:, split : 2 * split]
    right = recv_ref[:, 2 * split :]
    turned = left.T.astype(jnp.float32)
    parts = left_ref.shape[0]
    for n in range(parts):
        left_ref[n] = turned[:, n * LANES : (n + 1) * LANES]
    left = jnp.concatenate(
        [
            jnp.concatenate(
                [left_ref[n, pl.ds(c, row_block, stride=hidden), :] for n in range(parts)], axis=1
            )
            for c in range(hidden)
        ],
        axis=0,
    ).astype(jnp.bfloat16)
    outer = jnp.dot(left, right, preferred_element_type=jnp.float32)
    per_group = LANES // hidden
    lane_block = lax.broadcasted_iota(jnp.int32, (2 * row_block, LANES), 1) // hidden
    rows = []
    for g in range(0, col_block // per_group, 2):
        lines = [[] for _ in range(per_group)]
        for c in range(0, hidden, per_group):
            rolled = []
            for k in range(per_group):
                at = (c + k) * row_block
                tile = jnp.concatenate(
                    [
                        outer[at : at + row_block, (g + h) * LANES : (g + h + 1) * LANES]
                        for h in range(2)
                    ],
                    axis=0,
                )
                rolled.append(roll_blocks(tile.astype(jnp.bfloat16), k, hidden))
            for j in range(per_group):
                mixed = rolled[(per_group - 1 - j) % per_group]
                for p in range(per_group - 1):
                    mixed = jnp.where(lane_block == p, rolled[(p - j) % per_group], mixed)
                lines[j].append(roll_blocks(mixed, -j, hidden))
        rows += [jnp.concatenate(line, axis=1) for line in lines]
    flat = jnp.concatenate(rows, axis=0)
    term = jnp.dot(flat, weight_ref[...], preferred_element_type=jnp.float32)
    out_ref[...] = (term * (1.0 / float(2 * seqs))).astype(out_ref.dtype)


def roll_blocks(tile, count, hidden):
    shift = count * hidden % LANES
    return pltpu.roll(tile, shift, 1) if shift else tile


def column_order(col_block, per_group):
    double = 2 * per_group
    return [
        double * (p // double) + 2 * (p % per_group) + (p // per_group) % 2 for p in range(col_block)
    ]


def add_kernel(mine_ref, came_ref, bias_ref, out_ref, term_ref):
    row_block, col_block, _ = out_ref.shape
    term_ref[...] = mine_ref[...] + came_ref[...].astype(jnp.float32) + bias_ref[...]
    for i in range(row_block):
        out_ref[i] = term_ref[pl.ds(i, col_block, stride=row_block), :].astype(jnp.bfloat16)


def in_hbm(array):
    return pltpu.with_memory_space_constraint(array, pltpu.HBM)


def body(
    alignment,
    layer_norm_gain,
    layer_norm_bias,
    left_projection_weight,
    left_bias,
    right_projection_weight,
    right_bias,
    out_weight,
    out_bias,
):
    seq_count = lax.axis_size("seq")
    half_count = lax.axis_size("half")
    rest_count = lax.axis_size("rest")
    rows, res_total, chan = alignment.shape
    hidden = left_projection_weight.shape[1]
    pair_width = out_weight.shape[1]
    row_block = res_total // (half_count * rest_count)
    col_block = res_total // seq_count
    peers = seq_count * rest_count
    width = (half_count * row_block + col_block) * hidden
    pairs = row_block * col_block
    vmem = pl.BlockSpec(memory_space=pltpu.VMEM)
    hbm = pl.BlockSpec(memory_space=pltpu.HBM)
    params = pltpu.CompilerParams(vmem_limit_bytes=32 * 1024 * 1024)
    send, bias_row = pl.pallas_call(
        functools.partial(project_kernel, seq_count, half_count, rest_count),
        out_shape=[
            jax.ShapeDtypeStruct((peers * rows, width), jnp.bfloat16),
            jax.ShapeDtypeStruct((1, pair_width), jnp.float32),
        ],
        in_specs=[hbm] * 8,
        out_specs=[vmem] * 2,
        scratch_shapes=[
            pltpu.VMEM((rows, res_total, chan), jnp.bfloat16),
            pltpu.VMEM((1, chan), jnp.float32),
            pltpu.VMEM((1, chan), jnp.float32),
            pltpu.VMEM((hidden, chan), jnp.bfloat16),
            pltpu.VMEM((1, hidden), jnp.float32),
            pltpu.VMEM((hidden, chan), jnp.bfloat16),
            pltpu.VMEM((1, hidden), jnp.float32),
            pltpu.VMEM((rows * res_total, LANES), jnp.float32),
            pltpu.VMEM((half_count * rest_count, rows, row_block * hidden), jnp.float32),
            pltpu.SemaphoreType.DMA((8,)),
        ],
        compiler_params=params,
    )(
        in_hbm(alignment),
        in_hbm(layer_norm_gain.reshape(1, chan)),
        in_hbm(layer_norm_bias.reshape(1, chan)),
        in_hbm(left_projection_weight.T),
        in_hbm(left_bias.reshape(1, hidden)),
        in_hbm(right_projection_weight.T),
        in_hbm(right_bias.reshape(1, hidden)),
        in_hbm(out_bias.reshape(1, pair_width)),
    )
    groups = [
        [(b * half_count + h) * rest_count + a for b, a in peer_order(seq_count, rest_count)]
        for h in range(half_count)
    ]
    recv = lax.all_to_all(
        send,
        ("seq", "half", "rest"),
        split_axis=0,
        concat_axis=0,
        tiled=True,
        axis_index_groups=groups,
    )
    outer_values = pairs * hidden * hidden

    def pair_block(own, dtype):
        return pl.pallas_call(
            functools.partial(pair_kernel, own, hidden, row_block, col_block),
            out_shape=jax.ShapeDtypeStruct((pairs, pair_width), dtype),
            in_specs=[vmem] * 2,
            out_specs=vmem,
            scratch_shapes=[
                pltpu.VMEM((recv.shape[0] // LANES, row_block * hidden, LANES), jnp.float32)
            ],
            compiler_params=params,
            cost_estimate=pl.CostEstimate(
                flops=2 * outer_values * (recv.shape[0] + pair_width),
                bytes_accessed=2 * (recv.size + out_weight.size),
                transcendentals=0,
            ),
        )(recv, out_weight)

    theirs = pair_block(False, jnp.bfloat16)
    swap = [
        (h * rest_count + q, (1 - h) * rest_count + partner(q, rest_count))
        for h in range(half_count)
        for q in range(rest_count)
    ]
    came = lax.ppermute(theirs, ("half", "rest"), swap)
    mine = pair_block(True, jnp.float32)
    return pl.pallas_call(
        add_kernel,
        out_shape=jax.ShapeDtypeStruct((row_block, col_block, pair_width), jnp.bfloat16),
        in_specs=[vmem] * 3,
        out_specs=vmem,
        scratch_shapes=[pltpu.VMEM((pairs, pair_width), jnp.float32)],
        compiler_params=params,
    )(mine, came, bias_row)


def solution(mesh):
    seq_count, res_count = mesh.devices.shape
    split = Mesh(mesh.devices.reshape(seq_count, 2, res_count // 2), ("seq", "half", "rest"))
    in_specs = (P(("seq", "half", "rest"), None, None), P(), P(), P(), P(), P(), P(), P(), P())
    out_specs = P(("half", "rest"), "seq", None)
    return jax.shard_map(body, mesh=split, in_specs=in_specs, out_specs=out_specs, check_vma=False)
```

```python
import functools

import jax
import jax.numpy as jnp
from jax import lax
from jax.experimental import pallas as pl
from jax.experimental.pallas import tpu as pltpu
from jax.sharding import Mesh
from jax.sharding import PartitionSpec as P

LANES = 128


def peer_order(seq_count, rest_count):
    peers = [(b, a) for b in range(seq_count) for a in range(rest_count)]
    return peers[:-3:-1] + peers[:-2]


def partner(at, rest_count):
    return at ^ 1 if rest_count % 2 == 0 else at


def project_kernel(
    seq_count,
    half_count,
    rest_count,
    align_hbm,
    gain_hbm,
    offset_hbm,
    left_w_hbm,
    left_b_hbm,
    right_w_hbm,
    right_b_hbm,
    out_b_hbm,
    send_ref,
    out_b_ref,
    align_ref,
    gain_ref,
    offset_ref,
    left_w_ref,
    left_b_ref,
    right_w_ref,
    right_b_ref,
    proj_ref,
    left_ref,
    sems,
):
    copies = [
        pltpu.make_async_copy(source, target, sems.at[n])
        for n, (source, target) in enumerate(
            [
                (align_hbm, align_ref),
                (gain_hbm, gain_ref),
                (offset_hbm, offset_ref),
                (left_w_hbm, left_w_ref),
                (left_b_hbm, left_b_ref),
                (right_w_hbm, right_w_ref),
                (right_b_hbm, right_b_ref),
                (out_b_hbm, out_b_ref),
            ]
        )
    ]
    for copy in copies:
        copy.start()
    for copy in copies:
        copy.wait()
    rows, res_total, chan = align_ref.shape
    hidden = left_w_ref.shape[0]
    weights = jnp.concatenate([left_w_ref[...], right_w_ref[...]], axis=0)
    scaled = (weights.astype(jnp.float32) * gain_ref[...]).astype(jnp.bfloat16)
    inner = (((1,), (1,)), ((), ()))
    offset = jnp.broadcast_to(offset_ref[...], (8, chan))
    high = offset.astype(jnp.bfloat16)
    low = (offset - high.astype(jnp.float32)).astype(jnp.bfloat16)
    shift = (
        lax.dot_general(high, weights, inner, preferred_element_type=jnp.float32)
        + lax.dot_general(low, weights, inner, preferred_element_type=jnp.float32)
    )[:1] + jnp.concatenate([left_b_ref[...], right_b_ref[...]], axis=1)
    values = align_ref[...].astype(jnp.float32).reshape(rows * res_total, chan)
    centred = values - jnp.mean(values, axis=-1, keepdims=True)
    spread = jnp.mean(centred * centred, axis=-1, keepdims=True)
    product = lax.dot_general(
        centred.astype(jnp.bfloat16), scaled, inner, preferred_element_type=jnp.float32
    )
    proj_ref[:, : 2 * hidden] = product * lax.rsqrt(spread + 1e-05) + shift
    tiles = [proj_ref[pl.ds(r, rows, stride=res_total), :][:, : 2 * hidden] for r in range(res_total)]
    row_block = res_total // (half_count * rest_count)
    col_block = res_total // seq_count
    for a in range(half_count * rest_count):
        left_ref[a] = jnp.concatenate(
            [t[:, :hidden] for t in tiles[a * row_block : (a + 1) * row_block]], axis=1
        )
    order = column_order(col_block, LANES // hidden)
    right = [
        jnp.concatenate([tiles[b * col_block + j][:, hidden:] for j in order], axis=1)
        for b in range(seq_count)
    ]
    half = lax.axis_index("half")
    own = [left_ref[half * rest_count + a] for a in range(rest_count)]
    other = [left_ref[(1 - half) * rest_count + partner(a, rest_count)] for a in range(rest_count)]
    lefts = [jnp.concatenate([own[a], other[a]], axis=1) for a in range(rest_count)]
    peers = peer_order(seq_count, rest_count)
    split = lefts[0].shape[1]
    group = max(1, 16 // rows)
    packed = {}

    def pack(blocks, picks):
        if picks not in packed:
            block = jnp.concatenate([blocks[at] for _, at in picks], axis=0)
            packed[picks] = block.astype(jnp.bfloat16)
        return packed[picks]

    for start in range(0, len(peers), group):
        block = peers[start : start + group]
        place = pl.ds(start * rows, group * rows)
        send_ref[place, :split] = pack(lefts, tuple(("left", a) for _, a in block))
        send_ref[place, split:] = pack(right, tuple(("right", b) for b, _ in block))


def pair_kernel(own, hidden, row_block, col_block, recv_ref, weight_ref, out_ref, left_ref):
    seqs = recv_ref.shape[0]
    split = row_block * hidden
    left = recv_ref[:, :split] if own else recv_ref[:, split : 2 * split]
    right = recv_ref[:, 2 * split :]
    turned = left.T.astype(jnp.float32)
    parts = left_ref.shape[0]
    for n in range(parts):
        left_ref[n] = turned[:, n * LANES : (n + 1) * LANES]
    left = jnp.concatenate(
        [
            jnp.concatenate(
                [left_ref[n, pl.ds(c, row_block, stride=hidden), :] for n in range(parts)], axis=1
            )
            for c in range(hidden)
        ],
        axis=0,
    ).astype(jnp.bfloat16)
    outer = jnp.dot(left, right, preferred_element_type=jnp.float32)
    per_group = LANES // hidden
    lane_block = lax.broadcasted_iota(jnp.int32, (2 * row_block, LANES), 1) // hidden
    rows = []
    for g in range(0, col_block // per_group, 2):
        lines = [[] for _ in range(per_group)]
        for c in range(0, hidden, per_group):
            rolled = []
            for k in range(per_group):
                at = (c + k) * row_block
                tile = jnp.concatenate(
                    [
                        outer[at : at + row_block, (g + h) * LANES : (g + h + 1) * LANES]
                        for h in range(2)
                    ],
                    axis=0,
                )
                rolled.append(roll_blocks(tile.astype(jnp.bfloat16), k, hidden))
            for j in range(per_group):
                mixed = rolled[(per_group - 1 - j) % per_group]
                for p in range(per_group - 1):
                    mixed = jnp.where(lane_block == p, rolled[(p - j) % per_group], mixed)
                lines[j].append(roll_blocks(mixed, -j, hidden))
        rows += [jnp.concatenate(line, axis=1) for line in lines]
    flat = jnp.concatenate(rows, axis=0)
    term = jnp.dot(flat, weight_ref[...], preferred_element_type=jnp.float32)
    out_ref[...] = (term * (1.0 / float(2 * seqs))).astype(out_ref.dtype)


def roll_blocks(tile, count, hidden):
    shift = count * hidden % LANES
    return pltpu.roll(tile, shift, 1) if shift else tile


def column_order(col_block, per_group):
    double = 2 * per_group
    return [
        double * (p // double) + 2 * (p % per_group) + (p // per_group) % 2 for p in range(col_block)
    ]


def add_kernel(mine_ref, came_ref, bias_ref, out_ref, term_ref):
    row_block, col_block, _ = out_ref.shape
    term_ref[...] = mine_ref[...] + came_ref[...].astype(jnp.float32) + bias_ref[...]
    for i in range(row_block):
        out_ref[i] = term_ref[pl.ds(i, col_block, stride=row_block), :].astype(jnp.bfloat16)


def in_hbm(array):
    return pltpu.with_memory_space_constraint(array, pltpu.HBM)


def body(
    alignment,
    layer_norm_gain,
    layer_norm_bias,
    left_projection_weight,
    left_bias,
    right_projection_weight,
    right_bias,
    out_weight,
    out_bias,
):
    seq_count = lax.axis_size("seq")
    half_count = lax.axis_size("half")
    rest_count = lax.axis_size("rest")
    rows, res_total, chan = alignment.shape
    hidden = left_projection_weight.shape[1]
    pair_width = out_weight.shape[1]
    row_block = res_total // (half_count * rest_count)
    col_block = res_total // seq_count
    peers = seq_count * rest_count
    width = (half_count * row_block + col_block) * hidden
    pairs = row_block * col_block
    vmem = pl.BlockSpec(memory_space=pltpu.VMEM)
    hbm = pl.BlockSpec(memory_space=pltpu.HBM)
    params = pltpu.CompilerParams(vmem_limit_bytes=32 * 1024 * 1024)
    send, bias_row = pl.pallas_call(
        functools.partial(project_kernel, seq_count, half_count, rest_count),
        out_shape=[
            jax.ShapeDtypeStruct((peers * rows, width), jnp.bfloat16),
            jax.ShapeDtypeStruct((1, pair_width), jnp.float32),
        ],
        in_specs=[hbm] * 8,
        out_specs=[vmem] * 2,
        scratch_shapes=[
            pltpu.VMEM((rows, res_total, chan), jnp.bfloat16),
            pltpu.VMEM((1, chan), jnp.float32),
            pltpu.VMEM((1, chan), jnp.float32),
            pltpu.VMEM((hidden, chan), jnp.bfloat16),
            pltpu.VMEM((1, hidden), jnp.float32),
            pltpu.VMEM((hidden, chan), jnp.bfloat16),
            pltpu.VMEM((1, hidden), jnp.float32),
            pltpu.VMEM((rows * res_total, LANES), jnp.float32),
            pltpu.VMEM((half_count * rest_count, rows, row_block * hidden), jnp.float32),
            pltpu.SemaphoreType.DMA((8,)),
        ],
        compiler_params=params,
    )(
        in_hbm(alignment),
        in_hbm(layer_norm_gain.reshape(1, chan)),
        in_hbm(layer_norm_bias.reshape(1, chan)),
        in_hbm(left_projection_weight.T),
        in_hbm(left_bias.reshape(1, hidden)),
        in_hbm(right_projection_weight.T),
        in_hbm(right_bias.reshape(1, hidden)),
        in_hbm(out_bias.reshape(1, pair_width)),
    )
    groups = [
        [(b * half_count + h) * rest_count + a for b, a in peer_order(seq_count, rest_count)]
        for h in range(half_count)
    ]
    recv = lax.all_to_all(
        send,
        ("seq", "half", "rest"),
        split_axis=0,
        concat_axis=0,
        tiled=True,
        axis_index_groups=groups,
    )
    outer_values = pairs * hidden * hidden

    def pair_block(own, dtype):
        return pl.pallas_call(
            functools.partial(pair_kernel, own, hidden, row_block, col_block),
            out_shape=jax.ShapeDtypeStruct((pairs, pair_width), dtype),
            in_specs=[vmem] * 2,
            out_specs=vmem,
            scratch_shapes=[
                pltpu.VMEM((recv.shape[0] // LANES, row_block * hidden, LANES), jnp.float32)
            ],
            compiler_params=params,
            cost_estimate=pl.CostEstimate(
                flops=2 * outer_values * (recv.shape[0] + pair_width),
                bytes_accessed=2 * (recv.size + out_weight.size),
                transcendentals=0,
            ),
        )(recv, out_weight)

    theirs = pair_block(False, jnp.bfloat16)
    swap = [
        (h * rest_count + q, (1 - h) * rest_count + partner(q, rest_count))
        for h in range(half_count)
        for q in range(rest_count)
    ]
    came = lax.ppermute(theirs, ("half", "rest"), swap)
    mine = pair_block(True, jnp.float32)
    return pl.pallas_call(
        add_kernel,
        out_shape=jax.ShapeDtypeStruct((row_block, col_block, pair_width), jnp.bfloat16),
        in_specs=[vmem] * 3,
        out_specs=vmem,
        scratch_shapes=[pltpu.VMEM((pairs, pair_width), jnp.float32)],
        compiler_params=params,
    )(mine, came, bias_row)


def solution(mesh):
    seq_count, res_count = mesh.devices.shape
    split = Mesh(mesh.devices.reshape(seq_count, 2, res_count // 2), ("seq", "half", "rest"))
    in_specs = (P(("seq", "half", "rest"), None, None), P(), P(), P(), P(), P(), P(), P(), P())
    out_specs = P(("half", "rest"), "seq", None)
    return jax.shard_map(body, mesh=split, in_specs=in_specs, out_specs=out_specs, check_vma=False)
```

```python
import functools

import jax
import jax.numpy as jnp
from jax import lax
from jax.experimental import pallas as pl
from jax.experimental.pallas import tpu as pltpu
from jax.sharding import Mesh
from jax.sharding import PartitionSpec as P

LANES = 128


def peer_order(seq_count, rest_count):
    peers = [(b, a) for a in range(rest_count) for b in range(seq_count)]
    return peers[-1:] + peers[:-1]


def partner(at, rest_count):
    return at ^ 1 if rest_count % 2 == 0 else at


def project_kernel(
    seq_count,
    half_count,
    rest_count,
    align_hbm,
    gain_hbm,
    offset_hbm,
    left_w_hbm,
    left_b_hbm,
    right_w_hbm,
    right_b_hbm,
    send_ref,
    align_ref,
    gain_ref,
    offset_ref,
    left_w_ref,
    left_b_ref,
    right_w_ref,
    right_b_ref,
    proj_ref,
    left_ref,
    sems,
):
    copies = [
        pltpu.make_async_copy(source, target, sems.at[n])
        for n, (source, target) in enumerate(
            [
                (align_hbm, align_ref),
                (gain_hbm, gain_ref),
                (offset_hbm, offset_ref),
                (left_w_hbm, left_w_ref),
                (left_b_hbm, left_b_ref),
                (right_w_hbm, right_w_ref),
                (right_b_hbm, right_b_ref),
            ]
        )
    ]
    for copy in copies:
        copy.start()
    for copy in copies:
        copy.wait()
    rows, res_total, chan = align_ref.shape
    hidden = left_w_ref.shape[0]
    weights = jnp.concatenate([left_w_ref[...], right_w_ref[...]], axis=0)
    scaled = (weights.astype(jnp.float32) * gain_ref[...]).astype(jnp.bfloat16)
    inner = (((1,), (1,)), ((), ()))
    offset = jnp.broadcast_to(offset_ref[...], (8, chan))
    high = offset.astype(jnp.bfloat16)
    low = (offset - high.astype(jnp.float32)).astype(jnp.bfloat16)
    shift = (
        lax.dot_general(high, weights, inner, preferred_element_type=jnp.float32)
        + lax.dot_general(low, weights, inner, preferred_element_type=jnp.float32)
    )[:1] + jnp.concatenate([left_b_ref[...], right_b_ref[...]], axis=1)
    values = align_ref[...].astype(jnp.float32).reshape(rows * res_total, chan)
    centred = values - jnp.mean(values, axis=-1, keepdims=True)
    spread = jnp.mean(centred * centred, axis=-1, keepdims=True)
    product = lax.dot_general(
        centred.astype(jnp.bfloat16), scaled, inner, preferred_element_type=jnp.float32
    )
    proj_ref[:, : 2 * hidden] = product * lax.rsqrt(spread + 1e-05) + shift
    tiles = [proj_ref[pl.ds(r, rows, stride=res_total), :][:, : 2 * hidden] for r in range(res_total)]
    row_block = res_total // (half_count * rest_count)
    col_block = res_total // seq_count
    for a in range(half_count * rest_count):
        left_ref[a] = jnp.concatenate(
            [t[:, :hidden] for t in tiles[a * row_block : (a + 1) * row_block]], axis=1
        )
    order = column_order(col_block, LANES // hidden)
    right = [
        jnp.concatenate([tiles[b * col_block + j][:, hidden:] for j in order], axis=1)
        for b in range(seq_count)
    ]
    half = lax.axis_index("half")
    own = [left_ref[half * rest_count + a] for a in range(rest_count)]
    other = [left_ref[(1 - half) * rest_count + partner(a, rest_count)] for a in range(rest_count)]
    lefts = [jnp.concatenate([own[a], other[a]], axis=1) for a in range(rest_count)]
    peers = peer_order(seq_count, rest_count)
    split = lefts[0].shape[1]
    group = max(1, 16 // rows)
    packed = {}

    def pack(blocks, picks):
        if picks not in packed:
            block = jnp.concatenate([blocks[at] for _, at in picks], axis=0)
            packed[picks] = block.astype(jnp.bfloat16)
        return packed[picks]

    for start in range(0, len(peers), group):
        block = peers[start : start + group]
        place = pl.ds(start * rows, group * rows)
        send_ref[place, :split] = pack(lefts, tuple(("left", a) for _, a in block))
        send_ref[place, split:] = pack(right, tuple(("right", b) for b, _ in block))


def pair_terms(own, hidden, row_block, col_block, recv_ref, weight_ref, left_ref):
    seqs = recv_ref.shape[0]
    split = row_block * hidden
    left = recv_ref[:, :split] if own else recv_ref[:, split : 2 * split]
    right = recv_ref[:, 2 * split :]
    turned = left.T.astype(jnp.float32)
    parts = left_ref.shape[0]
    for n in range(parts):
        left_ref[n] = turned[:, n * LANES : (n + 1) * LANES]
    left = jnp.concatenate(
        [
            jnp.concatenate(
                [left_ref[n, pl.ds(c, row_block, stride=hidden), :] for n in range(parts)], axis=1
            )
            for c in range(hidden)
        ],
        axis=0,
    ).astype(jnp.bfloat16)
    outer = jnp.dot(left, right, preferred_element_type=jnp.float32)
    per_group = LANES // hidden
    lane_block = lax.broadcasted_iota(jnp.int32, (2 * row_block, LANES), 1) // hidden
    rows = []
    for g in range(0, col_block // per_group, 2):
        lines = [[] for _ in range(per_group)]
        for c in range(0, hidden, per_group):
            rolled = []
            for k in range(per_group):
                at = (c + k) * row_block
                tile = jnp.concatenate(
                    [
                        outer[at : at + row_block, (g + h) * LANES : (g + h + 1) * LANES]
                        for h in range(2)
                    ],
                    axis=0,
                )
                rolled.append(roll_blocks(tile.astype(jnp.bfloat16), k, hidden))
            for j in range(per_group):
                mixed = rolled[(per_group - 1 - j) % per_group]
                for p in range(per_group - 1):
                    mixed = jnp.where(lane_block == p, rolled[(p - j) % per_group], mixed)
                lines[j].append(roll_blocks(mixed, -j, hidden))
        rows += [jnp.concatenate(line, axis=1) for line in lines]
    flat = jnp.concatenate(rows, axis=0)
    term = jnp.dot(flat, weight_ref[...], preferred_element_type=jnp.float32)
    return term * (1.0 / float(2 * seqs))


def swaps_late():
    return (lax.axis_index("seq") == 0) & (lax.axis_index("rest") // 2 % 2 == 1)


def theirs_kernel(sizes, recv_ref, weight_ref, theirs_ref, early_ref, left_ref):
    @pl.when(swaps_late())
    def _():
        early_ref[...] = pair_terms(True, *sizes, recv_ref, weight_ref, left_ref)

    theirs_ref[...] = pair_terms(False, *sizes, recv_ref, weight_ref, left_ref).astype(
        theirs_ref.dtype
    )


def mine_kernel(
    sizes, recv_ref, weight_ref, early_ref, bias_hbm, mine_ref, left_ref, bias_ref, sem
):
    bias = pltpu.make_async_copy(bias_hbm, bias_ref, sem)
    bias.start()
    late = swaps_late()

    @pl.when(late)
    def _():
        mine_ref[...] = early_ref[...]

    @pl.when(jnp.logical_not(late))
    def _():
        mine_ref[...] = pair_terms(True, *sizes, recv_ref, weight_ref, left_ref)

    bias.wait()
    mine_ref[...] += bias_ref[...]


def roll_blocks(tile, count, hidden):
    shift = count * hidden % LANES
    return pltpu.roll(tile, shift, 1) if shift else tile


def column_order(col_block, per_group):
    double = 2 * per_group
    return [
        double * (p // double) + 2 * (p % per_group) + (p // per_group) % 2 for p in range(col_block)
    ]


def add_kernel(mine_ref, came_ref, out_ref, term_ref):
    row_block, col_block, _ = out_ref.shape
    term_ref[...] = mine_ref[...] + came_ref[...].astype(jnp.float32)
    for i in range(row_block):
        out_ref[i] = term_ref[pl.ds(i, col_block, stride=row_block), :].astype(jnp.bfloat16)


def in_hbm(array):
    return pltpu.with_memory_space_constraint(array, pltpu.HBM)


def body(
    alignment,
    layer_norm_gain,
    layer_norm_bias,
    left_projection_weight,
    left_bias,
    right_projection_weight,
    right_bias,
    out_weight,
    out_bias,
):
    seq_count = lax.axis_size("seq")
    half_count = lax.axis_size("half")
    rest_count = lax.axis_size("rest")
    rows, res_total, chan = alignment.shape
    hidden = left_projection_weight.shape[1]
    pair_width = out_weight.shape[1]
    row_block = res_total // (half_count * rest_count)
    col_block = res_total // seq_count
    peers = seq_count * rest_count
    width = (half_count * row_block + col_block) * hidden
    pairs = row_block * col_block
    vmem = pl.BlockSpec(memory_space=pltpu.VMEM)
    hbm = pl.BlockSpec(memory_space=pltpu.HBM)
    params = pltpu.CompilerParams(vmem_limit_bytes=32 * 1024 * 1024)
    send = pl.pallas_call(
        functools.partial(project_kernel, seq_count, half_count, rest_count),
        out_shape=jax.ShapeDtypeStruct((peers * rows, width), jnp.bfloat16),
        in_specs=[hbm] * 7,
        out_specs=vmem,
        scratch_shapes=[
            pltpu.VMEM((rows, res_total, chan), jnp.bfloat16),
            pltpu.VMEM((1, chan), jnp.float32),
            pltpu.VMEM((1, chan), jnp.float32),
            pltpu.VMEM((hidden, chan), jnp.bfloat16),
            pltpu.VMEM((1, hidden), jnp.float32),
            pltpu.VMEM((hidden, chan), jnp.bfloat16),
            pltpu.VMEM((1, hidden), jnp.float32),
            pltpu.VMEM((rows * res_total, LANES), jnp.float32),
            pltpu.VMEM((half_count * rest_count, rows, row_block * hidden), jnp.float32),
            pltpu.SemaphoreType.DMA((7,)),
        ],
        compiler_params=params,
    )(
        in_hbm(alignment),
        in_hbm(layer_norm_gain.reshape(1, chan)),
        in_hbm(layer_norm_bias.reshape(1, chan)),
        in_hbm(left_projection_weight.T),
        in_hbm(left_bias.reshape(1, hidden)),
        in_hbm(right_projection_weight.T),
        in_hbm(right_bias.reshape(1, hidden)),
    )
    groups = [
        [(b * half_count + h) * rest_count + a for b, a in peer_order(seq_count, rest_count)]
        for h in range(half_count)
    ]
    recv = lax.all_to_all(
        send,
        ("seq", "half", "rest"),
        split_axis=0,
        concat_axis=0,
        tiled=True,
        axis_index_groups=groups,
    )
    sizes = (hidden, row_block, col_block)
    outer_values = pairs * hidden * hidden
    cost = pl.CostEstimate(
        flops=2 * outer_values * (recv.shape[0] + pair_width),
        bytes_accessed=2 * (recv.size + out_weight.size),
        transcendentals=0,
    )
    turned = pltpu.VMEM((recv.shape[0] // LANES, row_block * hidden, LANES), jnp.float32)
    term = jax.ShapeDtypeStruct((pairs, pair_width), jnp.float32)
    theirs, early = pl.pallas_call(
        functools.partial(theirs_kernel, sizes),
        out_shape=[jax.ShapeDtypeStruct((pairs, pair_width), jnp.bfloat16), term],
        in_specs=[vmem] * 2,
        out_specs=[vmem] * 2,
        scratch_shapes=[turned],
        compiler_params=params,
        cost_estimate=cost,
    )(recv, out_weight)
    swap = [
        (h * rest_count + q, (1 - h) * rest_count + partner(q, rest_count))
        for h in range(half_count)
        for q in range(rest_count)
    ]
    came = lax.ppermute(theirs, ("half", "rest"), swap)
    mine = pl.pallas_call(
        functools.partial(mine_kernel, sizes),
        out_shape=term,
        in_specs=[vmem, vmem, vmem, hbm],
        out_specs=vmem,
        scratch_shapes=[
            turned,
            pltpu.VMEM((1, pair_width), jnp.float32),
            pltpu.SemaphoreType.DMA,
        ],
        compiler_params=params,
        cost_estimate=cost,
    )(recv, out_weight, early, in_hbm(out_bias.reshape(1, pair_width)))
    return pl.pallas_call(
        add_kernel,
        out_shape=jax.ShapeDtypeStruct((row_block, col_block, pair_width), jnp.bfloat16),
        in_specs=[vmem] * 2,
        out_specs=vmem,
        scratch_shapes=[pltpu.VMEM((pairs, pair_width), jnp.float32)],
        compiler_params=params,
    )(mine, came)


def solution(mesh):
    seq_count, res_count = mesh.devices.shape
    split = Mesh(mesh.devices.reshape(seq_count, 2, res_count // 2), ("seq", "half", "rest"))
    in_specs = (P(("seq", "half", "rest"), None, None), P(), P(), P(), P(), P(), P(), P(), P())
    out_specs = P(("half", "rest"), "seq", None)
    return jax.shard_map(body, mesh=split, in_specs=in_specs, out_specs=out_specs, check_vma=False)
```

```python
import functools

import jax
import jax.numpy as jnp
from jax import lax
from jax.experimental import pallas as pl
from jax.experimental.pallas import tpu as pltpu
from jax.sharding import Mesh
from jax.sharding import PartitionSpec as P

LANES = 128


def peer_order(seq_count, rest_count):
    peers = [(b, a) for a in range(rest_count) for b in range(seq_count)]
    return peers[-1:] + peers[:-1]


def partner(at, rest_count):
    return at ^ 1 if rest_count % 2 == 0 else at


def project_kernel(
    seq_count,
    half_count,
    rest_count,
    align_hbm,
    gain_hbm,
    offset_hbm,
    left_w_hbm,
    left_b_hbm,
    right_w_hbm,
    right_b_hbm,
    send_ref,
    align_ref,
    gain_ref,
    offset_ref,
    left_w_ref,
    left_b_ref,
    right_w_ref,
    right_b_ref,
    proj_ref,
    left_ref,
    sems,
):
    copies = [
        pltpu.make_async_copy(source, target, sems.at[n])
        for n, (source, target) in enumerate(
            [
                (align_hbm, align_ref),
                (gain_hbm, gain_ref),
                (offset_hbm, offset_ref),
                (left_w_hbm, left_w_ref),
                (left_b_hbm, left_b_ref),
                (right_w_hbm, right_w_ref),
                (right_b_hbm, right_b_ref),
            ]
        )
    ]
    for copy in copies:
        copy.start()
    for copy in copies:
        copy.wait()
    rows, res_total, chan = align_ref.shape
    hidden = left_w_ref.shape[0]
    copies_of = LANES // (2 * hidden)
    weights = jnp.concatenate([left_w_ref[...], right_w_ref[...]] * copies_of, axis=0)
    scaled = (weights.astype(jnp.float32) * gain_ref[...]).astype(jnp.bfloat16)
    inner = (((1,), (1,)), ((), ()))
    offset = jnp.broadcast_to(offset_ref[...], (8, chan))
    high = offset.astype(jnp.bfloat16)
    low = (offset - high.astype(jnp.float32)).astype(jnp.bfloat16)
    shift = (
        lax.dot_general(high, weights, inner, preferred_element_type=jnp.float32)
        + lax.dot_general(low, weights, inner, preferred_element_type=jnp.float32)
    )[:1] + jnp.concatenate([left_b_ref[...], right_b_ref[...]] * copies_of, axis=1)
    values = align_ref[...].astype(jnp.float32).reshape(rows * res_total, chan)
    centred = values - jnp.mean(values, axis=-1, keepdims=True)
    spread = jnp.mean(centred * centred, axis=-1, keepdims=True)
    product = lax.dot_general(
        centred.astype(jnp.bfloat16), scaled, inner, preferred_element_type=jnp.float32
    )
    proj_ref[...] = product * lax.rsqrt(spread + 1e-05) + shift
    tiles = [proj_ref[pl.ds(r, rows, stride=res_total), :] for r in range(res_total)]
    moved = {}
    lane_block = lax.broadcasted_iota(jnp.int32, (rows, LANES), 1) // hidden
    per_group = LANES // hidden

    def lined_up(side, residues):
        lines = []
        for at in range(0, len(residues), per_group):
            line = None
            for p, r in enumerate(residues[at : at + per_group]):
                if (p - side) % 2 == 0:
                    tile = tiles[r]
                else:
                    if r not in moved:
                        moved[r] = pltpu.roll(tiles[r], hidden, 1)
                    tile = moved[r]
                line = tile if line is None else jnp.where(lane_block == p, tile, line)
            lines.append(line)
        return jnp.concatenate(lines, axis=1)

    row_block = res_total // (half_count * rest_count)
    col_block = res_total // seq_count
    order = column_order(col_block, per_group)
    for a in range(half_count * rest_count):
        left_ref[a] = lined_up(0, [a * row_block + i for i in range(row_block)])
    right = [lined_up(1, [b * col_block + j for j in order]) for b in range(seq_count)]
    half = lax.axis_index("half")
    own = [left_ref[half * rest_count + a] for a in range(rest_count)]
    other = [left_ref[(1 - half) * rest_count + partner(a, rest_count)] for a in range(rest_count)]
    lefts = [jnp.concatenate([own[a], other[a]], axis=1) for a in range(rest_count)]
    peers = peer_order(seq_count, rest_count)
    split = lefts[0].shape[1]
    group = max(1, 16 // rows)
    packed = {}

    def pack(blocks, picks):
        if picks not in packed:
            block = jnp.concatenate([blocks[at] for _, at in picks], axis=0)
            packed[picks] = block.astype(jnp.bfloat16)
        return packed[picks]

    for start in range(0, len(peers), group):
        block = peers[start : start + group]
        place = pl.ds(start * rows, group * rows)
        send_ref[place, :split] = pack(lefts, tuple(("left", a) for _, a in block))
        send_ref[place, split:] = pack(right, tuple(("right", b) for b, _ in block))


def pair_terms(own, hidden, row_block, col_block, recv_ref, weight_ref, left_ref):
    seqs = recv_ref.shape[0]
    split = row_block * hidden
    left = recv_ref[:, :split] if own else recv_ref[:, split : 2 * split]
    right = recv_ref[:, 2 * split :]
    turned = left.T.astype(jnp.float32)
    parts = left_ref.shape[0]
    for n in range(parts):
        left_ref[n] = turned[:, n * LANES : (n + 1) * LANES]
    left = jnp.concatenate(
        [
            jnp.concatenate(
                [left_ref[n, pl.ds(c, row_block, stride=hidden), :] for n in range(parts)], axis=1
            )
            for c in range(hidden)
        ],
        axis=0,
    ).astype(jnp.bfloat16)
    outer = jnp.dot(left, right, preferred_element_type=jnp.float32)
    per_group = LANES // hidden
    lane_block = lax.broadcasted_iota(jnp.int32, (2 * row_block, LANES), 1) // hidden
    rows = []
    for g in range(0, col_block // per_group, 2):
        lines = [[] for _ in range(per_group)]
        for c in range(0, hidden, per_group):
            rolled = []
            for k in range(per_group):
                at = (c + k) * row_block
                tile = jnp.concatenate(
                    [
                        outer[at : at + row_block, (g + h) * LANES : (g + h + 1) * LANES]
                        for h in range(2)
                    ],
                    axis=0,
                )
                rolled.append(roll_blocks(tile.astype(jnp.bfloat16), k, hidden))
            for j in range(per_group):
                mixed = rolled[(per_group - 1 - j) % per_group]
                for p in range(per_group - 1):
                    mixed = jnp.where(lane_block == p, rolled[(p - j) % per_group], mixed)
                lines[j].append(roll_blocks(mixed, -j, hidden))
        rows += [jnp.concatenate(line, axis=1) for line in lines]
    flat = jnp.concatenate(rows, axis=0)
    term = jnp.dot(flat, weight_ref[...], preferred_element_type=jnp.float32)
    return term * (1.0 / float(2 * seqs))


def swaps_late():
    return (lax.axis_index("seq") == 0) & (lax.axis_index("rest") // 2 % 2 == 1)


def theirs_kernel(sizes, recv_ref, weight_ref, theirs_ref, early_ref, left_ref):
    @pl.when(swaps_late())
    def _():
        early_ref[...] = pair_terms(True, *sizes, recv_ref, weight_ref, left_ref)

    theirs_ref[...] = pair_terms(False, *sizes, recv_ref, weight_ref, left_ref).astype(
        theirs_ref.dtype
    )


def mine_kernel(
    sizes, recv_ref, weight_ref, early_ref, bias_hbm, mine_ref, left_ref, bias_ref, sem
):
    bias = pltpu.make_async_copy(bias_hbm, bias_ref, sem)
    bias.start()
    late = swaps_late()

    @pl.when(late)
    def _():
        mine_ref[...] = early_ref[...]

    @pl.when(jnp.logical_not(late))
    def _():
        mine_ref[...] = pair_terms(True, *sizes, recv_ref, weight_ref, left_ref)

    bias.wait()
    mine_ref[...] += bias_ref[...]


def roll_blocks(tile, count, hidden):
    shift = count * hidden % LANES
    return pltpu.roll(tile, shift, 1) if shift else tile


def column_order(col_block, per_group):
    double = 2 * per_group
    return [
        double * (p // double) + 2 * (p % per_group) + (p // per_group) % 2 for p in range(col_block)
    ]


def add_kernel(mine_ref, came_ref, out_ref, term_ref):
    row_block, col_block, _ = out_ref.shape
    term_ref[...] = mine_ref[...] + came_ref[...].astype(jnp.float32)
    for i in range(row_block):
        out_ref[i] = term_ref[pl.ds(i, col_block, stride=row_block), :].astype(jnp.bfloat16)


def in_hbm(array):
    return pltpu.with_memory_space_constraint(array, pltpu.HBM)


def body(
    alignment,
    layer_norm_gain,
    layer_norm_bias,
    left_projection_weight,
    left_bias,
    right_projection_weight,
    right_bias,
    out_weight,
    out_bias,
):
    seq_count = lax.axis_size("seq")
    half_count = lax.axis_size("half")
    rest_count = lax.axis_size("rest")
    rows, res_total, chan = alignment.shape
    hidden = left_projection_weight.shape[1]
    pair_width = out_weight.shape[1]
    row_block = res_total // (half_count * rest_count)
    col_block = res_total // seq_count
    peers = seq_count * rest_count
    width = (half_count * row_block + col_block) * hidden
    pairs = row_block * col_block
    vmem = pl.BlockSpec(memory_space=pltpu.VMEM)
    hbm = pl.BlockSpec(memory_space=pltpu.HBM)
    params = pltpu.CompilerParams(vmem_limit_bytes=32 * 1024 * 1024)
    send = pl.pallas_call(
        functools.partial(project_kernel, seq_count, half_count, rest_count),
        out_shape=jax.ShapeDtypeStruct((peers * rows, width), jnp.bfloat16),
        in_specs=[hbm] * 7,
        out_specs=vmem,
        scratch_shapes=[
            pltpu.VMEM((rows, res_total, chan), jnp.bfloat16),
            pltpu.VMEM((1, chan), jnp.float32),
            pltpu.VMEM((1, chan), jnp.float32),
            pltpu.VMEM((hidden, chan), jnp.bfloat16),
            pltpu.VMEM((1, hidden), jnp.float32),
            pltpu.VMEM((hidden, chan), jnp.bfloat16),
            pltpu.VMEM((1, hidden), jnp.float32),
            pltpu.VMEM((rows * res_total, LANES), jnp.float32),
            pltpu.VMEM((half_count * rest_count, rows, row_block * hidden), jnp.float32),
            pltpu.SemaphoreType.DMA((7,)),
        ],
        compiler_params=params,
    )(
        in_hbm(alignment),
        in_hbm(layer_norm_gain.reshape(1, chan)),
        in_hbm(layer_norm_bias.reshape(1, chan)),
        in_hbm(left_projection_weight.T),
        in_hbm(left_bias.reshape(1, hidden)),
        in_hbm(right_projection_weight.T),
        in_hbm(right_bias.reshape(1, hidden)),
    )
    groups = [
        [(b * half_count + h) * rest_count + a for b, a in peer_order(seq_count, rest_count)]
        for h in range(half_count)
    ]
    recv = lax.all_to_all(
        send,
        ("seq", "half", "rest"),
        split_axis=0,
        concat_axis=0,
        tiled=True,
        axis_index_groups=groups,
    )
    sizes = (hidden, row_block, col_block)
    outer_values = pairs * hidden * hidden
    cost = pl.CostEstimate(
        flops=2 * outer_values * (recv.shape[0] + pair_width),
        bytes_accessed=2 * (recv.size + out_weight.size),
        transcendentals=0,
    )
    turned = pltpu.VMEM((recv.shape[0] // LANES, row_block * hidden, LANES), jnp.float32)
    term = jax.ShapeDtypeStruct((pairs, pair_width), jnp.float32)
    theirs, early = pl.pallas_call(
        functools.partial(theirs_kernel, sizes),
        out_shape=[jax.ShapeDtypeStruct((pairs, pair_width), jnp.bfloat16), term],
        in_specs=[vmem] * 2,
        out_specs=[vmem] * 2,
        scratch_shapes=[turned],
        compiler_params=params,
        cost_estimate=cost,
    )(recv, out_weight)
    swap = [
        (h * rest_count + q, (1 - h) * rest_count + partner(q, rest_count))
        for h in range(half_count)
        for q in range(rest_count)
    ]
    came = lax.ppermute(theirs, ("half", "rest"), swap)
    mine = pl.pallas_call(
        functools.partial(mine_kernel, sizes),
        out_shape=term,
        in_specs=[vmem, vmem, vmem, hbm],
        out_specs=vmem,
        scratch_shapes=[
            turned,
            pltpu.VMEM((1, pair_width), jnp.float32),
            pltpu.SemaphoreType.DMA,
        ],
        compiler_params=params,
        cost_estimate=cost,
    )(recv, out_weight, early, in_hbm(out_bias.reshape(1, pair_width)))
    return pl.pallas_call(
        add_kernel,
        out_shape=jax.ShapeDtypeStruct((row_block, col_block, pair_width), jnp.bfloat16),
        in_specs=[vmem] * 2,
        out_specs=vmem,
        scratch_shapes=[pltpu.VMEM((pairs, pair_width), jnp.float32)],
        compiler_params=params,
    )(mine, came)


def solution(mesh):
    seq_count, res_count = mesh.devices.shape
    split = Mesh(mesh.devices.reshape(seq_count, 2, res_count // 2), ("seq", "half", "rest"))
    in_specs = (P(("seq", "half", "rest"), None, None), P(), P(), P(), P(), P(), P(), P(), P())
    out_specs = P(("half", "rest"), "seq", None)
    return jax.shard_map(body, mesh=split, in_specs=in_specs, out_specs=out_specs, check_vma=False)
```

```python
import functools

import jax
import jax.numpy as jnp
from jax import lax
from jax.experimental import pallas as pl
from jax.experimental.pallas import tpu as pltpu
from jax.sharding import Mesh
from jax.sharding import PartitionSpec as P

LANES = 128


def peer_order(seq_count, rest_count):
    peers = [(b, a) for a in range(rest_count) for b in range(seq_count)]
    return peers[-1:] + peers[:-1]


def partner(at, rest_count):
    return at ^ 1 if rest_count % 2 == 0 else at


def project_kernel(
    seq_count,
    half_count,
    rest_count,
    align_hbm,
    gain_hbm,
    offset_hbm,
    left_w_hbm,
    left_b_hbm,
    right_w_hbm,
    right_b_hbm,
    send_ref,
    align_ref,
    gain_ref,
    offset_ref,
    left_w_ref,
    left_b_ref,
    right_w_ref,
    right_b_ref,
    proj_ref,
    left_ref,
    sems,
):
    copies = [
        pltpu.make_async_copy(source, target, sems.at[n])
        for n, (source, target) in enumerate(
            [
                (align_hbm, align_ref),
                (gain_hbm, gain_ref),
                (offset_hbm, offset_ref),
                (left_w_hbm, left_w_ref),
                (left_b_hbm, left_b_ref),
                (right_w_hbm, right_w_ref),
                (right_b_hbm, right_b_ref),
            ]
        )
    ]
    for copy in copies:
        copy.start()
    for copy in copies:
        copy.wait()
    rows, res_total, chan = align_ref.shape
    hidden = left_w_ref.shape[0]
    copies_of = LANES // (2 * hidden)
    weights = jnp.concatenate([left_w_ref[...], right_w_ref[...]] * copies_of, axis=0)
    scaled = (weights.astype(jnp.float32) * gain_ref[...]).astype(jnp.bfloat16)
    inner = (((1,), (1,)), ((), ()))
    offset = jnp.broadcast_to(offset_ref[...], (8, chan))
    high = offset.astype(jnp.bfloat16)
    low = (offset - high.astype(jnp.float32)).astype(jnp.bfloat16)
    shift = (
        lax.dot_general(high, weights, inner, preferred_element_type=jnp.float32)
        + lax.dot_general(low, weights, inner, preferred_element_type=jnp.float32)
    )[:1] + jnp.concatenate([left_b_ref[...], right_b_ref[...]] * copies_of, axis=1)
    values = align_ref[...].astype(jnp.float32).reshape(rows * res_total, chan)
    centred = values - jnp.mean(values, axis=-1, keepdims=True)
    spread = jnp.mean(centred * centred, axis=-1, keepdims=True)
    product = lax.dot_general(
        centred.astype(jnp.bfloat16), scaled, inner, preferred_element_type=jnp.float32
    )
    proj_ref[...] = product * lax.rsqrt(spread + 1e-05) + shift
    tiles = [proj_ref[pl.ds(r, rows, stride=res_total), :] for r in range(res_total)]
    moved = {}
    lane_block = lax.broadcasted_iota(jnp.int32, (rows, LANES), 1) // hidden
    per_group = LANES // hidden

    def lined_up(side, residues):
        lines = []
        for at in range(0, len(residues), per_group):
            line = None
            for p, r in enumerate(residues[at : at + per_group]):
                if (p - side) % 2 == 0:
                    tile = tiles[r]
                else:
                    if r not in moved:
                        moved[r] = pltpu.roll(tiles[r], hidden, 1)
                    tile = moved[r]
                line = tile if line is None else jnp.where(lane_block == p, tile, line)
            lines.append(line)
        return jnp.concatenate(lines, axis=1)

    row_block = res_total // (half_count * rest_count)
    col_block = res_total // seq_count
    order = column_order(col_block, per_group)
    for a in range(half_count * rest_count):
        left_ref[a] = lined_up(0, [a * row_block + i for i in range(row_block)])
    right = [lined_up(1, [b * col_block + j for j in order]) for b in range(seq_count)]
    half = lax.axis_index("half")
    own = [left_ref[half * rest_count + a] for a in range(rest_count)]
    other = [left_ref[(1 - half) * rest_count + partner(a, rest_count)] for a in range(rest_count)]
    lefts = [jnp.concatenate([own[a], other[a]], axis=1) for a in range(rest_count)]
    peers = peer_order(seq_count, rest_count)
    split = lefts[0].shape[1]
    group = max(1, 16 // rows)
    packed = {}

    def pack(blocks, picks):
        if picks not in packed:
            block = jnp.concatenate([blocks[at] for _, at in picks], axis=0)
            packed[picks] = block.astype(jnp.bfloat16)
        return packed[picks]

    for start in range(0, len(peers), group):
        block = peers[start : start + group]
        place = pl.ds(start * rows, group * rows)
        send_ref[place, :split] = pack(lefts, tuple(("left", a) for _, a in block))
        send_ref[place, split:] = pack(right, tuple(("right", b) for b, _ in block))


def pair_terms(own, hidden, row_block, col_block, recv_ref, weight_ref, left_ref):
    seqs = recv_ref.shape[0]
    split = row_block * hidden
    left = recv_ref[:, :split] if own else recv_ref[:, split : 2 * split]
    right = recv_ref[:, 2 * split :]
    turned = left.T.astype(jnp.float32)
    parts = left_ref.shape[0]
    for n in range(parts):
        left_ref[n] = turned[:, n * LANES : (n + 1) * LANES]
    left = jnp.concatenate(
        [
            jnp.concatenate(
                [left_ref[n, pl.ds(c, row_block, stride=hidden), :] for n in range(parts)], axis=1
            )
            for c in range(hidden)
        ],
        axis=0,
    ).astype(jnp.bfloat16)
    outer = jnp.dot(left, right, preferred_element_type=jnp.float32)
    per_group = LANES // hidden
    lane_block = lax.broadcasted_iota(jnp.int32, (2 * row_block, LANES), 1) // hidden
    rows = []
    for g in range(0, col_block // per_group, 2):
        lines = [[] for _ in range(per_group)]
        for c in range(0, hidden, per_group):
            rolled = []
            for k in range(per_group):
                at = (c + k) * row_block
                tile = jnp.concatenate(
                    [
                        outer[at : at + row_block, (g + h) * LANES : (g + h + 1) * LANES]
                        for h in range(2)
                    ],
                    axis=0,
                )
                rolled.append(roll_blocks(tile.astype(jnp.bfloat16), k, hidden))
            for j in range(per_group):
                mixed = rolled[(per_group - 1 - j) % per_group]
                for p in range(per_group - 1):
                    mixed = jnp.where(lane_block == p, rolled[(p - j) % per_group], mixed)
                lines[j].append(roll_blocks(mixed, -j, hidden))
        rows += [jnp.concatenate(line, axis=1) for line in lines]
    flat = jnp.concatenate(rows, axis=0)
    term = jnp.dot(flat, weight_ref[...], preferred_element_type=jnp.float32)
    return term * (1.0 / float(2 * seqs))


def swaps_late():
    return (lax.axis_index("seq") == 0) & (lax.axis_index("rest") // 2 % 2 == 1)


def theirs_kernel(sizes, recv_ref, weight_ref, theirs_ref, early_ref, left_ref):
    @pl.when(swaps_late())
    def _():
        early_ref[...] = pair_terms(True, *sizes, recv_ref, weight_ref, left_ref)

    theirs_ref[...] = pair_terms(False, *sizes, recv_ref, weight_ref, left_ref).astype(
        theirs_ref.dtype
    )


def mine_kernel(
    sizes, recv_ref, weight_ref, early_ref, bias_hbm, mine_ref, left_ref, bias_ref, sem
):
    bias = pltpu.make_async_copy(bias_hbm, bias_ref, sem)
    bias.start()
    late = swaps_late()

    @pl.when(late)
    def _():
        mine_ref[...] = early_ref[...]

    @pl.when(jnp.logical_not(late))
    def _():
        mine_ref[...] = pair_terms(True, *sizes, recv_ref, weight_ref, left_ref)

    bias.wait()
    mine_ref[...] += bias_ref[...]


def roll_blocks(tile, count, hidden):
    shift = count * hidden % LANES
    return pltpu.roll(tile, shift, 1) if shift else tile


def column_order(col_block, per_group):
    double = 2 * per_group
    return [
        double * (p // double) + 2 * (p % per_group) + (p // per_group) % 2 for p in range(col_block)
    ]


def add_kernel(mine_ref, down_ref, up_ref, out_ref, term_ref):
    row_block, col_block, _ = out_ref.shape
    came = down_ref[...].astype(jnp.float32) + up_ref[...].astype(jnp.float32)
    term_ref[...] = mine_ref[...] + came
    for i in range(row_block):
        out_ref[i] = term_ref[pl.ds(i, col_block, stride=row_block), :].astype(jnp.bfloat16)


def in_hbm(array):
    return pltpu.with_memory_space_constraint(array, pltpu.HBM)


def body(
    alignment,
    layer_norm_gain,
    layer_norm_bias,
    left_projection_weight,
    left_bias,
    right_projection_weight,
    right_bias,
    out_weight,
    out_bias,
):
    seq_count = lax.axis_size("seq")
    half_count = lax.axis_size("half")
    rest_count = lax.axis_size("rest")
    rows, res_total, chan = alignment.shape
    hidden = left_projection_weight.shape[1]
    pair_width = out_weight.shape[1]
    row_block = res_total // (half_count * rest_count)
    col_block = res_total // seq_count
    peers = seq_count * rest_count
    width = (half_count * row_block + col_block) * hidden
    pairs = row_block * col_block
    vmem = pl.BlockSpec(memory_space=pltpu.VMEM)
    hbm = pl.BlockSpec(memory_space=pltpu.HBM)
    params = pltpu.CompilerParams(vmem_limit_bytes=32 * 1024 * 1024)
    send = pl.pallas_call(
        functools.partial(project_kernel, seq_count, half_count, rest_count),
        out_shape=jax.ShapeDtypeStruct((peers * rows, width), jnp.bfloat16),
        in_specs=[hbm] * 7,
        out_specs=vmem,
        scratch_shapes=[
            pltpu.VMEM((rows, res_total, chan), jnp.bfloat16),
            pltpu.VMEM((1, chan), jnp.float32),
            pltpu.VMEM((1, chan), jnp.float32),
            pltpu.VMEM((hidden, chan), jnp.bfloat16),
            pltpu.VMEM((1, hidden), jnp.float32),
            pltpu.VMEM((hidden, chan), jnp.bfloat16),
            pltpu.VMEM((1, hidden), jnp.float32),
            pltpu.VMEM((rows * res_total, LANES), jnp.float32),
            pltpu.VMEM((half_count * rest_count, rows, row_block * hidden), jnp.float32),
            pltpu.SemaphoreType.DMA((7,)),
        ],
        compiler_params=params,
    )(
        in_hbm(alignment),
        in_hbm(layer_norm_gain.reshape(1, chan)),
        in_hbm(layer_norm_bias.reshape(1, chan)),
        in_hbm(left_projection_weight.T),
        in_hbm(left_bias.reshape(1, hidden)),
        in_hbm(right_projection_weight.T),
        in_hbm(right_bias.reshape(1, hidden)),
    )
    groups = [
        [(b * half_count + h) * rest_count + a for b, a in peer_order(seq_count, rest_count)]
        for h in range(half_count)
    ]
    recv = lax.all_to_all(
        send,
        ("seq", "half", "rest"),
        split_axis=0,
        concat_axis=0,
        tiled=True,
        axis_index_groups=groups,
    )
    sizes = (hidden, row_block, col_block)
    outer_values = pairs * hidden * hidden
    cost = pl.CostEstimate(
        flops=2 * outer_values * (recv.shape[0] + pair_width),
        bytes_accessed=2 * (recv.size + out_weight.size),
        transcendentals=0,
    )
    turned = pltpu.VMEM((recv.shape[0] // LANES, row_block * hidden, LANES), jnp.float32)
    term = jax.ShapeDtypeStruct((pairs, pair_width), jnp.float32)
    theirs, early = pl.pallas_call(
        functools.partial(theirs_kernel, sizes),
        out_shape=[jax.ShapeDtypeStruct((pairs, pair_width), jnp.bfloat16), term],
        in_specs=[vmem] * 2,
        out_specs=[vmem] * 2,
        scratch_shapes=[turned],
        compiler_params=params,
        cost_estimate=cost,
    )(recv, out_weight)
    downward = [(rest_count + q, partner(q, rest_count)) for q in range(rest_count)]
    came_down = lax.ppermute(theirs, ("half", "rest"), downward)
    came_up = lax.ppermute(theirs, ("half", "rest"), [(low, high) for high, low in downward])
    mine = pl.pallas_call(
        functools.partial(mine_kernel, sizes),
        out_shape=term,
        in_specs=[vmem, vmem, vmem, hbm],
        out_specs=vmem,
        scratch_shapes=[
            turned,
            pltpu.VMEM((1, pair_width), jnp.float32),
            pltpu.SemaphoreType.DMA,
        ],
        compiler_params=params,
        cost_estimate=cost,
    )(recv, out_weight, early, in_hbm(out_bias.reshape(1, pair_width)))
    return pl.pallas_call(
        add_kernel,
        out_shape=jax.ShapeDtypeStruct((row_block, col_block, pair_width), jnp.bfloat16),
        in_specs=[vmem] * 3,
        out_specs=vmem,
        scratch_shapes=[pltpu.VMEM((pairs, pair_width), jnp.float32)],
        compiler_params=params,
    )(mine, came_down, came_up)


def solution(mesh):
    seq_count, res_count = mesh.devices.shape
    split = Mesh(mesh.devices.reshape(seq_count, 2, res_count // 2), ("seq", "half", "rest"))
    in_specs = (P(("seq", "half", "rest"), None, None), P(), P(), P(), P(), P(), P(), P(), P())
    out_specs = P(("half", "rest"), "seq", None)
    return jax.shard_map(body, mesh=split, in_specs=in_specs, out_specs=out_specs, check_vma=False)
```

```python
import functools

import jax
import jax.numpy as jnp
from jax import lax
from jax.experimental import pallas as pl
from jax.experimental.pallas import tpu as pltpu
from jax.sharding import Mesh
from jax.sharding import PartitionSpec as P

LANES = 128


def peer_order(seq_count, rest_count):
    peers = [(b, a) for a in range(rest_count) for b in range(seq_count)]
    return peers[-1:] + peers[:-1]


def partner(at, rest_count):
    return at ^ 1 if rest_count % 2 == 0 else at


def project_kernel(
    seq_count,
    half_count,
    rest_count,
    align_hbm,
    gain_hbm,
    offset_hbm,
    left_w_hbm,
    left_b_hbm,
    right_w_hbm,
    right_b_hbm,
    send_ref,
    align_ref,
    gain_ref,
    offset_ref,
    left_w_ref,
    left_b_ref,
    right_w_ref,
    right_b_ref,
    proj_ref,
    left_ref,
    sems,
):
    copies = [
        pltpu.make_async_copy(source, target, sems.at[n])
        for n, (source, target) in enumerate(
            [
                (align_hbm, align_ref),
                (gain_hbm, gain_ref),
                (offset_hbm, offset_ref),
                (left_w_hbm, left_w_ref),
                (left_b_hbm, left_b_ref),
                (right_w_hbm, right_w_ref),
                (right_b_hbm, right_b_ref),
            ]
        )
    ]
    for copy in copies:
        copy.start()
    for copy in copies:
        copy.wait()
    rows, res_total, chan = align_ref.shape
    hidden = left_w_ref.shape[0]
    copies_of = LANES // (2 * hidden)
    weights = jnp.concatenate([left_w_ref[...], right_w_ref[...]] * copies_of, axis=0)
    scaled = (weights.astype(jnp.float32) * gain_ref[...]).astype(jnp.bfloat16)
    inner = (((1,), (1,)), ((), ()))
    offset = jnp.broadcast_to(offset_ref[...], (8, chan))
    high = offset.astype(jnp.bfloat16)
    low = (offset - high.astype(jnp.float32)).astype(jnp.bfloat16)
    shift = (
        lax.dot_general(high, weights, inner, preferred_element_type=jnp.float32)
        + lax.dot_general(low, weights, inner, preferred_element_type=jnp.float32)
    )[:1] + jnp.concatenate([left_b_ref[...], right_b_ref[...]] * copies_of, axis=1)
    flat, factors = [], []
    for row in range(rows):
        values = align_ref[row].astype(jnp.float32)
        centred = values - jnp.mean(values, axis=-1, keepdims=True)
        spread = jnp.mean(centred * centred, axis=-1, keepdims=True)
        flat.append(centred.astype(jnp.bfloat16))
        factors.append(lax.rsqrt(spread + 1e-05))
    product = lax.dot_general(
        jnp.concatenate(flat, axis=0), scaled, inner, preferred_element_type=jnp.float32
    )
    for row, factor in enumerate(factors):
        place = slice(row * res_total, (row + 1) * res_total)
        proj_ref[place, :] = product[place] * factor + shift
    tiles = [proj_ref[pl.ds(r, rows, stride=res_total), :] for r in range(res_total)]
    moved = {}
    lane_block = lax.broadcasted_iota(jnp.int32, (rows, LANES), 1) // hidden
    per_group = LANES // hidden

    def lined_up(side, residues):
        lines = []
        for at in range(0, len(residues), per_group):
            line = None
            for p, r in enumerate(residues[at : at + per_group]):
                if (p - side) % 2 == 0:
                    tile = tiles[r]
                else:
                    if r not in moved:
                        moved[r] = pltpu.roll(tiles[r], hidden, 1)
                    tile = moved[r]
                line = tile if line is None else jnp.where(lane_block == p, tile, line)
            lines.append(line)
        return jnp.concatenate(lines, axis=1)

    row_block = res_total // (half_count * rest_count)
    col_block = res_total // seq_count
    order = column_order(col_block, per_group)
    for a in range(half_count * rest_count):
        left_ref[a] = lined_up(0, [a * row_block + i for i in range(row_block)])
    right = [lined_up(1, [b * col_block + j for j in order]) for b in range(seq_count)]
    half = lax.axis_index("half")
    own = [left_ref[half * rest_count + a] for a in range(rest_count)]
    other = [left_ref[(1 - half) * rest_count + partner(a, rest_count)] for a in range(rest_count)]
    lefts = [jnp.concatenate([own[a], other[a]], axis=1) for a in range(rest_count)]
    peers = peer_order(seq_count, rest_count)
    split = lefts[0].shape[1]
    group = max(1, 16 // rows)
    packed = {}

    def pack(blocks, picks):
        if picks not in packed:
            block = jnp.concatenate([blocks[at] for _, at in picks], axis=0)
            packed[picks] = block.astype(jnp.bfloat16)
        return packed[picks]

    for start in range(0, len(peers), group):
        block = peers[start : start + group]
        place = pl.ds(start * rows, group * rows)
        send_ref[place, :split] = pack(lefts, tuple(("left", a) for _, a in block))
        send_ref[place, split:] = pack(right, tuple(("right", b) for b, _ in block))


def pair_terms(own, hidden, row_block, col_block, recv_ref, weight_ref, left_ref):
    seqs = recv_ref.shape[0]
    split = row_block * hidden
    left = recv_ref[:, :split] if own else recv_ref[:, split : 2 * split]
    right = recv_ref[:, 2 * split :]
    turned = left.T.astype(jnp.float32)
    parts = left_ref.shape[0]
    for n in range(parts):
        left_ref[n] = turned[:, n * LANES : (n + 1) * LANES]
    left = jnp.concatenate(
        [
            jnp.concatenate(
                [left_ref[n, pl.ds(c, row_block, stride=hidden), :] for n in range(parts)], axis=1
            )
            for c in range(hidden)
        ],
        axis=0,
    ).astype(jnp.bfloat16)
    per_group = LANES // hidden
    lane_block = lax.broadcasted_iota(jnp.int32, (2 * row_block, LANES), 1) // hidden
    rows = []
    for g in range(0, col_block // per_group, 2):
        outer = jnp.dot(
            left, right[:, g * LANES : (g + 2) * LANES], preferred_element_type=jnp.float32
        )
        lines = [[] for _ in range(per_group)]
        for c in range(0, hidden, per_group):
            rolled = []
            for k in range(per_group):
                at = (c + k) * row_block
                tile = jnp.concatenate(
                    [
                        outer[at : at + row_block, h * LANES : (h + 1) * LANES]
                        for h in range(2)
                    ],
                    axis=0,
                )
                rolled.append(roll_blocks(tile.astype(jnp.bfloat16), k, hidden))
            for j in range(per_group):
                mixed = rolled[(per_group - 1 - j) % per_group]
                for p in range(per_group - 1):
                    mixed = jnp.where(lane_block == p, rolled[(p - j) % per_group], mixed)
                lines[j].append(roll_blocks(mixed, -j, hidden))
        rows += [jnp.concatenate(line, axis=1) for line in lines]
    flat = jnp.concatenate(rows, axis=0)
    term = jnp.dot(flat, weight_ref[...], preferred_element_type=jnp.float32)
    return term * (1.0 / float(2 * seqs))


def swaps_late():
    return (lax.axis_index("seq") == 0) & (lax.axis_index("rest") // 2 % 2 == 1)


def theirs_kernel(sizes, recv_ref, weight_ref, theirs_ref, early_ref, left_ref):
    @pl.when(swaps_late())
    def _():
        early_ref[...] = pair_terms(True, *sizes, recv_ref, weight_ref, left_ref)

    theirs_ref[...] = pair_terms(False, *sizes, recv_ref, weight_ref, left_ref).astype(
        theirs_ref.dtype
    )


def mine_kernel(
    sizes, recv_ref, weight_ref, early_ref, bias_hbm, mine_ref, left_ref, bias_ref, sem
):
    bias = pltpu.make_async_copy(bias_hbm, bias_ref, sem)
    bias.start()
    late = swaps_late()

    @pl.when(late)
    def _():
        mine_ref[...] = early_ref[...]

    @pl.when(jnp.logical_not(late))
    def _():
        mine_ref[...] = pair_terms(True, *sizes, recv_ref, weight_ref, left_ref)

    bias.wait()
    mine_ref[...] += bias_ref[...]


def roll_blocks(tile, count, hidden):
    shift = count * hidden % LANES
    return pltpu.roll(tile, shift, 1) if shift else tile


def column_order(col_block, per_group):
    double = 2 * per_group
    return [
        double * (p // double) + 2 * (p % per_group) + (p // per_group) % 2 for p in range(col_block)
    ]


def add_kernel(mine_ref, came_ref, out_ref, term_ref):
    row_block, col_block, _ = out_ref.shape
    term_ref[...] = mine_ref[...] + came_ref[...].astype(jnp.float32)
    for i in range(row_block):
        out_ref[i] = term_ref[pl.ds(i, col_block, stride=row_block), :].astype(jnp.bfloat16)


def in_hbm(array):
    return pltpu.with_memory_space_constraint(array, pltpu.HBM)


def body(
    alignment,
    layer_norm_gain,
    layer_norm_bias,
    left_projection_weight,
    left_bias,
    right_projection_weight,
    right_bias,
    out_weight,
    out_bias,
):
    seq_count = lax.axis_size("seq")
    half_count = lax.axis_size("half")
    rest_count = lax.axis_size("rest")
    rows, res_total, chan = alignment.shape
    hidden = left_projection_weight.shape[1]
    pair_width = out_weight.shape[1]
    row_block = res_total // (half_count * rest_count)
    col_block = res_total // seq_count
    peers = seq_count * rest_count
    width = (half_count * row_block + col_block) * hidden
    pairs = row_block * col_block
    vmem = pl.BlockSpec(memory_space=pltpu.VMEM)
    hbm = pl.BlockSpec(memory_space=pltpu.HBM)
    params = pltpu.CompilerParams(vmem_limit_bytes=32 * 1024 * 1024)
    send = pl.pallas_call(
        functools.partial(project_kernel, seq_count, half_count, rest_count),
        out_shape=jax.ShapeDtypeStruct((peers * rows, width), jnp.bfloat16),
        in_specs=[hbm] * 7,
        out_specs=vmem,
        scratch_shapes=[
            pltpu.VMEM((rows, res_total, chan), jnp.bfloat16),
            pltpu.VMEM((1, chan), jnp.float32),
            pltpu.VMEM((1, chan), jnp.float32),
            pltpu.VMEM((hidden, chan), jnp.bfloat16),
            pltpu.VMEM((1, hidden), jnp.float32),
            pltpu.VMEM((hidden, chan), jnp.bfloat16),
            pltpu.VMEM((1, hidden), jnp.float32),
            pltpu.VMEM((rows * res_total, LANES), jnp.float32),
            pltpu.VMEM((half_count * rest_count, rows, row_block * hidden), jnp.float32),
            pltpu.SemaphoreType.DMA((7,)),
        ],
        compiler_params=params,
    )(
        in_hbm(alignment),
        in_hbm(layer_norm_gain.reshape(1, chan)),
        in_hbm(layer_norm_bias.reshape(1, chan)),
        in_hbm(left_projection_weight.T),
        in_hbm(left_bias.reshape(1, hidden)),
        in_hbm(right_projection_weight.T),
        in_hbm(right_bias.reshape(1, hidden)),
    )
    groups = [
        [(b * half_count + h) * rest_count + a for b, a in peer_order(seq_count, rest_count)]
        for h in range(half_count)
    ]
    recv = lax.all_to_all(
        send,
        ("seq", "half", "rest"),
        split_axis=0,
        concat_axis=0,
        tiled=True,
        axis_index_groups=groups,
    )
    sizes = (hidden, row_block, col_block)
    outer_values = pairs * hidden * hidden
    cost = pl.CostEstimate(
        flops=2 * outer_values * (recv.shape[0] + pair_width),
        bytes_accessed=2 * (recv.size + out_weight.size),
        transcendentals=0,
    )
    turned = pltpu.VMEM((recv.shape[0] // LANES, row_block * hidden, LANES), jnp.float32)
    term = jax.ShapeDtypeStruct((pairs, pair_width), jnp.float32)
    theirs, early = pl.pallas_call(
        functools.partial(theirs_kernel, sizes),
        out_shape=[jax.ShapeDtypeStruct((pairs, pair_width), jnp.bfloat16), term],
        in_specs=[vmem] * 2,
        out_specs=[vmem] * 2,
        scratch_shapes=[turned],
        compiler_params=params,
        cost_estimate=cost,
    )(recv, out_weight)
    swap = [
        (h * rest_count + q, (1 - h) * rest_count + partner(q, rest_count))
        for h in range(half_count)
        for q in range(rest_count)
    ]
    came = lax.ppermute(theirs, ("half", "rest"), swap)
    mine = pl.pallas_call(
        functools.partial(mine_kernel, sizes),
        out_shape=term,
        in_specs=[vmem, vmem, vmem, hbm],
        out_specs=vmem,
        scratch_shapes=[
            turned,
            pltpu.VMEM((1, pair_width), jnp.float32),
            pltpu.SemaphoreType.DMA,
        ],
        compiler_params=params,
        cost_estimate=cost,
    )(recv, out_weight, early, in_hbm(out_bias.reshape(1, pair_width)))
    return pl.pallas_call(
        add_kernel,
        out_shape=jax.ShapeDtypeStruct((row_block, col_block, pair_width), jnp.bfloat16),
        in_specs=[vmem] * 2,
        out_specs=vmem,
        scratch_shapes=[pltpu.VMEM((pairs, pair_width), jnp.float32)],
        compiler_params=params,
    )(mine, came)


def solution(mesh):
    seq_count, res_count = mesh.devices.shape
    split = Mesh(mesh.devices.reshape(seq_count, 2, res_count // 2), ("seq", "half", "rest"))
    in_specs = (P(("seq", "half", "rest"), None, None), P(), P(), P(), P(), P(), P(), P(), P())
    out_specs = P(("half", "rest"), "seq", None)
    return jax.shard_map(body, mesh=split, in_specs=in_specs, out_specs=out_specs, check_vma=False)
```

```python
import functools

import jax
import jax.numpy as jnp
from jax import lax
from jax.experimental import pallas as pl
from jax.experimental.pallas import tpu as pltpu
from jax.sharding import Mesh
from jax.sharding import PartitionSpec as P

LANES = 128


def peer_order(seq_count, rest_count):
    peers = [(b, a) for a in range(rest_count) for b in range(seq_count)]
    return peers[-1:] + peers[:-1]


def partner(at, rest_count):
    return at ^ 1 if rest_count % 2 == 0 else at


def project_kernel(
    seq_count,
    half_count,
    rest_count,
    align_hbm,
    gain_hbm,
    offset_hbm,
    left_w_hbm,
    left_b_hbm,
    right_w_hbm,
    right_b_hbm,
    send_ref,
    align_ref,
    gain_ref,
    offset_ref,
    left_w_ref,
    left_b_ref,
    right_w_ref,
    right_b_ref,
    proj_ref,
    left_ref,
    sems,
):
    copies = [
        pltpu.make_async_copy(source, target, sems.at[n])
        for n, (source, target) in enumerate(
            [
                (align_hbm, align_ref),
                (gain_hbm, gain_ref),
                (offset_hbm, offset_ref),
                (left_w_hbm, left_w_ref),
                (left_b_hbm, left_b_ref),
                (right_w_hbm, right_w_ref),
                (right_b_hbm, right_b_ref),
            ]
        )
    ]
    for copy in copies:
        copy.start()
    for copy in copies[1:]:
        copy.wait()
    rows, res_total, chan = align_ref.shape
    hidden = left_w_ref.shape[0]
    copies_of = LANES // (2 * hidden)
    weights = jnp.concatenate([left_w_ref[...], right_w_ref[...]] * copies_of, axis=0)
    scaled = (weights.astype(jnp.float32) * gain_ref[...]).astype(jnp.bfloat16).T
    inner = (((1,), (1,)), ((), ()))
    offset = jnp.broadcast_to(offset_ref[...], (8, chan))
    high = offset.astype(jnp.bfloat16)
    low = (offset - high.astype(jnp.float32)).astype(jnp.bfloat16)
    shift = (
        lax.dot_general(high, weights, inner, preferred_element_type=jnp.float32)
        + lax.dot_general(low, weights, inner, preferred_element_type=jnp.float32)
    )[:1] + jnp.concatenate([left_b_ref[...], right_b_ref[...]] * copies_of, axis=1)
    copies[0].wait()
    flat, factors = [], []
    for row in range(rows):
        values = align_ref[row].astype(jnp.float32)
        centred = values - jnp.mean(values, axis=-1, keepdims=True)
        spread = jnp.mean(centred * centred, axis=-1, keepdims=True)
        flat.append(centred.astype(jnp.bfloat16))
        factors.append(lax.rsqrt(spread + 1e-05))
    product = jnp.dot(
        jnp.concatenate(flat, axis=0), scaled, preferred_element_type=jnp.float32
    )
    for row, factor in enumerate(factors):
        place = slice(row * res_total, (row + 1) * res_total)
        proj_ref[place, :] = product[place] * factor + shift
    tiles = [proj_ref[pl.ds(r, rows, stride=res_total), :] for r in range(res_total)]
    moved = {}
    lane_block = lax.broadcasted_iota(jnp.int32, (rows, LANES), 1) // hidden
    per_group = LANES // hidden

    def lined_up(side, residues):
        lines = []
        for at in range(0, len(residues), per_group):
            line = None
            for p, r in enumerate(residues[at : at + per_group]):
                if (p - side) % 2 == 0:
                    tile = tiles[r]
                else:
                    if r not in moved:
                        moved[r] = pltpu.roll(tiles[r], hidden, 1)
                    tile = moved[r]
                line = tile if line is None else jnp.where(lane_block == p, tile, line)
            lines.append(line)
        return jnp.concatenate(lines, axis=1)

    row_block = res_total // (half_count * rest_count)
    col_block = res_total // seq_count
    order = column_order(col_block, per_group)
    for a in range(half_count * rest_count):
        left_ref[a] = lined_up(0, [a * row_block + i for i in range(row_block)])
    right = [lined_up(1, [b * col_block + j for j in order]) for b in range(seq_count)]
    half = lax.axis_index("half")
    own = [left_ref[half * rest_count + a] for a in range(rest_count)]
    other = [left_ref[(1 - half) * rest_count + partner(a, rest_count)] for a in range(rest_count)]
    lefts = [jnp.concatenate([own[a], other[a]], axis=1) for a in range(rest_count)]
    peers = peer_order(seq_count, rest_count)
    split = lefts[0].shape[1]
    group = max(1, 16 // rows)
    packed = {}

    def pack(blocks, picks):
        if picks not in packed:
            block = jnp.concatenate([blocks[at] for _, at in picks], axis=0)
            packed[picks] = block.astype(jnp.bfloat16)
        return packed[picks]

    for start in range(0, len(peers), group):
        block = peers[start : start + group]
        place = pl.ds(start * rows, group * rows)
        send_ref[place, :split] = pack(lefts, tuple(("left", a) for _, a in block))
        send_ref[place, split:] = pack(right, tuple(("right", b) for b, _ in block))


def pair_terms(own, hidden, row_block, col_block, recv_ref, weight_ref, left_ref):
    seqs = recv_ref.shape[0]
    split = row_block * hidden
    left = recv_ref[:, :split] if own else recv_ref[:, split : 2 * split]
    right = recv_ref[:, 2 * split :]
    turned = left.T.astype(jnp.float32)
    parts = left_ref.shape[0]
    for n in range(parts):
        left_ref[n] = turned[:, n * LANES : (n + 1) * LANES]
    left = jnp.concatenate(
        [
            jnp.concatenate(
                [left_ref[n, pl.ds(c, row_block, stride=hidden), :] for n in range(parts)], axis=1
            )
            for c in range(hidden)
        ],
        axis=0,
    ).astype(jnp.bfloat16)
    per_group = LANES // hidden
    lane_block = lax.broadcasted_iota(jnp.int32, (2 * row_block, LANES), 1) // hidden
    rows = []
    for g in range(0, col_block // per_group, 2):
        outer = jnp.dot(
            left, right[:, g * LANES : (g + 2) * LANES], preferred_element_type=jnp.float32
        )
        lines = [[] for _ in range(per_group)]
        for c in range(0, hidden, per_group):
            rolled = []
            for k in range(per_group):
                at = (c + k) * row_block
                tile = jnp.concatenate(
                    [
                        outer[at : at + row_block, h * LANES : (h + 1) * LANES]
                        for h in range(2)
                    ],
                    axis=0,
                )
                rolled.append(roll_blocks(tile.astype(jnp.bfloat16), k, hidden))
            for j in range(per_group):
                mixed = rolled[(per_group - 1 - j) % per_group]
                for p in range(per_group - 1):
                    mixed = jnp.where(lane_block == p, rolled[(p - j) % per_group], mixed)
                lines[j].append(roll_blocks(mixed, -j, hidden))
        rows += [jnp.concatenate(line, axis=1) for line in lines]
    flat = jnp.concatenate(rows, axis=0)
    term = jnp.dot(flat, weight_ref[...], preferred_element_type=jnp.float32)
    return term * (1.0 / float(2 * seqs))


def swaps_late():
    return (lax.axis_index("seq") == 0) & (lax.axis_index("rest") // 2 % 2 == 1)


def theirs_kernel(sizes, recv_ref, weight_ref, theirs_ref, early_ref, left_ref):
    @pl.when(swaps_late())
    def _():
        early_ref[...] = pair_terms(True, *sizes, recv_ref, weight_ref, left_ref)

    theirs_ref[...] = pair_terms(False, *sizes, recv_ref, weight_ref, left_ref).astype(
        theirs_ref.dtype
    )


def mine_kernel(
    sizes, recv_ref, weight_ref, early_ref, bias_hbm, mine_ref, left_ref, bias_ref, sem
):
    bias = pltpu.make_async_copy(bias_hbm, bias_ref, sem)
    bias.start()
    late = swaps_late()

    @pl.when(late)
    def _():
        mine_ref[...] = early_ref[...]

    @pl.when(jnp.logical_not(late))
    def _():
        mine_ref[...] = pair_terms(True, *sizes, recv_ref, weight_ref, left_ref)

    bias.wait()
    mine_ref[...] += bias_ref[...]


def roll_blocks(tile, count, hidden):
    shift = count * hidden % LANES
    return pltpu.roll(tile, shift, 1) if shift else tile


def column_order(col_block, per_group):
    double = 2 * per_group
    return [
        double * (p // double) + 2 * (p % per_group) + (p // per_group) % 2 for p in range(col_block)
    ]


def add_kernel(mine_ref, came_ref, out_hbm, term_ref, out_ref, sems):
    row_block, col_block, _ = out_ref.shape
    term_ref[...] = mine_ref[...] + came_ref[...].astype(jnp.float32)
    step = max(1, row_block // 2)
    copies = []
    for n, at in enumerate(range(0, row_block, step)):
        for i in range(at, at + step):
            out_ref[i] = term_ref[pl.ds(i, col_block, stride=row_block), :].astype(jnp.bfloat16)
        part = pl.ds(at, step)
        copies.append(pltpu.make_async_copy(out_ref.at[part], out_hbm.at[part], sems.at[n]))
        copies[-1].start()
    for copy in copies:
        copy.wait()


def in_hbm(array):
    return pltpu.with_memory_space_constraint(array, pltpu.HBM)


def body(
    alignment,
    layer_norm_gain,
    layer_norm_bias,
    left_projection_weight,
    left_bias,
    right_projection_weight,
    right_bias,
    out_weight,
    out_bias,
):
    seq_count = lax.axis_size("seq")
    half_count = lax.axis_size("half")
    rest_count = lax.axis_size("rest")
    rows, res_total, chan = alignment.shape
    hidden = left_projection_weight.shape[1]
    pair_width = out_weight.shape[1]
    row_block = res_total // (half_count * rest_count)
    col_block = res_total // seq_count
    peers = seq_count * rest_count
    width = (half_count * row_block + col_block) * hidden
    pairs = row_block * col_block
    vmem = pl.BlockSpec(memory_space=pltpu.VMEM)
    hbm = pl.BlockSpec(memory_space=pltpu.HBM)
    params = pltpu.CompilerParams(vmem_limit_bytes=32 * 1024 * 1024)
    send = pl.pallas_call(
        functools.partial(project_kernel, seq_count, half_count, rest_count),
        out_shape=jax.ShapeDtypeStruct((peers * rows, width), jnp.bfloat16),
        in_specs=[hbm] * 7,
        out_specs=vmem,
        scratch_shapes=[
            pltpu.VMEM((rows, res_total, chan), jnp.bfloat16),
            pltpu.VMEM((1, chan), jnp.float32),
            pltpu.VMEM((1, chan), jnp.float32),
            pltpu.VMEM((hidden, chan), jnp.bfloat16),
            pltpu.VMEM((1, hidden), jnp.float32),
            pltpu.VMEM((hidden, chan), jnp.bfloat16),
            pltpu.VMEM((1, hidden), jnp.float32),
            pltpu.VMEM((rows * res_total, LANES), jnp.float32),
            pltpu.VMEM((half_count * rest_count, rows, row_block * hidden), jnp.float32),
            pltpu.SemaphoreType.DMA((7,)),
        ],
        compiler_params=params,
    )(
        in_hbm(alignment),
        in_hbm(layer_norm_gain.reshape(1, chan)),
        in_hbm(layer_norm_bias.reshape(1, chan)),
        in_hbm(left_projection_weight.T),
        in_hbm(left_bias.reshape(1, hidden)),
        in_hbm(right_projection_weight.T),
        in_hbm(right_bias.reshape(1, hidden)),
    )
    groups = [
        [(b * half_count + h) * rest_count + a for b, a in peer_order(seq_count, rest_count)]
        for h in range(half_count)
    ]
    recv = lax.all_to_all(
        send,
        ("seq", "half", "rest"),
        split_axis=0,
        concat_axis=0,
        tiled=True,
        axis_index_groups=groups,
    )
    sizes = (hidden, row_block, col_block)
    outer_values = pairs * hidden * hidden
    cost = pl.CostEstimate(
        flops=2 * outer_values * (recv.shape[0] + pair_width),
        bytes_accessed=2 * (recv.size + out_weight.size),
        transcendentals=0,
    )
    turned = pltpu.VMEM((recv.shape[0] // LANES, row_block * hidden, LANES), jnp.float32)
    term = jax.ShapeDtypeStruct((pairs, pair_width), jnp.float32)
    theirs, early = pl.pallas_call(
        functools.partial(theirs_kernel, sizes),
        out_shape=[jax.ShapeDtypeStruct((pairs, pair_width), jnp.bfloat16), term],
        in_specs=[vmem] * 2,
        out_specs=[vmem] * 2,
        scratch_shapes=[turned],
        compiler_params=params,
        cost_estimate=cost,
    )(recv, out_weight)
    swap = [
        (h * rest_count + q, (1 - h) * rest_count + partner(q, rest_count))
        for h in range(half_count)
        for q in range(rest_count)
    ]
    came = lax.ppermute(theirs, ("half", "rest"), swap)
    mine = pl.pallas_call(
        functools.partial(mine_kernel, sizes),
        out_shape=term,
        in_specs=[vmem, vmem, vmem, hbm],
        out_specs=vmem,
        scratch_shapes=[
            turned,
            pltpu.VMEM((1, pair_width), jnp.float32),
            pltpu.SemaphoreType.DMA,
        ],
        compiler_params=params,
        cost_estimate=cost,
    )(recv, out_weight, early, in_hbm(out_bias.reshape(1, pair_width)))
    return pl.pallas_call(
        add_kernel,
        out_shape=jax.ShapeDtypeStruct((row_block, col_block, pair_width), jnp.bfloat16),
        in_specs=[vmem] * 2,
        out_specs=hbm,
        scratch_shapes=[
            pltpu.VMEM((pairs, pair_width), jnp.float32),
            pltpu.VMEM((row_block, col_block, pair_width), jnp.bfloat16),
            pltpu.SemaphoreType.DMA((2,)),
        ],
        compiler_params=params,
    )(mine, came)


def solution(mesh):
    seq_count, res_count = mesh.devices.shape
    split = Mesh(mesh.devices.reshape(seq_count, 2, res_count // 2), ("seq", "half", "rest"))
    in_specs = (P(("seq", "half", "rest"), None, None), P(), P(), P(), P(), P(), P(), P(), P())
    out_specs = P(("half", "rest"), "seq", None)
    return jax.shard_map(body, mesh=split, in_specs=in_specs, out_specs=out_specs, check_vma=False)
```

```python
import functools

import jax
import jax.numpy as jnp
from jax import lax
from jax.experimental import pallas as pl
from jax.experimental.pallas import tpu as pltpu
from jax.sharding import Mesh
from jax.sharding import PartitionSpec as P

LANES = 128


def peer_order(seq_count, rest_count):
    peers = [(b, a) for a in range(rest_count) for b in range(seq_count)]
    return peers[-1:] + peers[:-1]


def partner(at, rest_count):
    return at ^ 1 if rest_count % 2 == 0 else at


def project_kernel(
    seq_count,
    half_count,
    rest_count,
    align_hbm,
    gain_hbm,
    offset_hbm,
    left_w_hbm,
    left_b_hbm,
    right_w_hbm,
    right_b_hbm,
    send_ref,
    align_ref,
    gain_ref,
    offset_ref,
    left_w_ref,
    left_b_ref,
    right_w_ref,
    right_b_ref,
    proj_ref,
    left_ref,
    sems,
):
    copies = [
        pltpu.make_async_copy(source, target, sems.at[n])
        for n, (source, target) in enumerate(
            [
                (left_w_hbm, left_w_ref),
                (right_w_hbm, right_w_ref),
                (gain_hbm, gain_ref),
                (offset_hbm, offset_ref),
                (align_hbm, align_ref),
                (left_b_hbm, left_b_ref),
                (right_b_hbm, right_b_ref),
            ]
        )
    ]
    for copy in copies:
        copy.start()
    for copy in copies[:4]:
        copy.wait()
    rows, res_total, chan = align_ref.shape
    hidden = left_w_ref.shape[0]
    copies_of = LANES // (2 * hidden)
    weights = jnp.concatenate([left_w_ref[...], right_w_ref[...]] * copies_of, axis=0)
    scaled = (weights.astype(jnp.float32) * gain_ref[...]).astype(jnp.bfloat16).T
    inner = (((1,), (1,)), ((), ()))
    offset = jnp.broadcast_to(offset_ref[...], (8, chan))
    high = offset.astype(jnp.bfloat16)
    low = (offset - high.astype(jnp.float32)).astype(jnp.bfloat16)
    shift = (
        lax.dot_general(high, weights, inner, preferred_element_type=jnp.float32)
        + lax.dot_general(low, weights, inner, preferred_element_type=jnp.float32)
    )[:1]
    for copy in copies[4:]:
        copy.wait()
    shift += jnp.concatenate([left_b_ref[...], right_b_ref[...]] * copies_of, axis=1)
    flat, factors = [], []
    for row in range(rows):
        values = align_ref[row].astype(jnp.float32)
        centred = values - jnp.mean(values, axis=-1, keepdims=True)
        spread = jnp.mean(centred * centred, axis=-1, keepdims=True)
        flat.append(centred.astype(jnp.bfloat16))
        factors.append(lax.rsqrt(spread + 1e-05))
    product = jnp.dot(
        jnp.concatenate(flat, axis=0), scaled, preferred_element_type=jnp.float32
    )
    for row, factor in enumerate(factors):
        place = slice(row * res_total, (row + 1) * res_total)
        proj_ref[place, :] = product[place] * factor + shift
    tiles = [proj_ref[pl.ds(r, rows, stride=res_total), :] for r in range(res_total)]
    moved = {}
    lane_block = lax.broadcasted_iota(jnp.int32, (rows, LANES), 1) // hidden
    per_group = LANES // hidden

    def lined_up(side, residues):
        lines = []
        for at in range(0, len(residues), per_group):
            line = None
            for p, r in enumerate(residues[at : at + per_group]):
                if (p - side) % 2 == 0:
                    tile = tiles[r]
                else:
                    if r not in moved:
                        moved[r] = pltpu.roll(tiles[r], hidden, 1)
                    tile = moved[r]
                line = tile if line is None else jnp.where(lane_block == p, tile, line)
            lines.append(line)
        return jnp.concatenate(lines, axis=1)

    row_block = res_total // (half_count * rest_count)
    col_block = res_total // seq_count
    order = column_order(col_block, per_group)
    for a in range(half_count * rest_count):
        left_ref[a] = lined_up(0, [a * row_block + i for i in range(row_block)])
    right = [lined_up(1, [b * col_block + j for j in order]) for b in range(seq_count)]
    half = lax.axis_index("half")
    own = [left_ref[half * rest_count + a] for a in range(rest_count)]
    other = [left_ref[(1 - half) * rest_count + partner(a, rest_count)] for a in range(rest_count)]
    lefts = [jnp.concatenate([own[a], other[a]], axis=1) for a in range(rest_count)]
    peers = peer_order(seq_count, rest_count)
    split = lefts[0].shape[1]
    group = max(1, 16 // rows)
    packed = {}

    def pack(blocks, picks):
        if picks not in packed:
            block = jnp.concatenate([blocks[at] for _, at in picks], axis=0)
            packed[picks] = block.astype(jnp.bfloat16)
        return packed[picks]

    for start in range(0, len(peers), group):
        block = peers[start : start + group]
        place = pl.ds(start * rows, group * rows)
        send_ref[place, :split] = pack(lefts, tuple(("left", a) for _, a in block))
        send_ref[place, split:] = pack(right, tuple(("right", b) for b, _ in block))


def pair_terms(own, hidden, row_block, col_block, recv_ref, weight_ref, left_ref):
    seqs = recv_ref.shape[0]
    split = row_block * hidden
    left = recv_ref[:, :split] if own else recv_ref[:, split : 2 * split]
    right = recv_ref[:, 2 * split :]
    turned = left.T.astype(jnp.float32)
    parts = left_ref.shape[0]
    for n in range(parts):
        left_ref[n] = turned[:, n * LANES : (n + 1) * LANES]
    left = jnp.concatenate(
        [
            jnp.concatenate(
                [left_ref[n, pl.ds(c, row_block, stride=hidden), :] for n in range(parts)], axis=1
            )
            for c in range(hidden)
        ],
        axis=0,
    ).astype(jnp.bfloat16)
    per_group = LANES // hidden
    lane_block = lax.broadcasted_iota(jnp.int32, (2 * row_block, LANES), 1) // hidden
    rows = []
    for g in range(0, col_block // per_group, 2):
        outer = jnp.dot(
            left, right[:, g * LANES : (g + 2) * LANES], preferred_element_type=jnp.float32
        )
        lines = [[] for _ in range(per_group)]
        for c in range(0, hidden, per_group):
            rolled = []
            for k in range(per_group):
                at = (c + k) * row_block
                tile = jnp.concatenate(
                    [
                        outer[at : at + row_block, h * LANES : (h + 1) * LANES]
                        for h in range(2)
                    ],
                    axis=0,
                )
                rolled.append(roll_blocks(tile.astype(jnp.bfloat16), k, hidden))
            for j in range(per_group):
                mixed = rolled[(per_group - 1 - j) % per_group]
                for p in range(per_group - 1):
                    mixed = jnp.where(lane_block == p, rolled[(p - j) % per_group], mixed)
                lines[j].append(roll_blocks(mixed, -j, hidden))
        rows += [jnp.concatenate(line, axis=1) for line in lines]
    flat = jnp.concatenate(rows, axis=0)
    term = jnp.dot(flat, weight_ref[...], preferred_element_type=jnp.float32)
    return term * (1.0 / float(2 * seqs))


def swaps_late():
    return (lax.axis_index("seq") == 0) & (lax.axis_index("rest") // 2 % 2 == 1)


def theirs_kernel(sizes, recv_ref, weight_ref, theirs_ref, early_ref, left_ref):
    @pl.when(swaps_late())
    def _():
        early_ref[...] = pair_terms(True, *sizes, recv_ref, weight_ref, left_ref)

    theirs_ref[...] = pair_terms(False, *sizes, recv_ref, weight_ref, left_ref).astype(
        theirs_ref.dtype
    )


def mine_kernel(
    sizes, recv_ref, weight_ref, early_ref, bias_hbm, mine_ref, left_ref, bias_ref, sem
):
    bias = pltpu.make_async_copy(bias_hbm, bias_ref, sem)
    bias.start()
    late = swaps_late()

    @pl.when(late)
    def _():
        mine_ref[...] = early_ref[...]

    @pl.when(jnp.logical_not(late))
    def _():
        mine_ref[...] = pair_terms(True, *sizes, recv_ref, weight_ref, left_ref)

    bias.wait()
    mine_ref[...] += bias_ref[...]


def roll_blocks(tile, count, hidden):
    shift = count * hidden % LANES
    return pltpu.roll(tile, shift, 1) if shift else tile


def column_order(col_block, per_group):
    double = 2 * per_group
    return [
        double * (p // double) + 2 * (p % per_group) + (p // per_group) % 2 for p in range(col_block)
    ]


def add_kernel(mine_ref, came_ref, out_ref, term_ref):
    row_block, col_block, _ = out_ref.shape
    term_ref[...] = mine_ref[...] + came_ref[...].astype(jnp.float32)
    for i in range(row_block):
        out_ref[i] = term_ref[pl.ds(i, col_block, stride=row_block), :].astype(jnp.bfloat16)


def in_hbm(array):
    return pltpu.with_memory_space_constraint(array, pltpu.HBM)


def body(
    alignment,
    layer_norm_gain,
    layer_norm_bias,
    left_projection_weight,
    left_bias,
    right_projection_weight,
    right_bias,
    out_weight,
    out_bias,
):
    seq_count = lax.axis_size("seq")
    half_count = lax.axis_size("half")
    rest_count = lax.axis_size("rest")
    rows, res_total, chan = alignment.shape
    hidden = left_projection_weight.shape[1]
    pair_width = out_weight.shape[1]
    row_block = res_total // (half_count * rest_count)
    col_block = res_total // seq_count
    peers = seq_count * rest_count
    width = (half_count * row_block + col_block) * hidden
    pairs = row_block * col_block
    vmem = pl.BlockSpec(memory_space=pltpu.VMEM)
    hbm = pl.BlockSpec(memory_space=pltpu.HBM)
    params = pltpu.CompilerParams(vmem_limit_bytes=32 * 1024 * 1024)
    send = pl.pallas_call(
        functools.partial(project_kernel, seq_count, half_count, rest_count),
        out_shape=jax.ShapeDtypeStruct((peers * rows, width), jnp.bfloat16),
        in_specs=[hbm] * 7,
        out_specs=vmem,
        scratch_shapes=[
            pltpu.VMEM((rows, res_total, chan), jnp.bfloat16),
            pltpu.VMEM((1, chan), jnp.float32),
            pltpu.VMEM((1, chan), jnp.float32),
            pltpu.VMEM((hidden, chan), jnp.bfloat16),
            pltpu.VMEM((1, hidden), jnp.float32),
            pltpu.VMEM((hidden, chan), jnp.bfloat16),
            pltpu.VMEM((1, hidden), jnp.float32),
            pltpu.VMEM((rows * res_total, LANES), jnp.float32),
            pltpu.VMEM((half_count * rest_count, rows, row_block * hidden), jnp.float32),
            pltpu.SemaphoreType.DMA((7,)),
        ],
        compiler_params=params,
    )(
        in_hbm(alignment),
        in_hbm(layer_norm_gain.reshape(1, chan)),
        in_hbm(layer_norm_bias.reshape(1, chan)),
        in_hbm(left_projection_weight.T),
        in_hbm(left_bias.reshape(1, hidden)),
        in_hbm(right_projection_weight.T),
        in_hbm(right_bias.reshape(1, hidden)),
    )
    groups = [
        [(b * half_count + h) * rest_count + a for b, a in peer_order(seq_count, rest_count)]
        for h in range(half_count)
    ]
    recv = lax.all_to_all(
        send,
        ("seq", "half", "rest"),
        split_axis=0,
        concat_axis=0,
        tiled=True,
        axis_index_groups=groups,
    )
    sizes = (hidden, row_block, col_block)
    outer_values = pairs * hidden * hidden
    cost = pl.CostEstimate(
        flops=2 * outer_values * (recv.shape[0] + pair_width),
        bytes_accessed=2 * (recv.size + out_weight.size),
        transcendentals=0,
    )
    turned = pltpu.VMEM((recv.shape[0] // LANES, row_block * hidden, LANES), jnp.float32)
    term = jax.ShapeDtypeStruct((pairs, pair_width), jnp.float32)
    theirs, early = pl.pallas_call(
        functools.partial(theirs_kernel, sizes),
        out_shape=[jax.ShapeDtypeStruct((pairs, pair_width), jnp.bfloat16), term],
        in_specs=[vmem] * 2,
        out_specs=[vmem] * 2,
        scratch_shapes=[turned],
        compiler_params=params,
        cost_estimate=cost,
    )(recv, out_weight)
    swap = [
        (h * rest_count + q, (1 - h) * rest_count + partner(q, rest_count))
        for h in range(half_count)
        for q in range(rest_count)
    ]
    came = lax.ppermute(theirs, ("half", "rest"), swap)
    mine = pl.pallas_call(
        functools.partial(mine_kernel, sizes),
        out_shape=term,
        in_specs=[vmem, vmem, vmem, hbm],
        out_specs=vmem,
        scratch_shapes=[
            turned,
            pltpu.VMEM((1, pair_width), jnp.float32),
            pltpu.SemaphoreType.DMA,
        ],
        compiler_params=params,
        cost_estimate=cost,
    )(recv, out_weight, early, in_hbm(out_bias.reshape(1, pair_width)))
    return pl.pallas_call(
        add_kernel,
        out_shape=jax.ShapeDtypeStruct((row_block, col_block, pair_width), jnp.bfloat16),
        in_specs=[vmem] * 2,
        out_specs=vmem,
        scratch_shapes=[pltpu.VMEM((pairs, pair_width), jnp.float32)],
        compiler_params=params,
    )(mine, came)


def solution(mesh):
    seq_count, res_count = mesh.devices.shape
    split = Mesh(mesh.devices.reshape(seq_count, 2, res_count // 2), ("seq", "half", "rest"))
    in_specs = (P(("seq", "half", "rest"), None, None), P(), P(), P(), P(), P(), P(), P(), P())
    out_specs = P(("half", "rest"), "seq", None)
    return jax.shard_map(body, mesh=split, in_specs=in_specs, out_specs=out_specs, check_vma=False)
```

```python
import functools

import jax
import jax.numpy as jnp
from jax import lax
from jax.experimental import pallas as pl
from jax.experimental.pallas import tpu as pltpu
from jax.sharding import Mesh
from jax.sharding import PartitionSpec as P

LANES = 128


def peer_order(seq_count, rest_count):
    chips = range(0, rest_count, 2) if rest_count % 2 == 0 else ()
    peers = [(b, a + core) for a in chips for b in range(seq_count) for core in (1, 0)]
    if not peers:
        peers = [(b, a) for a in range(rest_count) for b in range(seq_count)]
    return peers[-2:-1] + peers[:-2] + peers[-1:]


def partner(at, rest_count):
    return at ^ 1 if rest_count % 2 == 0 else at


def project_kernel(
    seq_count,
    half_count,
    rest_count,
    align_hbm,
    gain_hbm,
    offset_hbm,
    left_w_hbm,
    left_b_hbm,
    right_w_hbm,
    right_b_hbm,
    send_ref,
    align_ref,
    gain_ref,
    offset_ref,
    left_w_ref,
    left_b_ref,
    right_w_ref,
    right_b_ref,
    proj_ref,
    left_ref,
    sems,
):
    copies = [
        pltpu.make_async_copy(source, target, sems.at[n])
        for n, (source, target) in enumerate(
            [
                (align_hbm, align_ref),
                (gain_hbm, gain_ref),
                (offset_hbm, offset_ref),
                (left_w_hbm, left_w_ref),
                (left_b_hbm, left_b_ref),
                (right_w_hbm, right_w_ref),
                (right_b_hbm, right_b_ref),
            ]
        )
    ]
    for copy in copies:
        copy.start()
    for copy in copies:
        copy.wait()
    rows, res_total, chan = align_ref.shape
    hidden = left_w_ref.shape[0]
    copies_of = LANES // (2 * hidden)
    weights = jnp.concatenate([left_w_ref[...], right_w_ref[...]] * copies_of, axis=0)
    scaled = (weights.astype(jnp.float32) * gain_ref[...]).astype(jnp.bfloat16)
    inner = (((1,), (1,)), ((), ()))
    offset = jnp.broadcast_to(offset_ref[...], (8, chan))
    high = offset.astype(jnp.bfloat16)
    low = (offset - high.astype(jnp.float32)).astype(jnp.bfloat16)
    shift = (
        lax.dot_general(high, weights, inner, preferred_element_type=jnp.float32)
        + lax.dot_general(low, weights, inner, preferred_element_type=jnp.float32)
    )[:1] + jnp.concatenate([left_b_ref[...], right_b_ref[...]] * copies_of, axis=1)
    flat, factors = [], []
    for row in range(rows):
        values = align_ref[row].astype(jnp.float32)
        centred = values - jnp.mean(values, axis=-1, keepdims=True)
        spread = jnp.mean(centred * centred, axis=-1, keepdims=True)
        flat.append(centred.astype(jnp.bfloat16))
        factors.append(lax.rsqrt(spread + 1e-05))
    product = lax.dot_general(
        jnp.concatenate(flat, axis=0), scaled, inner, preferred_element_type=jnp.float32
    )
    for row, factor in enumerate(factors):
        place = slice(row * res_total, (row + 1) * res_total)
        proj_ref[place, :] = product[place] * factor + shift
    tiles = [proj_ref[pl.ds(r, rows, stride=res_total), :] for r in range(res_total)]
    moved = {}
    lane_block = lax.broadcasted_iota(jnp.int32, (rows, LANES), 1) // hidden
    per_group = LANES // hidden

    def lined_up(side, residues):
        lines = []
        for at in range(0, len(residues), per_group):
            line = None
            for p, r in enumerate(residues[at : at + per_group]):
                if (p - side) % 2 == 0:
                    tile = tiles[r]
                else:
                    if r not in moved:
                        moved[r] = pltpu.roll(tiles[r], hidden, 1)
                    tile = moved[r]
                line = tile if line is None else jnp.where(lane_block == p, tile, line)
            lines.append(line)
        return jnp.concatenate(lines, axis=1)

    row_block = res_total // (half_count * rest_count)
    col_block = res_total // seq_count
    order = column_order(col_block, per_group)
    for a in range(half_count * rest_count):
        left_ref[a] = lined_up(0, [a * row_block + i for i in range(row_block)])
    right = [lined_up(1, [b * col_block + j for j in order]) for b in range(seq_count)]
    half = lax.axis_index("half")
    own = [left_ref[half * rest_count + a] for a in range(rest_count)]
    other = [left_ref[(1 - half) * rest_count + partner(a, rest_count)] for a in range(rest_count)]
    lefts = [jnp.concatenate([own[a], other[a]], axis=1) for a in range(rest_count)]
    peers = peer_order(seq_count, rest_count)
    split = lefts[0].shape[1]
    group = max(1, 16 // rows)
    packed = {}

    def pack(blocks, picks):
        if picks not in packed:
            block = jnp.concatenate([blocks[at] for _, at in picks], axis=0)
            packed[picks] = block.astype(jnp.bfloat16)
        return packed[picks]

    for start in range(0, len(peers), group):
        block = peers[start : start + group]
        place = pl.ds(start * rows, group * rows)
        send_ref[place, :split] = pack(lefts, tuple(("left", a) for _, a in block))
        send_ref[place, split:] = pack(right, tuple(("right", b) for b, _ in block))


def pair_terms(own, hidden, row_block, col_block, recv_ref, weight_ref, left_ref):
    seqs = recv_ref.shape[0]
    split = row_block * hidden
    left = recv_ref[:, :split] if own else recv_ref[:, split : 2 * split]
    right = recv_ref[:, 2 * split :]
    turned = left.T.astype(jnp.float32)
    parts = left_ref.shape[0]
    for n in range(parts):
        left_ref[n] = turned[:, n * LANES : (n + 1) * LANES]
    left = jnp.concatenate(
        [
            jnp.concatenate(
                [left_ref[n, pl.ds(c, row_block, stride=hidden), :] for n in range(parts)], axis=1
            )
            for c in range(hidden)
        ],
        axis=0,
    ).astype(jnp.bfloat16)
    per_group = LANES // hidden
    lane_block = lax.broadcasted_iota(jnp.int32, (2 * row_block, LANES), 1) // hidden
    rows = []
    for g in range(0, col_block // per_group, 2):
        outer = jnp.dot(
            left, right[:, g * LANES : (g + 2) * LANES], preferred_element_type=jnp.float32
        )
        lines = [[] for _ in range(per_group)]
        for c in range(0, hidden, per_group):
            rolled = []
            for k in range(per_group):
                at = (c + k) * row_block
                tile = jnp.concatenate(
                    [
                        outer[at : at + row_block, h * LANES : (h + 1) * LANES]
                        for h in range(2)
                    ],
                    axis=0,
                )
                rolled.append(roll_blocks(tile.astype(jnp.bfloat16), k, hidden))
            for j in range(per_group):
                mixed = rolled[(per_group - 1 - j) % per_group]
                for p in range(per_group - 1):
                    mixed = jnp.where(lane_block == p, rolled[(p - j) % per_group], mixed)
                lines[j].append(roll_blocks(mixed, -j, hidden))
        rows += [jnp.concatenate(line, axis=1) for line in lines]
    flat = jnp.concatenate(rows, axis=0)
    term = jnp.dot(flat, weight_ref[...], preferred_element_type=jnp.float32)
    return term * (1.0 / float(2 * seqs))


def swaps_late():
    return (lax.axis_index("seq") == 0) & (lax.axis_index("rest") // 2 % 2 == 1)


def theirs_kernel(sizes, recv_ref, weight_ref, theirs_ref, early_ref, left_ref):
    @pl.when(swaps_late())
    def _():
        early_ref[...] = pair_terms(True, *sizes, recv_ref, weight_ref, left_ref)

    theirs_ref[...] = pair_terms(False, *sizes, recv_ref, weight_ref, left_ref).astype(
        theirs_ref.dtype
    )


def mine_kernel(
    sizes, recv_ref, weight_ref, early_ref, bias_hbm, mine_ref, left_ref, bias_ref, sem
):
    bias = pltpu.make_async_copy(bias_hbm, bias_ref, sem)
    bias.start()
    late = swaps_late()

    @pl.when(late)
    def _():
        mine_ref[...] = early_ref[...]

    @pl.when(jnp.logical_not(late))
    def _():
        mine_ref[...] = pair_terms(True, *sizes, recv_ref, weight_ref, left_ref)

    bias.wait()
    mine_ref[...] += bias_ref[...]


def roll_blocks(tile, count, hidden):
    shift = count * hidden % LANES
    return pltpu.roll(tile, shift, 1) if shift else tile


def column_order(col_block, per_group):
    double = 2 * per_group
    return [
        double * (p // double) + 2 * (p % per_group) + (p // per_group) % 2 for p in range(col_block)
    ]


def add_kernel(mine_ref, came_ref, out_ref, term_ref):
    row_block, col_block, _ = out_ref.shape
    term_ref[...] = mine_ref[...] + came_ref[...].astype(jnp.float32)
    for i in range(row_block):
        out_ref[i] = term_ref[pl.ds(i, col_block, stride=row_block), :].astype(jnp.bfloat16)


def in_hbm(array):
    return pltpu.with_memory_space_constraint(array, pltpu.HBM)


def body(
    alignment,
    layer_norm_gain,
    layer_norm_bias,
    left_projection_weight,
    left_bias,
    right_projection_weight,
    right_bias,
    out_weight,
    out_bias,
):
    seq_count = lax.axis_size("seq")
    half_count = lax.axis_size("half")
    rest_count = lax.axis_size("rest")
    rows, res_total, chan = alignment.shape
    hidden = left_projection_weight.shape[1]
    pair_width = out_weight.shape[1]
    row_block = res_total // (half_count * rest_count)
    col_block = res_total // seq_count
    peers = seq_count * rest_count
    width = (half_count * row_block + col_block) * hidden
    pairs = row_block * col_block
    vmem = pl.BlockSpec(memory_space=pltpu.VMEM)
    hbm = pl.BlockSpec(memory_space=pltpu.HBM)
    params = pltpu.CompilerParams(vmem_limit_bytes=32 * 1024 * 1024)
    send = pl.pallas_call(
        functools.partial(project_kernel, seq_count, half_count, rest_count),
        out_shape=jax.ShapeDtypeStruct((peers * rows, width), jnp.bfloat16),
        in_specs=[hbm] * 7,
        out_specs=vmem,
        scratch_shapes=[
            pltpu.VMEM((rows, res_total, chan), jnp.bfloat16),
            pltpu.VMEM((1, chan), jnp.float32),
            pltpu.VMEM((1, chan), jnp.float32),
            pltpu.VMEM((hidden, chan), jnp.bfloat16),
            pltpu.VMEM((1, hidden), jnp.float32),
            pltpu.VMEM((hidden, chan), jnp.bfloat16),
            pltpu.VMEM((1, hidden), jnp.float32),
            pltpu.VMEM((rows * res_total, LANES), jnp.float32),
            pltpu.VMEM((half_count * rest_count, rows, row_block * hidden), jnp.float32),
            pltpu.SemaphoreType.DMA((7,)),
        ],
        compiler_params=params,
    )(
        in_hbm(alignment),
        in_hbm(layer_norm_gain.reshape(1, chan)),
        in_hbm(layer_norm_bias.reshape(1, chan)),
        in_hbm(left_projection_weight.T),
        in_hbm(left_bias.reshape(1, hidden)),
        in_hbm(right_projection_weight.T),
        in_hbm(right_bias.reshape(1, hidden)),
    )
    groups = [
        [(b * half_count + h) * rest_count + a for b, a in peer_order(seq_count, rest_count)]
        for h in range(half_count)
    ]
    recv = lax.all_to_all(
        send,
        ("seq", "half", "rest"),
        split_axis=0,
        concat_axis=0,
        tiled=True,
        axis_index_groups=groups,
    )
    sizes = (hidden, row_block, col_block)
    outer_values = pairs * hidden * hidden
    cost = pl.CostEstimate(
        flops=2 * outer_values * (recv.shape[0] + pair_width),
        bytes_accessed=2 * (recv.size + out_weight.size),
        transcendentals=0,
    )
    turned = pltpu.VMEM((recv.shape[0] // LANES, row_block * hidden, LANES), jnp.float32)
    term = jax.ShapeDtypeStruct((pairs, pair_width), jnp.float32)
    theirs, early = pl.pallas_call(
        functools.partial(theirs_kernel, sizes),
        out_shape=[jax.ShapeDtypeStruct((pairs, pair_width), jnp.bfloat16), term],
        in_specs=[vmem] * 2,
        out_specs=[vmem] * 2,
        scratch_shapes=[turned],
        compiler_params=params,
        cost_estimate=cost,
    )(recv, out_weight)
    swap = [
        (h * rest_count + q, (1 - h) * rest_count + partner(q, rest_count))
        for h in range(half_count)
        for q in range(rest_count)
    ]
    came = lax.ppermute(theirs, ("half", "rest"), swap)
    mine = pl.pallas_call(
        functools.partial(mine_kernel, sizes),
        out_shape=term,
        in_specs=[vmem, vmem, vmem, hbm],
        out_specs=vmem,
        scratch_shapes=[
            turned,
            pltpu.VMEM((1, pair_width), jnp.float32),
            pltpu.SemaphoreType.DMA,
        ],
        compiler_params=params,
        cost_estimate=cost,
    )(recv, out_weight, early, in_hbm(out_bias.reshape(1, pair_width)))
    return pl.pallas_call(
        add_kernel,
        out_shape=jax.ShapeDtypeStruct((row_block, col_block, pair_width), jnp.bfloat16),
        in_specs=[vmem] * 2,
        out_specs=vmem,
        scratch_shapes=[pltpu.VMEM((pairs, pair_width), jnp.float32)],
        compiler_params=params,
    )(mine, came)


def solution(mesh):
    seq_count, res_count = mesh.devices.shape
    split = Mesh(mesh.devices.reshape(seq_count, 2, res_count // 2), ("seq", "half", "rest"))
    in_specs = (P(("seq", "half", "rest"), None, None), P(), P(), P(), P(), P(), P(), P(), P())
    out_specs = P(("half", "rest"), "seq", None)
    return jax.shard_map(body, mesh=split, in_specs=in_specs, out_specs=out_specs, check_vma=False)
```

```python
import functools

import jax
import jax.numpy as jnp
from jax import lax
from jax.experimental import pallas as pl
from jax.experimental.pallas import tpu as pltpu
from jax.sharding import Mesh
from jax.sharding import PartitionSpec as P

LANES = 128


def peer_order(seq_count, rest_count):
    chips = range(0, rest_count, 2) if rest_count % 2 == 0 else ()
    peers = [(b, a + core) for a in chips for b in range(seq_count) for core in (1, 0)]
    if not peers:
        peers = [(b, a) for a in range(rest_count) for b in range(seq_count)]
    return peers[-2:-1] + peers[:-2] + peers[-1:]


def partner(at, rest_count):
    return at ^ 1 if rest_count % 2 == 0 else at


def project_kernel(
    seq_count,
    half_count,
    rest_count,
    align_hbm,
    gain_hbm,
    offset_hbm,
    left_w_hbm,
    left_b_hbm,
    right_w_hbm,
    right_b_hbm,
    send_ref,
    align_ref,
    gain_ref,
    offset_ref,
    left_w_ref,
    left_b_ref,
    right_w_ref,
    right_b_ref,
    proj_ref,
    left_ref,
    sems,
):
    copies = [
        pltpu.make_async_copy(source, target, sems.at[n])
        for n, (source, target) in enumerate(
            [
                (align_hbm, align_ref),
                (gain_hbm, gain_ref),
                (offset_hbm, offset_ref),
                (left_w_hbm, left_w_ref),
                (left_b_hbm, left_b_ref),
                (right_w_hbm, right_w_ref),
                (right_b_hbm, right_b_ref),
            ]
        )
    ]
    for copy in copies:
        copy.start()
    for copy in copies:
        copy.wait()
    rows, res_total, chan = align_ref.shape
    hidden = left_w_ref.shape[0]
    copies_of = LANES // (2 * hidden)
    weights = jnp.concatenate([left_w_ref[...], right_w_ref[...]] * copies_of, axis=0)
    scaled = (weights.astype(jnp.float32) * gain_ref[...]).astype(jnp.bfloat16)
    inner = (((1,), (1,)), ((), ()))
    offset = jnp.broadcast_to(offset_ref[...], (8, chan))
    high = offset.astype(jnp.bfloat16)
    low = (offset - high.astype(jnp.float32)).astype(jnp.bfloat16)
    shift = (
        lax.dot_general(high, weights, inner, preferred_element_type=jnp.float32)
        + lax.dot_general(low, weights, inner, preferred_element_type=jnp.float32)
    )[:1] + jnp.concatenate([left_b_ref[...], right_b_ref[...]] * copies_of, axis=1)
    flat, factors = [], []
    for row in range(rows):
        values = align_ref[row].astype(jnp.float32)
        centred = values - jnp.mean(values, axis=-1, keepdims=True)
        spread = jnp.mean(centred * centred, axis=-1, keepdims=True)
        flat.append(centred.astype(jnp.bfloat16))
        factors.append(lax.rsqrt(spread + 1e-05))
    product = lax.dot_general(
        jnp.concatenate(flat, axis=0), scaled, inner, preferred_element_type=jnp.float32
    )
    for row, factor in enumerate(factors):
        place = slice(row * res_total, (row + 1) * res_total)
        proj_ref[place, :] = product[place] * factor + shift
    tiles = [proj_ref[pl.ds(r, rows, stride=res_total), :] for r in range(res_total)]
    moved = {}
    lane_block = lax.broadcasted_iota(jnp.int32, (rows, LANES), 1) // hidden
    per_group = LANES // hidden

    def lined_up(side, residues):
        lines = []
        for at in range(0, len(residues), per_group):
            line = None
            for p, r in enumerate(residues[at : at + per_group]):
                if (p - side) % 2 == 0:
                    tile = tiles[r]
                else:
                    if r not in moved:
                        moved[r] = pltpu.roll(tiles[r], hidden, 1)
                    tile = moved[r]
                line = tile if line is None else jnp.where(lane_block == p, tile, line)
            lines.append(line)
        return jnp.concatenate(lines, axis=1)

    row_block = res_total // (half_count * rest_count)
    col_block = res_total // seq_count
    order = column_order(col_block, per_group)
    for a in range(half_count * rest_count):
        left_ref[a] = lined_up(0, [a * row_block + i for i in range(row_block)])
    right = [lined_up(1, [b * col_block + j for j in order]) for b in range(seq_count)]
    half = lax.axis_index("half")
    own = [left_ref[half * rest_count + a] for a in range(rest_count)]
    other = [left_ref[(1 - half) * rest_count + partner(a, rest_count)] for a in range(rest_count)]
    lefts = [jnp.concatenate([own[a], other[a]], axis=1) for a in range(rest_count)]
    peers = peer_order(seq_count, rest_count)
    split = lefts[0].shape[1]
    group = max(1, 16 // rows)
    packed = {}

    def pack(blocks, picks):
        if picks not in packed:
            block = jnp.concatenate([blocks[at] for _, at in picks], axis=0)
            packed[picks] = block.astype(jnp.bfloat16)
        return packed[picks]

    for start in range(0, len(peers), group):
        block = peers[start : start + group]
        place = pl.ds(start * rows, group * rows)
        send_ref[place, :split] = pack(lefts, tuple(("left", a) for _, a in block))
        send_ref[place, split:] = pack(right, tuple(("right", b) for b, _ in block))


def pair_terms(own, hidden, row_block, col_block, recv_ref, weight_ref, left_ref):
    seqs = recv_ref.shape[0]
    split = row_block * hidden
    left = recv_ref[:, :split] if own else recv_ref[:, split : 2 * split]
    right = recv_ref[:, 2 * split :]
    turned = left.T.astype(jnp.float32)
    parts = left_ref.shape[0]
    for n in range(parts):
        left_ref[n] = turned[:, n * LANES : (n + 1) * LANES]
    left = jnp.concatenate(
        [
            jnp.concatenate(
                [left_ref[n, pl.ds(c, row_block, stride=hidden), :] for n in range(parts)], axis=1
            )
            for c in range(hidden)
        ],
        axis=0,
    ).astype(jnp.bfloat16)
    per_group = LANES // hidden
    lane_block = lax.broadcasted_iota(jnp.int32, (2 * row_block, LANES), 1) // hidden
    rows = []
    for g in range(0, col_block // per_group, 2):
        outer = jnp.dot(
            left, right[:, g * LANES : (g + 2) * LANES], preferred_element_type=jnp.float32
        )
        lines = [[] for _ in range(per_group)]
        for c in range(0, hidden, per_group):
            rolled = []
            for k in range(per_group):
                at = (c + k) * row_block
                tile = jnp.concatenate(
                    [
                        outer[at : at + row_block, h * LANES : (h + 1) * LANES]
                        for h in range(2)
                    ],
                    axis=0,
                )
                rolled.append(roll_blocks(tile.astype(jnp.bfloat16), k, hidden))
            for j in range(per_group):
                mixed = rolled[(per_group - 1 - j) % per_group]
                for p in range(per_group - 1):
                    mixed = jnp.where(lane_block == p, rolled[(p - j) % per_group], mixed)
                lines[j].append(roll_blocks(mixed, -j, hidden))
        rows += [jnp.concatenate(line, axis=1) for line in lines]
    flat = jnp.concatenate(rows, axis=0)
    term = jnp.dot(flat, weight_ref[...], preferred_element_type=jnp.float32)
    return term * (1.0 / float(2 * seqs))


def swaps_late():
    return (lax.axis_index("seq") < lax.axis_size("seq") - 1) & (
        lax.axis_index("rest") // 2 % 2 == 1
    )


def theirs_kernel(sizes, recv_ref, weight_ref, theirs_ref, early_ref, left_ref):
    @pl.when(swaps_late())
    def _():
        early_ref[...] = pair_terms(True, *sizes, recv_ref, weight_ref, left_ref)

    theirs_ref[...] = pair_terms(False, *sizes, recv_ref, weight_ref, left_ref).astype(
        theirs_ref.dtype
    )


def mine_kernel(
    sizes, recv_ref, weight_ref, early_ref, bias_hbm, mine_ref, left_ref, bias_ref, sem
):
    bias = pltpu.make_async_copy(bias_hbm, bias_ref, sem)
    bias.start()
    late = swaps_late()

    @pl.when(late)
    def _():
        mine_ref[...] = early_ref[...]

    @pl.when(jnp.logical_not(late))
    def _():
        mine_ref[...] = pair_terms(True, *sizes, recv_ref, weight_ref, left_ref)

    bias.wait()
    mine_ref[...] += bias_ref[...]


def roll_blocks(tile, count, hidden):
    shift = count * hidden % LANES
    return pltpu.roll(tile, shift, 1) if shift else tile


def column_order(col_block, per_group):
    double = 2 * per_group
    return [
        double * (p // double) + 2 * (p % per_group) + (p // per_group) % 2 for p in range(col_block)
    ]


def add_kernel(mine_ref, came_ref, out_ref, term_ref):
    row_block, col_block, _ = out_ref.shape
    term_ref[...] = mine_ref[...] + came_ref[...].astype(jnp.float32)
    for i in range(row_block):
        out_ref[i] = term_ref[pl.ds(i, col_block, stride=row_block), :].astype(jnp.bfloat16)


def in_hbm(array):
    return pltpu.with_memory_space_constraint(array, pltpu.HBM)


def body(
    alignment,
    layer_norm_gain,
    layer_norm_bias,
    left_projection_weight,
    left_bias,
    right_projection_weight,
    right_bias,
    out_weight,
    out_bias,
):
    seq_count = lax.axis_size("seq")
    half_count = lax.axis_size("half")
    rest_count = lax.axis_size("rest")
    rows, res_total, chan = alignment.shape
    hidden = left_projection_weight.shape[1]
    pair_width = out_weight.shape[1]
    row_block = res_total // (half_count * rest_count)
    col_block = res_total // seq_count
    peers = seq_count * rest_count
    width = (half_count * row_block + col_block) * hidden
    pairs = row_block * col_block
    vmem = pl.BlockSpec(memory_space=pltpu.VMEM)
    hbm = pl.BlockSpec(memory_space=pltpu.HBM)
    params = pltpu.CompilerParams(vmem_limit_bytes=32 * 1024 * 1024)
    send = pl.pallas_call(
        functools.partial(project_kernel, seq_count, half_count, rest_count),
        out_shape=jax.ShapeDtypeStruct((peers * rows, width), jnp.bfloat16),
        in_specs=[hbm] * 7,
        out_specs=vmem,
        scratch_shapes=[
            pltpu.VMEM((rows, res_total, chan), jnp.bfloat16),
            pltpu.VMEM((1, chan), jnp.float32),
            pltpu.VMEM((1, chan), jnp.float32),
            pltpu.VMEM((hidden, chan), jnp.bfloat16),
            pltpu.VMEM((1, hidden), jnp.float32),
            pltpu.VMEM((hidden, chan), jnp.bfloat16),
            pltpu.VMEM((1, hidden), jnp.float32),
            pltpu.VMEM((rows * res_total, LANES), jnp.float32),
            pltpu.VMEM((half_count * rest_count, rows, row_block * hidden), jnp.float32),
            pltpu.SemaphoreType.DMA((7,)),
        ],
        compiler_params=params,
    )(
        in_hbm(alignment),
        in_hbm(layer_norm_gain.reshape(1, chan)),
        in_hbm(layer_norm_bias.reshape(1, chan)),
        in_hbm(left_projection_weight.T),
        in_hbm(left_bias.reshape(1, hidden)),
        in_hbm(right_projection_weight.T),
        in_hbm(right_bias.reshape(1, hidden)),
    )
    groups = [
        [(b * half_count + h) * rest_count + a for b, a in peer_order(seq_count, rest_count)]
        for h in range(half_count)
    ]
    recv = lax.all_to_all(
        send,
        ("seq", "half", "rest"),
        split_axis=0,
        concat_axis=0,
        tiled=True,
        axis_index_groups=groups,
    )
    sizes = (hidden, row_block, col_block)
    outer_values = pairs * hidden * hidden
    cost = pl.CostEstimate(
        flops=2 * outer_values * (recv.shape[0] + pair_width),
        bytes_accessed=2 * (recv.size + out_weight.size),
        transcendentals=0,
    )
    turned = pltpu.VMEM((recv.shape[0] // LANES, row_block * hidden, LANES), jnp.float32)
    term = jax.ShapeDtypeStruct((pairs, pair_width), jnp.float32)
    theirs, early = pl.pallas_call(
        functools.partial(theirs_kernel, sizes),
        out_shape=[jax.ShapeDtypeStruct((pairs, pair_width), jnp.bfloat16), term],
        in_specs=[vmem] * 2,
        out_specs=[vmem] * 2,
        scratch_shapes=[turned],
        compiler_params=params,
        cost_estimate=cost,
    )(recv, out_weight)
    swap = [
        (h * rest_count + q, (1 - h) * rest_count + partner(q, rest_count))
        for h in range(half_count)
        for q in range(rest_count)
    ]
    came = lax.ppermute(theirs, ("half", "rest"), swap)
    mine = pl.pallas_call(
        functools.partial(mine_kernel, sizes),
        out_shape=term,
        in_specs=[vmem, vmem, vmem, hbm],
        out_specs=vmem,
        scratch_shapes=[
            turned,
            pltpu.VMEM((1, pair_width), jnp.float32),
            pltpu.SemaphoreType.DMA,
        ],
        compiler_params=params,
        cost_estimate=cost,
    )(recv, out_weight, early, in_hbm(out_bias.reshape(1, pair_width)))
    return pl.pallas_call(
        add_kernel,
        out_shape=jax.ShapeDtypeStruct((row_block, col_block, pair_width), jnp.bfloat16),
        in_specs=[vmem] * 2,
        out_specs=vmem,
        scratch_shapes=[pltpu.VMEM((pairs, pair_width), jnp.float32)],
        compiler_params=params,
    )(mine, came)


def solution(mesh):
    seq_count, res_count = mesh.devices.shape
    split = Mesh(mesh.devices.reshape(seq_count, 2, res_count // 2), ("seq", "half", "rest"))
    in_specs = (P(("seq", "half", "rest"), None, None), P(), P(), P(), P(), P(), P(), P(), P())
    out_specs = P(("half", "rest"), "seq", None)
    return jax.shard_map(body, mesh=split, in_specs=in_specs, out_specs=out_specs, check_vma=False)
```

```python
import functools

import jax
import jax.numpy as jnp
from jax import lax
from jax.experimental import pallas as pl
from jax.experimental.pallas import tpu as pltpu
from jax.sharding import Mesh
from jax.sharding import PartitionSpec as P

LANES = 128


def peer_order(seq_count, rest_count):
    chips = range(0, rest_count, 2) if rest_count % 2 == 0 else ()
    peers = [(b, a + core) for a in chips for b in range(seq_count) for core in (1, 0)]
    if not peers:
        peers = [(b, a) for a in range(rest_count) for b in range(seq_count)]
    return peers[-2:-1] + peers[:-2] + peers[-1:]


def partner(at, rest_count):
    return at ^ 1 if rest_count % 2 == 0 else at


def project_kernel(
    seq_count,
    half_count,
    rest_count,
    align_hbm,
    gain_hbm,
    offset_hbm,
    left_w_hbm,
    left_b_hbm,
    right_w_hbm,
    right_b_hbm,
    send_ref,
    align_ref,
    gain_ref,
    offset_ref,
    left_w_ref,
    left_b_ref,
    right_w_ref,
    right_b_ref,
    proj_ref,
    left_ref,
    sems,
):
    copies = [
        pltpu.make_async_copy(source, target, sems.at[n])
        for n, (source, target) in enumerate(
            [
                (align_hbm, align_ref),
                (gain_hbm, gain_ref),
                (offset_hbm, offset_ref),
                (left_w_hbm, left_w_ref),
                (left_b_hbm, left_b_ref),
                (right_w_hbm, right_w_ref),
                (right_b_hbm, right_b_ref),
            ]
        )
    ]
    for copy in copies:
        copy.start()
    for copy in copies:
        copy.wait()
    rows, res_total, chan = align_ref.shape
    hidden = left_w_ref.shape[0]
    copies_of = LANES // (2 * hidden)
    weights = jnp.concatenate([left_w_ref[...], right_w_ref[...]] * copies_of, axis=0)
    scaled = (weights.astype(jnp.float32) * gain_ref[...]).astype(jnp.bfloat16)
    inner = (((1,), (1,)), ((), ()))
    offset = jnp.broadcast_to(offset_ref[...], (8, chan))
    high = offset.astype(jnp.bfloat16)
    low = (offset - high.astype(jnp.float32)).astype(jnp.bfloat16)
    shift = (
        lax.dot_general(high, weights, inner, preferred_element_type=jnp.float32)
        + lax.dot_general(low, weights, inner, preferred_element_type=jnp.float32)
    )[:1] + jnp.concatenate([left_b_ref[...], right_b_ref[...]] * copies_of, axis=1)
    flat, factors = [], []
    for row in range(rows):
        values = align_ref[row].astype(jnp.float32)
        centred = values - jnp.mean(values, axis=-1, keepdims=True)
        spread = jnp.mean(centred * centred, axis=-1, keepdims=True)
        flat.append(centred.astype(jnp.bfloat16))
        factors.append(lax.rsqrt(spread + 1e-05))
    product = lax.dot_general(
        jnp.concatenate(flat, axis=0), scaled, inner, preferred_element_type=jnp.float32
    )
    for row, factor in enumerate(factors):
        place = slice(row * res_total, (row + 1) * res_total)
        proj_ref[place, :] = product[place] * factor + shift
    tiles = [proj_ref[pl.ds(r, rows, stride=res_total), :] for r in range(res_total)]
    moved = {}
    lane_block = lax.broadcasted_iota(jnp.int32, (rows, LANES), 1) // hidden
    per_group = LANES // hidden

    def lined_up(side, residues):
        lines = []
        for at in range(0, len(residues), per_group):
            line = None
            for p, r in enumerate(residues[at : at + per_group]):
                if (p - side) % 2 == 0:
                    tile = tiles[r]
                else:
                    if r not in moved:
                        moved[r] = pltpu.roll(tiles[r], hidden, 1)
                    tile = moved[r]
                line = tile if line is None else jnp.where(lane_block == p, tile, line)
            lines.append(line)
        return jnp.concatenate(lines, axis=1)

    row_block = res_total // (half_count * rest_count)
    col_block = res_total // seq_count
    order = column_order(col_block, per_group)
    for a in range(half_count * rest_count):
        left_ref[a] = lined_up(0, [a * row_block + i for i in range(row_block)])
    right = [lined_up(1, [b * col_block + j for j in order]) for b in range(seq_count)]
    half = lax.axis_index("half")
    own = [left_ref[half * rest_count + a] for a in range(rest_count)]
    other = [left_ref[(1 - half) * rest_count + partner(a, rest_count)] for a in range(rest_count)]
    lefts = [jnp.concatenate([own[a], other[a]], axis=1) for a in range(rest_count)]
    peers = peer_order(seq_count, rest_count)
    split = lefts[0].shape[1]
    group = max(1, 16 // rows)
    packed = {}

    def pack(blocks, picks):
        if picks not in packed:
            block = jnp.concatenate([blocks[at] for _, at in picks], axis=0)
            packed[picks] = block.astype(jnp.bfloat16)
        return packed[picks]

    for start in range(0, len(peers), group):
        block = peers[start : start + group]
        place = pl.ds(start * rows, group * rows)
        send_ref[place, :split] = pack(lefts, tuple(("left", a) for _, a in block))
        send_ref[place, split:] = pack(right, tuple(("right", b) for b, _ in block))


def pair_terms(own, hidden, row_block, col_block, recv_ref, weight_ref, left_ref):
    seqs = recv_ref.shape[0]
    split = row_block * hidden
    left = recv_ref[:, :split] if own else recv_ref[:, split : 2 * split]
    right = recv_ref[:, 2 * split :]
    turned = left.T.astype(jnp.float32)
    parts = left_ref.shape[0]
    for n in range(parts):
        left_ref[n] = turned[:, n * LANES : (n + 1) * LANES]
    left = jnp.concatenate(
        [
            jnp.concatenate(
                [left_ref[n, pl.ds(c, row_block, stride=hidden), :] for n in range(parts)], axis=1
            )
            for c in range(hidden)
        ],
        axis=0,
    ).astype(jnp.bfloat16)
    per_group = LANES // hidden
    lane_block = lax.broadcasted_iota(jnp.int32, (2 * row_block, LANES), 1) // hidden
    rows = []
    for g in range(0, col_block // per_group, 2):
        outer = jnp.dot(
            left, right[:, g * LANES : (g + 2) * LANES], preferred_element_type=jnp.float32
        )
        lines = [[] for _ in range(per_group)]
        for c in range(0, hidden, per_group):
            tiles = []
            for k in range(per_group):
                at = (c + k) * row_block
                tile = jnp.concatenate(
                    [
                        outer[at : at + row_block, h * LANES : (h + 1) * LANES]
                        for h in range(2)
                    ],
                    axis=0,
                )
                tiles.append(tile.astype(jnp.bfloat16))
            step = per_group // 2
            while step:
                upper = lane_block // step % 2 == 1
                for k in range(per_group):
                    if k // step % 2 == 0:
                        low, high = tiles[k], tiles[k + step]
                        tiles[k] = jnp.where(upper, roll_blocks(high, step, hidden), low)
                        tiles[k + step] = jnp.where(upper, high, roll_blocks(low, -step, hidden))
                step //= 2
            for j in range(per_group):
                lines[j].append(tiles[j])
        rows += [jnp.concatenate(line, axis=1) for line in lines]
    flat = jnp.concatenate(rows, axis=0)
    term = jnp.dot(flat, weight_ref[...], preferred_element_type=jnp.float32)
    return term * (1.0 / float(2 * seqs))


def swaps_late():
    return (lax.axis_index("seq") < lax.axis_size("seq") - 1) & (
        lax.axis_index("rest") // 2 % 2 == 1
    )


def theirs_kernel(sizes, recv_ref, weight_ref, theirs_ref, early_ref, left_ref):
    @pl.when(swaps_late())
    def _():
        early_ref[...] = pair_terms(True, *sizes, recv_ref, weight_ref, left_ref)

    theirs_ref[...] = pair_terms(False, *sizes, recv_ref, weight_ref, left_ref).astype(
        theirs_ref.dtype
    )


def mine_kernel(
    sizes, recv_ref, weight_ref, early_ref, bias_hbm, mine_ref, left_ref, bias_ref, sem
):
    bias = pltpu.make_async_copy(bias_hbm, bias_ref, sem)
    bias.start()
    late = swaps_late()

    @pl.when(late)
    def _():
        mine_ref[...] = early_ref[...]

    @pl.when(jnp.logical_not(late))
    def _():
        mine_ref[...] = pair_terms(True, *sizes, recv_ref, weight_ref, left_ref)

    bias.wait()
    mine_ref[...] += bias_ref[...]


def roll_blocks(tile, count, hidden):
    shift = count * hidden % LANES
    return pltpu.roll(tile, shift, 1) if shift else tile


def column_order(col_block, per_group):
    double = 2 * per_group
    return [
        double * (p // double) + 2 * (p % per_group) + (p // per_group) % 2 for p in range(col_block)
    ]


def add_kernel(mine_ref, came_ref, out_ref, term_ref):
    row_block, col_block, _ = out_ref.shape
    term_ref[...] = mine_ref[...] + came_ref[...].astype(jnp.float32)
    for i in range(row_block):
        out_ref[i] = term_ref[pl.ds(i, col_block, stride=row_block), :].astype(jnp.bfloat16)


def in_hbm(array):
    return pltpu.with_memory_space_constraint(array, pltpu.HBM)


def body(
    alignment,
    layer_norm_gain,
    layer_norm_bias,
    left_projection_weight,
    left_bias,
    right_projection_weight,
    right_bias,
    out_weight,
    out_bias,
):
    seq_count = lax.axis_size("seq")
    half_count = lax.axis_size("half")
    rest_count = lax.axis_size("rest")
    rows, res_total, chan = alignment.shape
    hidden = left_projection_weight.shape[1]
    pair_width = out_weight.shape[1]
    row_block = res_total // (half_count * rest_count)
    col_block = res_total // seq_count
    peers = seq_count * rest_count
    width = (half_count * row_block + col_block) * hidden
    pairs = row_block * col_block
    vmem = pl.BlockSpec(memory_space=pltpu.VMEM)
    hbm = pl.BlockSpec(memory_space=pltpu.HBM)
    params = pltpu.CompilerParams(vmem_limit_bytes=32 * 1024 * 1024)
    send = pl.pallas_call(
        functools.partial(project_kernel, seq_count, half_count, rest_count),
        out_shape=jax.ShapeDtypeStruct((peers * rows, width), jnp.bfloat16),
        in_specs=[hbm] * 7,
        out_specs=vmem,
        scratch_shapes=[
            pltpu.VMEM((rows, res_total, chan), jnp.bfloat16),
            pltpu.VMEM((1, chan), jnp.float32),
            pltpu.VMEM((1, chan), jnp.float32),
            pltpu.VMEM((hidden, chan), jnp.bfloat16),
            pltpu.VMEM((1, hidden), jnp.float32),
            pltpu.VMEM((hidden, chan), jnp.bfloat16),
            pltpu.VMEM((1, hidden), jnp.float32),
            pltpu.VMEM((rows * res_total, LANES), jnp.float32),
            pltpu.VMEM((half_count * rest_count, rows, row_block * hidden), jnp.float32),
            pltpu.SemaphoreType.DMA((7,)),
        ],
        compiler_params=params,
    )(
        in_hbm(alignment),
        in_hbm(layer_norm_gain.reshape(1, chan)),
        in_hbm(layer_norm_bias.reshape(1, chan)),
        in_hbm(left_projection_weight.T),
        in_hbm(left_bias.reshape(1, hidden)),
        in_hbm(right_projection_weight.T),
        in_hbm(right_bias.reshape(1, hidden)),
    )
    groups = [
        [(b * half_count + h) * rest_count + a for b, a in peer_order(seq_count, rest_count)]
        for h in range(half_count)
    ]
    recv = lax.all_to_all(
        send,
        ("seq", "half", "rest"),
        split_axis=0,
        concat_axis=0,
        tiled=True,
        axis_index_groups=groups,
    )
    sizes = (hidden, row_block, col_block)
    outer_values = pairs * hidden * hidden
    cost = pl.CostEstimate(
        flops=2 * outer_values * (recv.shape[0] + pair_width),
        bytes_accessed=2 * (recv.size + out_weight.size),
        transcendentals=0,
    )
    turned = pltpu.VMEM((recv.shape[0] // LANES, row_block * hidden, LANES), jnp.float32)
    term = jax.ShapeDtypeStruct((pairs, pair_width), jnp.float32)
    theirs, early = pl.pallas_call(
        functools.partial(theirs_kernel, sizes),
        out_shape=[jax.ShapeDtypeStruct((pairs, pair_width), jnp.bfloat16), term],
        in_specs=[vmem] * 2,
        out_specs=[vmem] * 2,
        scratch_shapes=[turned],
        compiler_params=params,
        cost_estimate=cost,
    )(recv, out_weight)
    swap = [
        (h * rest_count + q, (1 - h) * rest_count + partner(q, rest_count))
        for h in range(half_count)
        for q in range(rest_count)
    ]
    came = lax.ppermute(theirs, ("half", "rest"), swap)
    mine = pl.pallas_call(
        functools.partial(mine_kernel, sizes),
        out_shape=term,
        in_specs=[vmem, vmem, vmem, hbm],
        out_specs=vmem,
        scratch_shapes=[
            turned,
            pltpu.VMEM((1, pair_width), jnp.float32),
            pltpu.SemaphoreType.DMA,
        ],
        compiler_params=params,
        cost_estimate=cost,
    )(recv, out_weight, early, in_hbm(out_bias.reshape(1, pair_width)))
    return pl.pallas_call(
        add_kernel,
        out_shape=jax.ShapeDtypeStruct((row_block, col_block, pair_width), jnp.bfloat16),
        in_specs=[vmem] * 2,
        out_specs=vmem,
        scratch_shapes=[pltpu.VMEM((pairs, pair_width), jnp.float32)],
        compiler_params=params,
    )(mine, came)


def solution(mesh):
    seq_count, res_count = mesh.devices.shape
    split = Mesh(mesh.devices.reshape(seq_count, 2, res_count // 2), ("seq", "half", "rest"))
    in_specs = (P(("seq", "half", "rest"), None, None), P(), P(), P(), P(), P(), P(), P(), P())
    out_specs = P(("half", "rest"), "seq", None)
    return jax.shard_map(body, mesh=split, in_specs=in_specs, out_specs=out_specs, check_vma=False)
```

```python
import functools

import jax
import jax.numpy as jnp
from jax import lax
from jax.experimental import pallas as pl
from jax.experimental.pallas import tpu as pltpu
from jax.sharding import Mesh
from jax.sharding import PartitionSpec as P

LANES = 128


def peer_order(seq_count, rest_count):
    chips = range(0, rest_count, 2) if rest_count % 2 == 0 else ()
    peers = [(b, a + core) for a in chips for b in range(seq_count) for core in (1, 0)]
    if not peers:
        peers = [(b, a) for a in range(rest_count) for b in range(seq_count)]
    first = (seq_count - 1, min(1, rest_count - 1))
    return [first] + [peer for peer in peers if peer != first]


def partner(at, rest_count):
    return at ^ 1 if rest_count % 2 == 0 else at


def project_kernel(
    seq_count,
    half_count,
    rest_count,
    align_hbm,
    gain_hbm,
    offset_hbm,
    left_w_hbm,
    left_b_hbm,
    right_w_hbm,
    right_b_hbm,
    send_ref,
    align_ref,
    gain_ref,
    offset_ref,
    left_w_ref,
    left_b_ref,
    right_w_ref,
    right_b_ref,
    proj_ref,
    left_ref,
    sems,
):
    copies = [
        pltpu.make_async_copy(source, target, sems.at[n])
        for n, (source, target) in enumerate(
            [
                (align_hbm, align_ref),
                (gain_hbm, gain_ref),
                (offset_hbm, offset_ref),
                (left_w_hbm, left_w_ref),
                (left_b_hbm, left_b_ref),
                (right_w_hbm, right_w_ref),
                (right_b_hbm, right_b_ref),
            ]
        )
    ]
    for copy in copies:
        copy.start()
    for copy in copies:
        copy.wait()
    rows, res_total, chan = align_ref.shape
    hidden = left_w_ref.shape[0]
    copies_of = LANES // (2 * hidden)
    weights = jnp.concatenate([left_w_ref[...], right_w_ref[...]] * copies_of, axis=0)
    scaled = (weights.astype(jnp.float32) * gain_ref[...]).astype(jnp.bfloat16)
    inner = (((1,), (1,)), ((), ()))
    offset = jnp.broadcast_to(offset_ref[...], (8, chan))
    high = offset.astype(jnp.bfloat16)
    low = (offset - high.astype(jnp.float32)).astype(jnp.bfloat16)
    shift = (
        lax.dot_general(high, weights, inner, preferred_element_type=jnp.float32)
        + lax.dot_general(low, weights, inner, preferred_element_type=jnp.float32)
    )[:1] + jnp.concatenate([left_b_ref[...], right_b_ref[...]] * copies_of, axis=1)
    flat, factors = [], []
    for row in range(rows):
        values = align_ref[row].astype(jnp.float32)
        centred = values - jnp.mean(values, axis=-1, keepdims=True)
        spread = jnp.mean(centred * centred, axis=-1, keepdims=True)
        flat.append(centred.astype(jnp.bfloat16))
        factors.append(lax.rsqrt(spread + 1e-05))
    product = lax.dot_general(
        jnp.concatenate(flat, axis=0), scaled, inner, preferred_element_type=jnp.float32
    )
    for row, factor in enumerate(factors):
        place = slice(row * res_total, (row + 1) * res_total)
        proj_ref[place, :] = product[place] * factor + shift
    tiles = [proj_ref[pl.ds(r, rows, stride=res_total), :] for r in range(res_total)]
    moved = {}
    lane_block = lax.broadcasted_iota(jnp.int32, (rows, LANES), 1) // hidden
    per_group = LANES // hidden

    def lined_up(side, residues):
        lines = []
        for at in range(0, len(residues), per_group):
            line = None
            for p, r in enumerate(residues[at : at + per_group]):
                if (p - side) % 2 == 0:
                    tile = tiles[r]
                else:
                    if r not in moved:
                        moved[r] = pltpu.roll(tiles[r], hidden, 1)
                    tile = moved[r]
                line = tile if line is None else jnp.where(lane_block == p, tile, line)
            lines.append(line)
        return jnp.concatenate(lines, axis=1)

    row_block = res_total // (half_count * rest_count)
    col_block = res_total // seq_count
    order = column_order(col_block, per_group)
    for a in range(half_count * rest_count):
        left_ref[a] = lined_up(0, [a * row_block + i for i in range(row_block)])
    right = [lined_up(1, [b * col_block + j for j in order]) for b in range(seq_count)]
    half = lax.axis_index("half")
    own = [left_ref[half * rest_count + a] for a in range(rest_count)]
    other = [left_ref[(1 - half) * rest_count + partner(a, rest_count)] for a in range(rest_count)]
    lefts = [jnp.concatenate([own[a], other[a]], axis=1) for a in range(rest_count)]
    peers = peer_order(seq_count, rest_count)
    split = lefts[0].shape[1]
    group = max(1, 16 // rows)
    packed = {}

    def pack(blocks, picks):
        if picks not in packed:
            block = jnp.concatenate([blocks[at] for _, at in picks], axis=0)
            packed[picks] = block.astype(jnp.bfloat16)
        return packed[picks]

    for start in range(0, len(peers), group):
        block = peers[start : start + group]
        place = pl.ds(start * rows, group * rows)
        send_ref[place, :split] = pack(lefts, tuple(("left", a) for _, a in block))
        send_ref[place, split:] = pack(right, tuple(("right", b) for b, _ in block))


def pair_terms(own, hidden, row_block, col_block, recv_ref, weight_ref, left_ref):
    seqs = recv_ref.shape[0]
    split = row_block * hidden
    left = recv_ref[:, :split] if own else recv_ref[:, split : 2 * split]
    right = recv_ref[:, 2 * split :]
    turned = left.T.astype(jnp.float32)
    parts = left_ref.shape[0]
    for n in range(parts):
        left_ref[n] = turned[:, n * LANES : (n + 1) * LANES]
    left = jnp.concatenate(
        [
            jnp.concatenate(
                [left_ref[n, pl.ds(c, row_block, stride=hidden), :] for n in range(parts)], axis=1
            )
            for c in range(hidden)
        ],
        axis=0,
    ).astype(jnp.bfloat16)
    per_group = LANES // hidden
    lane_block = lax.broadcasted_iota(jnp.int32, (2 * row_block, LANES), 1) // hidden
    rows = []
    for g in range(0, col_block // per_group, 2):
        outer = jnp.dot(
            left, right[:, g * LANES : (g + 2) * LANES], preferred_element_type=jnp.float32
        )
        lines = [[] for _ in range(per_group)]
        for c in range(0, hidden, per_group):
            rolled = []
            for k in range(per_group):
                at = (c + k) * row_block
                tile = jnp.concatenate(
                    [
                        outer[at : at + row_block, h * LANES : (h + 1) * LANES]
                        for h in range(2)
                    ],
                    axis=0,
                )
                rolled.append(roll_blocks(tile.astype(jnp.bfloat16), k, hidden))
            for j in range(per_group):
                mixed = rolled[(per_group - 1 - j) % per_group]
                for p in range(per_group - 1):
                    mixed = jnp.where(lane_block == p, rolled[(p - j) % per_group], mixed)
                lines[j].append(roll_blocks(mixed, -j, hidden))
        rows += [jnp.concatenate(line, axis=1) for line in lines]
    flat = jnp.concatenate(rows, axis=0)
    term = jnp.dot(flat, weight_ref[...], preferred_element_type=jnp.float32)
    return term * (1.0 / float(2 * seqs))


def swaps_late():
    return (lax.axis_index("seq") < lax.axis_size("seq") - 1) & (
        lax.axis_index("rest") // 2 % 2 == 1
    )


def theirs_kernel(sizes, recv_ref, weight_ref, theirs_ref, early_ref, left_ref):
    @pl.when(swaps_late())
    def _():
        early_ref[...] = pair_terms(True, *sizes, recv_ref, weight_ref, left_ref)

    theirs_ref[...] = pair_terms(False, *sizes, recv_ref, weight_ref, left_ref).astype(
        theirs_ref.dtype
    )


def mine_kernel(
    sizes, recv_ref, weight_ref, early_ref, bias_hbm, mine_ref, left_ref, bias_ref, sem
):
    bias = pltpu.make_async_copy(bias_hbm, bias_ref, sem)
    bias.start()
    late = swaps_late()

    @pl.when(late)
    def _():
        mine_ref[...] = early_ref[...]

    @pl.when(jnp.logical_not(late))
    def _():
        mine_ref[...] = pair_terms(True, *sizes, recv_ref, weight_ref, left_ref)

    bias.wait()
    mine_ref[...] += bias_ref[...]


def roll_blocks(tile, count, hidden):
    shift = count * hidden % LANES
    return pltpu.roll(tile, shift, 1) if shift else tile


def column_order(col_block, per_group):
    double = 2 * per_group
    return [
        double * (p // double) + 2 * (p % per_group) + (p // per_group) % 2 for p in range(col_block)
    ]


def add_kernel(mine_ref, came_ref, out_ref, term_ref):
    row_block, col_block, _ = out_ref.shape
    term_ref[...] = mine_ref[...] + came_ref[...].astype(jnp.float32)
    for i in range(row_block):
        out_ref[i] = term_ref[pl.ds(i, col_block, stride=row_block), :].astype(jnp.bfloat16)


def in_hbm(array):
    return pltpu.with_memory_space_constraint(array, pltpu.HBM)


def body(
    alignment,
    layer_norm_gain,
    layer_norm_bias,
    left_projection_weight,
    left_bias,
    right_projection_weight,
    right_bias,
    out_weight,
    out_bias,
):
    seq_count = lax.axis_size("seq")
    half_count = lax.axis_size("half")
    rest_count = lax.axis_size("rest")
    rows, res_total, chan = alignment.shape
    hidden = left_projection_weight.shape[1]
    pair_width = out_weight.shape[1]
    row_block = res_total // (half_count * rest_count)
    col_block = res_total // seq_count
    peers = seq_count * rest_count
    width = (half_count * row_block + col_block) * hidden
    pairs = row_block * col_block
    vmem = pl.BlockSpec(memory_space=pltpu.VMEM)
    hbm = pl.BlockSpec(memory_space=pltpu.HBM)
    params = pltpu.CompilerParams(vmem_limit_bytes=32 * 1024 * 1024)
    send = pl.pallas_call(
        functools.partial(project_kernel, seq_count, half_count, rest_count),
        out_shape=jax.ShapeDtypeStruct((peers * rows, width), jnp.bfloat16),
        in_specs=[hbm] * 7,
        out_specs=vmem,
        scratch_shapes=[
            pltpu.VMEM((rows, res_total, chan), jnp.bfloat16),
            pltpu.VMEM((1, chan), jnp.float32),
            pltpu.VMEM((1, chan), jnp.float32),
            pltpu.VMEM((hidden, chan), jnp.bfloat16),
            pltpu.VMEM((1, hidden), jnp.float32),
            pltpu.VMEM((hidden, chan), jnp.bfloat16),
            pltpu.VMEM((1, hidden), jnp.float32),
            pltpu.VMEM((rows * res_total, LANES), jnp.float32),
            pltpu.VMEM((half_count * rest_count, rows, row_block * hidden), jnp.float32),
            pltpu.SemaphoreType.DMA((7,)),
        ],
        compiler_params=params,
    )(
        in_hbm(alignment),
        in_hbm(layer_norm_gain.reshape(1, chan)),
        in_hbm(layer_norm_bias.reshape(1, chan)),
        in_hbm(left_projection_weight.T),
        in_hbm(left_bias.reshape(1, hidden)),
        in_hbm(right_projection_weight.T),
        in_hbm(right_bias.reshape(1, hidden)),
    )
    groups = [
        [(b * half_count + h) * rest_count + a for b, a in peer_order(seq_count, rest_count)]
        for h in range(half_count)
    ]
    recv = lax.all_to_all(
        send,
        ("seq", "half", "rest"),
        split_axis=0,
        concat_axis=0,
        tiled=True,
        axis_index_groups=groups,
    )
    sizes = (hidden, row_block, col_block)
    outer_values = pairs * hidden * hidden
    cost = pl.CostEstimate(
        flops=2 * outer_values * (recv.shape[0] + pair_width),
        bytes_accessed=2 * (recv.size + out_weight.size),
        transcendentals=0,
    )
    turned = pltpu.VMEM((recv.shape[0] // LANES, row_block * hidden, LANES), jnp.float32)
    term = jax.ShapeDtypeStruct((pairs, pair_width), jnp.float32)
    theirs, early = pl.pallas_call(
        functools.partial(theirs_kernel, sizes),
        out_shape=[jax.ShapeDtypeStruct((pairs, pair_width), jnp.bfloat16), term],
        in_specs=[vmem] * 2,
        out_specs=[vmem] * 2,
        scratch_shapes=[turned],
        compiler_params=params,
        cost_estimate=cost,
    )(recv, out_weight)
    swap = [
        (h * rest_count + q, (1 - h) * rest_count + partner(q, rest_count))
        for h in range(half_count)
        for q in range(rest_count)
    ]
    came = lax.ppermute(theirs, ("half", "rest"), swap)
    mine = pl.pallas_call(
        functools.partial(mine_kernel, sizes),
        out_shape=term,
        in_specs=[vmem, vmem, vmem, hbm],
        out_specs=vmem,
        scratch_shapes=[
            turned,
            pltpu.VMEM((1, pair_width), jnp.float32),
            pltpu.SemaphoreType.DMA,
        ],
        compiler_params=params,
        cost_estimate=cost,
    )(recv, out_weight, early, in_hbm(out_bias.reshape(1, pair_width)))
    return pl.pallas_call(
        add_kernel,
        out_shape=jax.ShapeDtypeStruct((row_block, col_block, pair_width), jnp.bfloat16),
        in_specs=[vmem] * 2,
        out_specs=vmem,
        scratch_shapes=[pltpu.VMEM((pairs, pair_width), jnp.float32)],
        compiler_params=params,
    )(mine, came)


def solution(mesh):
    seq_count, res_count = mesh.devices.shape
    split = Mesh(mesh.devices.reshape(seq_count, 2, res_count // 2), ("seq", "half", "rest"))
    in_specs = (P(("seq", "half", "rest"), None, None), P(), P(), P(), P(), P(), P(), P(), P())
    out_specs = P(("half", "rest"), "seq", None)
    return jax.shard_map(body, mesh=split, in_specs=in_specs, out_specs=out_specs, check_vma=False)
```

```python
import functools

import jax
import jax.numpy as jnp
from jax import lax
from jax.experimental import pallas as pl
from jax.experimental.pallas import tpu as pltpu
from jax.sharding import Mesh
from jax.sharding import PartitionSpec as P

LANES = 128


def peer_order(seq_count, rest_count):
    chips = range(0, rest_count, 2) if rest_count % 2 == 0 else ()
    peers = [(b, a + core) for a in chips for b in range(seq_count) for core in (1, 0)]
    if not peers:
        peers = [(b, a) for a in range(rest_count) for b in range(seq_count)]
    return peers[-1:] + peers[:-1]


def partner(at, rest_count):
    return at ^ 1 if rest_count % 2 == 0 else at


def project_kernel(
    seq_count,
    half_count,
    rest_count,
    align_hbm,
    gain_hbm,
    offset_hbm,
    left_w_hbm,
    left_b_hbm,
    right_w_hbm,
    right_b_hbm,
    send_ref,
    align_ref,
    gain_ref,
    offset_ref,
    left_w_ref,
    left_b_ref,
    right_w_ref,
    right_b_ref,
    proj_ref,
    left_ref,
    sems,
):
    copies = [
        pltpu.make_async_copy(source, target, sems.at[n])
        for n, (source, target) in enumerate(
            [
                (align_hbm, align_ref),
                (gain_hbm, gain_ref),
                (offset_hbm, offset_ref),
                (left_w_hbm, left_w_ref),
                (left_b_hbm, left_b_ref),
                (right_w_hbm, right_w_ref),
                (right_b_hbm, right_b_ref),
            ]
        )
    ]
    for copy in copies:
        copy.start()
    for copy in copies:
        copy.wait()
    rows, res_total, chan = align_ref.shape
    hidden = left_w_ref.shape[0]
    copies_of = LANES // (2 * hidden)
    weights = jnp.concatenate([left_w_ref[...], right_w_ref[...]] * copies_of, axis=0)
    scaled = (weights.astype(jnp.float32) * gain_ref[...]).astype(jnp.bfloat16)
    inner = (((1,), (1,)), ((), ()))
    offset = jnp.broadcast_to(offset_ref[...], (8, chan))
    high = offset.astype(jnp.bfloat16)
    low = (offset - high.astype(jnp.float32)).astype(jnp.bfloat16)
    shift = (
        lax.dot_general(high, weights, inner, preferred_element_type=jnp.float32)
        + lax.dot_general(low, weights, inner, preferred_element_type=jnp.float32)
    )[:1] + jnp.concatenate([left_b_ref[...], right_b_ref[...]] * copies_of, axis=1)
    flat, factors = [], []
    for row in range(rows):
        values = align_ref[row].astype(jnp.float32)
        centred = values - jnp.mean(values, axis=-1, keepdims=True)
        spread = jnp.mean(centred * centred, axis=-1, keepdims=True)
        flat.append(centred.astype(jnp.bfloat16))
        factors.append(lax.rsqrt(spread + 1e-05))
    product = lax.dot_general(
        jnp.concatenate(flat, axis=0), scaled, inner, preferred_element_type=jnp.float32
    )
    for row, factor in enumerate(factors):
        place = slice(row * res_total, (row + 1) * res_total)
        proj_ref[place, :] = product[place] * factor + shift
    tiles = [proj_ref[pl.ds(r, rows, stride=res_total), :] for r in range(res_total)]
    moved = {}
    lane_block = lax.broadcasted_iota(jnp.int32, (rows, LANES), 1) // hidden
    per_group = LANES // hidden

    def lined_up(side, residues):
        lines = []
        for at in range(0, len(residues), per_group):
            line = None
            for p, r in enumerate(residues[at : at + per_group]):
                if (p - side) % 2 == 0:
                    tile = tiles[r]
                else:
                    if r not in moved:
                        moved[r] = pltpu.roll(tiles[r], hidden, 1)
                    tile = moved[r]
                line = tile if line is None else jnp.where(lane_block == p, tile, line)
            lines.append(line)
        return jnp.concatenate(lines, axis=1)

    row_block = res_total // (half_count * rest_count)
    col_block = res_total // seq_count
    order = column_order(col_block, per_group)
    for a in range(half_count * rest_count):
        left_ref[a] = lined_up(0, [a * row_block + i for i in range(row_block)])
    right = [lined_up(1, [b * col_block + j for j in order]) for b in range(seq_count)]
    half = lax.axis_index("half")
    own = [left_ref[half * rest_count + a] for a in range(rest_count)]
    other = [left_ref[(1 - half) * rest_count + partner(a, rest_count)] for a in range(rest_count)]
    lefts = [jnp.concatenate([own[a], other[a]], axis=1) for a in range(rest_count)]
    peers = peer_order(seq_count, rest_count)
    split = lefts[0].shape[1]
    group = max(1, 16 // rows)
    packed = {}

    def pack(blocks, picks):
        if picks not in packed:
            block = jnp.concatenate([blocks[at] for _, at in picks], axis=0)
            packed[picks] = block.astype(jnp.bfloat16)
        return packed[picks]

    for start in range(0, len(peers), group):
        block = peers[start : start + group]
        place = pl.ds(start * rows, group * rows)
        send_ref[place, :split] = pack(lefts, tuple(("left", a) for _, a in block))
        send_ref[place, split:] = pack(right, tuple(("right", b) for b, _ in block))


def pair_terms(own, hidden, row_block, col_block, recv_ref, weight_ref, left_ref):
    seqs = recv_ref.shape[0]
    split = row_block * hidden
    left = recv_ref[:, :split] if own else recv_ref[:, split : 2 * split]
    right = recv_ref[:, 2 * split :]
    turned = left.T.astype(jnp.float32)
    parts = left_ref.shape[0]
    for n in range(parts):
        left_ref[n] = turned[:, n * LANES : (n + 1) * LANES]
    left = jnp.concatenate(
        [
            jnp.concatenate(
                [left_ref[n, pl.ds(c, row_block, stride=hidden), :] for n in range(parts)], axis=1
            )
            for c in range(hidden)
        ],
        axis=0,
    ).astype(jnp.bfloat16)
    per_group = LANES // hidden
    lane_block = lax.broadcasted_iota(jnp.int32, (2 * row_block, LANES), 1) // hidden
    rows = []
    for g in range(0, col_block // per_group, 2):
        outer = jnp.dot(
            left, right[:, g * LANES : (g + 2) * LANES], preferred_element_type=jnp.float32
        )
        lines = [[] for _ in range(per_group)]
        for c in range(0, hidden, per_group):
            rolled = []
            for k in range(per_group):
                at = (c + k) * row_block
                tile = jnp.concatenate(
                    [
                        outer[at : at + row_block, h * LANES : (h + 1) * LANES]
                        for h in range(2)
                    ],
                    axis=0,
                )
                rolled.append(roll_blocks(tile.astype(jnp.bfloat16), k, hidden))
            for j in range(per_group):
                mixed = rolled[(per_group - 1 - j) % per_group]
                for p in range(per_group - 1):
                    mixed = jnp.where(lane_block == p, rolled[(p - j) % per_group], mixed)
                lines[j].append(roll_blocks(mixed, -j, hidden))
        rows += [jnp.concatenate(line, axis=1) for line in lines]
    flat = jnp.concatenate(rows, axis=0)
    term = jnp.dot(flat, weight_ref[...], preferred_element_type=jnp.float32)
    return term * (1.0 / float(2 * seqs))


def swaps_late():
    return (lax.axis_index("seq") < lax.axis_size("seq") - 1) & (
        lax.axis_index("rest") // 2 % 2 == 1
    )


def theirs_kernel(sizes, recv_ref, weight_ref, theirs_ref, early_ref, left_ref):
    @pl.when(swaps_late())
    def _():
        early_ref[...] = pair_terms(True, *sizes, recv_ref, weight_ref, left_ref)

    theirs_ref[...] = pair_terms(False, *sizes, recv_ref, weight_ref, left_ref).astype(
        theirs_ref.dtype
    )


def mine_kernel(
    sizes, recv_ref, weight_ref, early_ref, bias_hbm, mine_ref, left_ref, bias_ref, sem
):
    bias = pltpu.make_async_copy(bias_hbm, bias_ref, sem)
    bias.start()
    late = swaps_late()

    @pl.when(late)
    def _():
        mine_ref[...] = early_ref[...]

    @pl.when(jnp.logical_not(late))
    def _():
        mine_ref[...] = pair_terms(True, *sizes, recv_ref, weight_ref, left_ref)

    bias.wait()
    mine_ref[...] += bias_ref[...]


def roll_blocks(tile, count, hidden):
    shift = count * hidden % LANES
    return pltpu.roll(tile, shift, 1) if shift else tile


def column_order(col_block, per_group):
    double = 2 * per_group
    return [
        double * (p // double) + 2 * (p % per_group) + (p // per_group) % 2 for p in range(col_block)
    ]


def add_kernel(mine_ref, came_ref, out_ref, term_ref):
    row_block, col_block, _ = out_ref.shape
    term_ref[...] = mine_ref[...] + came_ref[...].astype(jnp.float32)
    for i in range(row_block):
        out_ref[i] = term_ref[pl.ds(i, col_block, stride=row_block), :].astype(jnp.bfloat16)


def in_hbm(array):
    return pltpu.with_memory_space_constraint(array, pltpu.HBM)


def body(
    alignment,
    layer_norm_gain,
    layer_norm_bias,
    left_projection_weight,
    left_bias,
    right_projection_weight,
    right_bias,
    out_weight,
    out_bias,
):
    seq_count = lax.axis_size("seq")
    half_count = lax.axis_size("half")
    rest_count = lax.axis_size("rest")
    rows, res_total, chan = alignment.shape
    hidden = left_projection_weight.shape[1]
    pair_width = out_weight.shape[1]
    row_block = res_total // (half_count * rest_count)
    col_block = res_total // seq_count
    peers = seq_count * rest_count
    width = (half_count * row_block + col_block) * hidden
    pairs = row_block * col_block
    vmem = pl.BlockSpec(memory_space=pltpu.VMEM)
    hbm = pl.BlockSpec(memory_space=pltpu.HBM)
    params = pltpu.CompilerParams(vmem_limit_bytes=32 * 1024 * 1024)
    send = pl.pallas_call(
        functools.partial(project_kernel, seq_count, half_count, rest_count),
        out_shape=jax.ShapeDtypeStruct((peers * rows, width), jnp.bfloat16),
        in_specs=[hbm] * 7,
        out_specs=vmem,
        scratch_shapes=[
            pltpu.VMEM((rows, res_total, chan), jnp.bfloat16),
            pltpu.VMEM((1, chan), jnp.float32),
            pltpu.VMEM((1, chan), jnp.float32),
            pltpu.VMEM((hidden, chan), jnp.bfloat16),
            pltpu.VMEM((1, hidden), jnp.float32),
            pltpu.VMEM((hidden, chan), jnp.bfloat16),
            pltpu.VMEM((1, hidden), jnp.float32),
            pltpu.VMEM((rows * res_total, LANES), jnp.float32),
            pltpu.VMEM((half_count * rest_count, rows, row_block * hidden), jnp.float32),
            pltpu.SemaphoreType.DMA((7,)),
        ],
        compiler_params=params,
    )(
        in_hbm(alignment),
        in_hbm(layer_norm_gain.reshape(1, chan)),
        in_hbm(layer_norm_bias.reshape(1, chan)),
        in_hbm(left_projection_weight.T),
        in_hbm(left_bias.reshape(1, hidden)),
        in_hbm(right_projection_weight.T),
        in_hbm(right_bias.reshape(1, hidden)),
    )
    groups = [
        [(b * half_count + h) * rest_count + a for b, a in peer_order(seq_count, rest_count)]
        for h in range(half_count)
    ]
    recv = lax.all_to_all(
        send,
        ("seq", "half", "rest"),
        split_axis=0,
        concat_axis=0,
        tiled=True,
        axis_index_groups=groups,
    )
    sizes = (hidden, row_block, col_block)
    outer_values = pairs * hidden * hidden
    cost = pl.CostEstimate(
        flops=2 * outer_values * (recv.shape[0] + pair_width),
        bytes_accessed=2 * (recv.size + out_weight.size),
        transcendentals=0,
    )
    turned = pltpu.VMEM((recv.shape[0] // LANES, row_block * hidden, LANES), jnp.float32)
    term = jax.ShapeDtypeStruct((pairs, pair_width), jnp.float32)
    theirs, early = pl.pallas_call(
        functools.partial(theirs_kernel, sizes),
        out_shape=[jax.ShapeDtypeStruct((pairs, pair_width), jnp.bfloat16), term],
        in_specs=[vmem] * 2,
        out_specs=[vmem] * 2,
        scratch_shapes=[turned],
        compiler_params=params,
        cost_estimate=cost,
    )(recv, out_weight)
    swap = [
        (h * rest_count + q, (1 - h) * rest_count + partner(q, rest_count))
        for h in range(half_count)
        for q in range(rest_count)
    ]
    came = lax.ppermute(theirs, ("half", "rest"), swap)
    mine = pl.pallas_call(
        functools.partial(mine_kernel, sizes),
        out_shape=term,
        in_specs=[vmem, vmem, vmem, hbm],
        out_specs=vmem,
        scratch_shapes=[
            turned,
            pltpu.VMEM((1, pair_width), jnp.float32),
            pltpu.SemaphoreType.DMA,
        ],
        compiler_params=params,
        cost_estimate=cost,
    )(recv, out_weight, early, in_hbm(out_bias.reshape(1, pair_width)))
    return pl.pallas_call(
        add_kernel,
        out_shape=jax.ShapeDtypeStruct((row_block, col_block, pair_width), jnp.bfloat16),
        in_specs=[vmem] * 2,
        out_specs=vmem,
        scratch_shapes=[pltpu.VMEM((pairs, pair_width), jnp.float32)],
        compiler_params=params,
    )(mine, came)


def solution(mesh):
    seq_count, res_count = mesh.devices.shape
    split = Mesh(mesh.devices.reshape(seq_count, 2, res_count // 2), ("seq", "half", "rest"))
    in_specs = (P(("seq", "half", "rest"), None, None), P(), P(), P(), P(), P(), P(), P(), P())
    out_specs = P(("half", "rest"), "seq", None)
    return jax.shard_map(body, mesh=split, in_specs=in_specs, out_specs=out_specs, check_vma=False)
```

```python
import functools

import jax
import jax.numpy as jnp
from jax import lax
from jax.experimental import pallas as pl
from jax.experimental.pallas import tpu as pltpu
from jax.sharding import Mesh
from jax.sharding import PartitionSpec as P

LANES = 128


def peer_order(seq_count, rest_count):
    chips = range(0, rest_count, 2) if rest_count % 2 == 0 else ()
    peers = [(b, a + core) for a in chips for core in (1, 0) for b in range(seq_count)]
    if not peers:
        peers = [(b, a) for a in range(rest_count) for b in range(seq_count)]
    first = (seq_count - 1, rest_count - 1)
    return [first] + [peer for peer in peers if peer != first]


def partner(at, rest_count):
    return at ^ 1 if rest_count % 2 == 0 else at


def project_kernel(
    seq_count,
    half_count,
    rest_count,
    align_hbm,
    gain_hbm,
    offset_hbm,
    left_w_hbm,
    left_b_hbm,
    right_w_hbm,
    right_b_hbm,
    send_ref,
    align_ref,
    gain_ref,
    offset_ref,
    left_w_ref,
    left_b_ref,
    right_w_ref,
    right_b_ref,
    proj_ref,
    left_ref,
    sems,
):
    copies = [
        pltpu.make_async_copy(source, target, sems.at[n])
        for n, (source, target) in enumerate(
            [
                (align_hbm, align_ref),
                (gain_hbm, gain_ref),
                (offset_hbm, offset_ref),
                (left_w_hbm, left_w_ref),
                (left_b_hbm, left_b_ref),
                (right_w_hbm, right_w_ref),
                (right_b_hbm, right_b_ref),
            ]
        )
    ]
    for copy in copies:
        copy.start()
    for copy in copies:
        copy.wait()
    rows, res_total, chan = align_ref.shape
    hidden = left_w_ref.shape[0]
    copies_of = LANES // (2 * hidden)
    weights = jnp.concatenate([left_w_ref[...], right_w_ref[...]] * copies_of, axis=0)
    scaled = (weights.astype(jnp.float32) * gain_ref[...]).astype(jnp.bfloat16)
    inner = (((1,), (1,)), ((), ()))
    offset = jnp.broadcast_to(offset_ref[...], (8, chan))
    high = offset.astype(jnp.bfloat16)
    low = (offset - high.astype(jnp.float32)).astype(jnp.bfloat16)
    shift = (
        lax.dot_general(high, weights, inner, preferred_element_type=jnp.float32)
        + lax.dot_general(low, weights, inner, preferred_element_type=jnp.float32)
    )[:1] + jnp.concatenate([left_b_ref[...], right_b_ref[...]] * copies_of, axis=1)
    flat, factors = [], []
    for row in range(rows):
        values = align_ref[row].astype(jnp.float32)
        centred = values - jnp.mean(values, axis=-1, keepdims=True)
        spread = jnp.mean(centred * centred, axis=-1, keepdims=True)
        flat.append(centred.astype(jnp.bfloat16))
        factors.append(lax.rsqrt(spread + 1e-05))
    product = lax.dot_general(
        jnp.concatenate(flat, axis=0), scaled, inner, preferred_element_type=jnp.float32
    )
    for row, factor in enumerate(factors):
        place = slice(row * res_total, (row + 1) * res_total)
        proj_ref[place, :] = product[place] * factor + shift
    tiles = [proj_ref[pl.ds(r, rows, stride=res_total), :] for r in range(res_total)]
    moved = {}
    lane_block = lax.broadcasted_iota(jnp.int32, (rows, LANES), 1) // hidden
    per_group = LANES // hidden

    def lined_up(side, residues):
        lines = []
        for at in range(0, len(residues), per_group):
            line = None
            for p, r in enumerate(residues[at : at + per_group]):
                if (p - side) % 2 == 0:
                    tile = tiles[r]
                else:
                    if r not in moved:
                        moved[r] = pltpu.roll(tiles[r], hidden, 1)
                    tile = moved[r]
                line = tile if line is None else jnp.where(lane_block == p, tile, line)
            lines.append(line)
        return jnp.concatenate(lines, axis=1)

    row_block = res_total // (half_count * rest_count)
    col_block = res_total // seq_count
    order = column_order(col_block, per_group)
    for a in range(half_count * rest_count):
        left_ref[a] = lined_up(0, [a * row_block + i for i in range(row_block)])
    right = [lined_up(1, [b * col_block + j for j in order]) for b in range(seq_count)]
    half = lax.axis_index("half")
    own = [left_ref[half * rest_count + a] for a in range(rest_count)]
    other = [left_ref[(1 - half) * rest_count + partner(a, rest_count)] for a in range(rest_count)]
    lefts = [jnp.concatenate([own[a], other[a]], axis=1) for a in range(rest_count)]
    peers = peer_order(seq_count, rest_count)
    split = lefts[0].shape[1]
    group = max(1, 16 // rows)
    packed = {}

    def pack(blocks, picks):
        if picks not in packed:
            block = jnp.concatenate([blocks[at] for _, at in picks], axis=0)
            packed[picks] = block.astype(jnp.bfloat16)
        return packed[picks]

    for start in range(0, len(peers), group):
        block = peers[start : start + group]
        place = pl.ds(start * rows, group * rows)
        send_ref[place, :split] = pack(lefts, tuple(("left", a) for _, a in block))
        send_ref[place, split:] = pack(right, tuple(("right", b) for b, _ in block))


def pair_terms(own, hidden, row_block, col_block, recv_ref, weight_ref, left_ref):
    seqs = recv_ref.shape[0]
    split = row_block * hidden
    left = recv_ref[:, :split] if own else recv_ref[:, split : 2 * split]
    right = recv_ref[:, 2 * split :]
    turned = left.T.astype(jnp.float32)
    parts = left_ref.shape[0]
    for n in range(parts):
        left_ref[n] = turned[:, n * LANES : (n + 1) * LANES]
    left = jnp.concatenate(
        [
            jnp.concatenate(
                [left_ref[n, pl.ds(c, row_block, stride=hidden), :] for n in range(parts)], axis=1
            )
            for c in range(hidden)
        ],
        axis=0,
    ).astype(jnp.bfloat16)
    per_group = LANES // hidden
    lane_block = lax.broadcasted_iota(jnp.int32, (2 * row_block, LANES), 1) // hidden
    rows = []
    for g in range(0, col_block // per_group, 2):
        outer = jnp.dot(
            left, right[:, g * LANES : (g + 2) * LANES], preferred_element_type=jnp.float32
        )
        lines = [[] for _ in range(per_group)]
        for c in range(0, hidden, per_group):
            rolled = []
            for k in range(per_group):
                at = (c + k) * row_block
                tile = jnp.concatenate(
                    [
                        outer[at : at + row_block, h * LANES : (h + 1) * LANES]
                        for h in range(2)
                    ],
                    axis=0,
                )
                rolled.append(roll_blocks(tile.astype(jnp.bfloat16), k, hidden))
            for j in range(per_group):
                mixed = rolled[(per_group - 1 - j) % per_group]
                for p in range(per_group - 1):
                    mixed = jnp.where(lane_block == p, rolled[(p - j) % per_group], mixed)
                lines[j].append(roll_blocks(mixed, -j, hidden))
        rows += [jnp.concatenate(line, axis=1) for line in lines]
    flat = jnp.concatenate(rows, axis=0)
    term = jnp.dot(flat, weight_ref[...], preferred_element_type=jnp.float32)
    return term * (1.0 / float(2 * seqs))


def swaps_late():
    return (lax.axis_index("seq") < lax.axis_size("seq") - 1) & (
        lax.axis_index("rest") // 2 % 2 == 1
    )


def theirs_kernel(sizes, recv_ref, weight_ref, theirs_ref, early_ref, left_ref):
    @pl.when(swaps_late())
    def _():
        early_ref[...] = pair_terms(True, *sizes, recv_ref, weight_ref, left_ref)

    theirs_ref[...] = pair_terms(False, *sizes, recv_ref, weight_ref, left_ref).astype(
        theirs_ref.dtype
    )


def mine_kernel(
    sizes, recv_ref, weight_ref, early_ref, bias_hbm, mine_ref, left_ref, bias_ref, sem
):
    bias = pltpu.make_async_copy(bias_hbm, bias_ref, sem)
    bias.start()
    late = swaps_late()

    @pl.when(late)
    def _():
        mine_ref[...] = early_ref[...]

    @pl.when(jnp.logical_not(late))
    def _():
        mine_ref[...] = pair_terms(True, *sizes, recv_ref, weight_ref, left_ref)

    bias.wait()
    mine_ref[...] += bias_ref[...]


def roll_blocks(tile, count, hidden):
    shift = count * hidden % LANES
    return pltpu.roll(tile, shift, 1) if shift else tile


def column_order(col_block, per_group):
    double = 2 * per_group
    return [
        double * (p // double) + 2 * (p % per_group) + (p // per_group) % 2 for p in range(col_block)
    ]


def add_kernel(mine_ref, came_ref, out_ref, term_ref):
    row_block, col_block, _ = out_ref.shape
    term_ref[...] = mine_ref[...] + came_ref[...].astype(jnp.float32)
    for i in range(row_block):
        out_ref[i] = term_ref[pl.ds(i, col_block, stride=row_block), :].astype(jnp.bfloat16)


def in_hbm(array):
    return pltpu.with_memory_space_constraint(array, pltpu.HBM)


def body(
    alignment,
    layer_norm_gain,
    layer_norm_bias,
    left_projection_weight,
    left_bias,
    right_projection_weight,
    right_bias,
    out_weight,
    out_bias,
):
    seq_count = lax.axis_size("seq")
    half_count = lax.axis_size("half")
    rest_count = lax.axis_size("rest")
    rows, res_total, chan = alignment.shape
    hidden = left_projection_weight.shape[1]
    pair_width = out_weight.shape[1]
    row_block = res_total // (half_count * rest_count)
    col_block = res_total // seq_count
    peers = seq_count * rest_count
    width = (half_count * row_block + col_block) * hidden
    pairs = row_block * col_block
    vmem = pl.BlockSpec(memory_space=pltpu.VMEM)
    hbm = pl.BlockSpec(memory_space=pltpu.HBM)
    params = pltpu.CompilerParams(vmem_limit_bytes=32 * 1024 * 1024)
    send = pl.pallas_call(
        functools.partial(project_kernel, seq_count, half_count, rest_count),
        out_shape=jax.ShapeDtypeStruct((peers * rows, width), jnp.bfloat16),
        in_specs=[hbm] * 7,
        out_specs=vmem,
        scratch_shapes=[
            pltpu.VMEM((rows, res_total, chan), jnp.bfloat16),
            pltpu.VMEM((1, chan), jnp.float32),
            pltpu.VMEM((1, chan), jnp.float32),
            pltpu.VMEM((hidden, chan), jnp.bfloat16),
            pltpu.VMEM((1, hidden), jnp.float32),
            pltpu.VMEM((hidden, chan), jnp.bfloat16),
            pltpu.VMEM((1, hidden), jnp.float32),
            pltpu.VMEM((rows * res_total, LANES), jnp.float32),
            pltpu.VMEM((half_count * rest_count, rows, row_block * hidden), jnp.float32),
            pltpu.SemaphoreType.DMA((7,)),
        ],
        compiler_params=params,
    )(
        in_hbm(alignment),
        in_hbm(layer_norm_gain.reshape(1, chan)),
        in_hbm(layer_norm_bias.reshape(1, chan)),
        in_hbm(left_projection_weight.T),
        in_hbm(left_bias.reshape(1, hidden)),
        in_hbm(right_projection_weight.T),
        in_hbm(right_bias.reshape(1, hidden)),
    )
    groups = [
        [(b * half_count + h) * rest_count + a for b, a in peer_order(seq_count, rest_count)]
        for h in range(half_count)
    ]
    recv = lax.all_to_all(
        send,
        ("seq", "half", "rest"),
        split_axis=0,
        concat_axis=0,
        tiled=True,
        axis_index_groups=groups,
    )
    sizes = (hidden, row_block, col_block)
    outer_values = pairs * hidden * hidden
    cost = pl.CostEstimate(
        flops=2 * outer_values * (recv.shape[0] + pair_width),
        bytes_accessed=2 * (recv.size + out_weight.size),
        transcendentals=0,
    )
    turned = pltpu.VMEM((recv.shape[0] // LANES, row_block * hidden, LANES), jnp.float32)
    term = jax.ShapeDtypeStruct((pairs, pair_width), jnp.float32)
    theirs, early = pl.pallas_call(
        functools.partial(theirs_kernel, sizes),
        out_shape=[jax.ShapeDtypeStruct((pairs, pair_width), jnp.bfloat16), term],
        in_specs=[vmem] * 2,
        out_specs=[vmem] * 2,
        scratch_shapes=[turned],
        compiler_params=params,
        cost_estimate=cost,
    )(recv, out_weight)
    swap = [
        (h * rest_count + q, (1 - h) * rest_count + partner(q, rest_count))
        for h in range(half_count)
        for q in range(rest_count)
    ]
    came = lax.ppermute(theirs, ("half", "rest"), swap)
    mine = pl.pallas_call(
        functools.partial(mine_kernel, sizes),
        out_shape=term,
        in_specs=[vmem, vmem, vmem, hbm],
        out_specs=vmem,
        scratch_shapes=[
            turned,
            pltpu.VMEM((1, pair_width), jnp.float32),
            pltpu.SemaphoreType.DMA,
        ],
        compiler_params=params,
        cost_estimate=cost,
    )(recv, out_weight, early, in_hbm(out_bias.reshape(1, pair_width)))
    return pl.pallas_call(
        add_kernel,
        out_shape=jax.ShapeDtypeStruct((row_block, col_block, pair_width), jnp.bfloat16),
        in_specs=[vmem] * 2,
        out_specs=vmem,
        scratch_shapes=[pltpu.VMEM((pairs, pair_width), jnp.float32)],
        compiler_params=params,
    )(mine, came)


def solution(mesh):
    seq_count, res_count = mesh.devices.shape
    split = Mesh(mesh.devices.reshape(seq_count, 2, res_count // 2), ("seq", "half", "rest"))
    in_specs = (P(("seq", "half", "rest"), None, None), P(), P(), P(), P(), P(), P(), P(), P())
    out_specs = P(("half", "rest"), "seq", None)
    return jax.shard_map(body, mesh=split, in_specs=in_specs, out_specs=out_specs, check_vma=False)
```

```python
import functools

import jax
import jax.numpy as jnp
from jax import lax
from jax.experimental import pallas as pl
from jax.experimental.pallas import tpu as pltpu
from jax.sharding import Mesh
from jax.sharding import PartitionSpec as P

LANES = 128


def peer_order(seq_count, rest_count):
    chips = range(0, rest_count, 2) if rest_count % 2 == 0 else ()
    peers = [(b, a + core) for a in chips for b in range(seq_count) for core in (1, 0)]
    if not peers:
        peers = [(b, a) for a in range(rest_count) for b in range(seq_count)]
    return peers[-2:-1] + peers[:-2] + peers[-1:]


def partner(at, rest_count):
    return at ^ 1 if rest_count % 2 == 0 else at


def project_kernel(
    seq_count,
    half_count,
    rest_count,
    align_hbm,
    gain_hbm,
    offset_hbm,
    left_w_hbm,
    left_b_hbm,
    right_w_hbm,
    right_b_hbm,
    send_ref,
    align_ref,
    gain_ref,
    offset_ref,
    left_w_ref,
    left_b_ref,
    right_w_ref,
    right_b_ref,
    proj_ref,
    left_ref,
    sems,
):
    copies = [
        pltpu.make_async_copy(source, target, sems.at[n])
        for n, (source, target) in enumerate(
            [
                (align_hbm, align_ref),
                (gain_hbm, gain_ref),
                (offset_hbm, offset_ref),
                (left_w_hbm, left_w_ref),
                (left_b_hbm, left_b_ref),
                (right_w_hbm, right_w_ref),
                (right_b_hbm, right_b_ref),
            ]
        )
    ]
    for copy in copies:
        copy.start()
    for copy in copies:
        copy.wait()
    rows, res_total, chan = align_ref.shape
    hidden = left_w_ref.shape[0]
    copies_of = LANES // (2 * hidden)
    weights = jnp.concatenate([left_w_ref[...], right_w_ref[...]] * copies_of, axis=0)
    scaled = (weights.astype(jnp.float32) * gain_ref[...]).astype(jnp.bfloat16)
    inner = (((1,), (1,)), ((), ()))
    offset = jnp.broadcast_to(offset_ref[...], (8, chan))
    high = offset.astype(jnp.bfloat16)
    low = (offset - high.astype(jnp.float32)).astype(jnp.bfloat16)
    shift = (
        lax.dot_general(high, weights, inner, preferred_element_type=jnp.float32)
        + lax.dot_general(low, weights, inner, preferred_element_type=jnp.float32)
    )[:1] + jnp.concatenate([left_b_ref[...], right_b_ref[...]] * copies_of, axis=1)
    flat, factors = [], []
    for row in range(rows):
        values = align_ref[row].astype(jnp.float32)
        centred = values - jnp.mean(values, axis=-1, keepdims=True)
        spread = jnp.mean(centred * centred, axis=-1, keepdims=True)
        flat.append(centred.astype(jnp.bfloat16))
        factors.append(lax.rsqrt(spread + 1e-05))
    product = lax.dot_general(
        jnp.concatenate(flat, axis=0), scaled, inner, preferred_element_type=jnp.float32
    )
    for row, factor in enumerate(factors):
        place = slice(row * res_total, (row + 1) * res_total)
        proj_ref[place, :] = product[place] * factor + shift
    tiles = [proj_ref[pl.ds(r, rows, stride=res_total), :] for r in range(res_total)]
    moved = {}
    lane_block = lax.broadcasted_iota(jnp.int32, (rows, LANES), 1) // hidden
    per_group = LANES // hidden

    def lined_up(side, residues):
        lines = []
        for at in range(0, len(residues), per_group):
            line = None
            for p, r in enumerate(residues[at : at + per_group]):
                if (p - side) % 2 == 0:
                    tile = tiles[r]
                else:
                    if r not in moved:
                        moved[r] = pltpu.roll(tiles[r], hidden, 1)
                    tile = moved[r]
                line = tile if line is None else jnp.where(lane_block == p, tile, line)
            lines.append(line)
        return jnp.concatenate(lines, axis=1)

    row_block = res_total // (half_count * rest_count)
    col_block = res_total // seq_count
    order = column_order(col_block, per_group)
    for a in range(half_count * rest_count):
        left_ref[a] = lined_up(0, [a * row_block + i for i in range(row_block)])
    right = [lined_up(1, [b * col_block + j for j in order]) for b in range(seq_count)]
    half = lax.axis_index("half")
    own = [left_ref[half * rest_count + a] for a in range(rest_count)]
    other = [left_ref[(1 - half) * rest_count + partner(a, rest_count)] for a in range(rest_count)]
    lefts = [jnp.concatenate([own[a], other[a]], axis=1) for a in range(rest_count)]
    peers = peer_order(seq_count, rest_count)
    split = lefts[0].shape[1]
    group = max(1, 16 // rows)
    packed = {}

    def pack(blocks, picks):
        if picks not in packed:
            block = jnp.concatenate([blocks[at] for _, at in picks], axis=0)
            packed[picks] = block.astype(jnp.bfloat16)
        return packed[picks]

    for start in range(0, len(peers), group):
        block = peers[start : start + group]
        place = pl.ds(start * rows, group * rows)
        send_ref[place, :split] = pack(lefts, tuple(("left", a) for _, a in block))
        send_ref[place, split:] = pack(right, tuple(("right", b) for b, _ in block))


def pair_terms(own, hidden, row_block, col_block, recv_ref, weight_ref, left_ref):
    seqs = recv_ref.shape[0]
    split = row_block * hidden
    left = recv_ref[:, :split] if own else recv_ref[:, split : 2 * split]
    right = recv_ref[:, 2 * split :]
    turned = left.T.astype(jnp.float32)
    parts = left_ref.shape[0]
    for n in range(parts):
        left_ref[n] = turned[:, n * LANES : (n + 1) * LANES]
    left = jnp.concatenate(
        [
            jnp.concatenate(
                [left_ref[n, pl.ds(c, row_block, stride=hidden), :] for n in range(parts)], axis=1
            )
            for c in range(hidden)
        ],
        axis=0,
    ).astype(jnp.bfloat16)
    per_group = LANES // hidden
    lane_block = lax.broadcasted_iota(jnp.int32, (2 * row_block, LANES), 1) // hidden
    rows = []
    for g in range(0, col_block // per_group, 2):
        outer = jnp.dot(
            left, right[:, g * LANES : (g + 2) * LANES], preferred_element_type=jnp.float32
        )
        lines = [[] for _ in range(per_group)]
        for c in range(0, hidden, per_group):
            rolled = []
            for k in range(per_group):
                at = (c + k) * row_block
                tile = jnp.concatenate(
                    [
                        outer[at : at + row_block, h * LANES : (h + 1) * LANES]
                        for h in range(2)
                    ],
                    axis=0,
                )
                rolled.append(roll_blocks(tile.astype(jnp.bfloat16), k, hidden))
            for j in range(per_group):
                mixed = rolled[(per_group - 1 - j) % per_group]
                for p in range(per_group - 1):
                    mixed = jnp.where(lane_block == p, rolled[(p - j) % per_group], mixed)
                lines[j].append(roll_blocks(mixed, -j, hidden))
        rows += [jnp.concatenate(line, axis=1) for line in lines]
    flat = jnp.concatenate(rows, axis=0)
    term = jnp.dot(flat, weight_ref[...], preferred_element_type=jnp.float32)
    return term * (1.0 / float(2 * seqs))


def swaps_late():
    return (
        (lax.axis_index("half") == 1)
        & (lax.axis_index("seq") < lax.axis_size("seq") - 1)
        & (lax.axis_index("rest") // 2 % 2 == 1)
    )


def theirs_kernel(sizes, recv_ref, weight_ref, theirs_ref, early_ref, left_ref):
    @pl.when(swaps_late())
    def _():
        early_ref[...] = pair_terms(True, *sizes, recv_ref, weight_ref, left_ref)

    theirs_ref[...] = pair_terms(False, *sizes, recv_ref, weight_ref, left_ref).astype(
        theirs_ref.dtype
    )


def mine_kernel(
    sizes, recv_ref, weight_ref, early_ref, bias_hbm, mine_ref, left_ref, bias_ref, sem
):
    bias = pltpu.make_async_copy(bias_hbm, bias_ref, sem)
    bias.start()
    late = swaps_late()

    @pl.when(late)
    def _():
        mine_ref[...] = early_ref[...]

    @pl.when(jnp.logical_not(late))
    def _():
        mine_ref[...] = pair_terms(True, *sizes, recv_ref, weight_ref, left_ref)

    bias.wait()
    mine_ref[...] += bias_ref[...]


def roll_blocks(tile, count, hidden):
    shift = count * hidden % LANES
    return pltpu.roll(tile, shift, 1) if shift else tile


def column_order(col_block, per_group):
    double = 2 * per_group
    return [
        double * (p // double) + 2 * (p % per_group) + (p // per_group) % 2 for p in range(col_block)
    ]


def add_kernel(mine_ref, came_ref, out_ref, term_ref):
    row_block, col_block, _ = out_ref.shape
    term_ref[...] = mine_ref[...] + came_ref[...].astype(jnp.float32)
    for i in range(row_block):
        out_ref[i] = term_ref[pl.ds(i, col_block, stride=row_block), :].astype(jnp.bfloat16)


def in_hbm(array):
    return pltpu.with_memory_space_constraint(array, pltpu.HBM)


def body(
    alignment,
    layer_norm_gain,
    layer_norm_bias,
    left_projection_weight,
    left_bias,
    right_projection_weight,
    right_bias,
    out_weight,
    out_bias,
):
    seq_count = lax.axis_size("seq")
    half_count = lax.axis_size("half")
    rest_count = lax.axis_size("rest")
    rows, res_total, chan = alignment.shape
    hidden = left_projection_weight.shape[1]
    pair_width = out_weight.shape[1]
    row_block = res_total // (half_count * rest_count)
    col_block = res_total // seq_count
    peers = seq_count * rest_count
    width = (half_count * row_block + col_block) * hidden
    pairs = row_block * col_block
    vmem = pl.BlockSpec(memory_space=pltpu.VMEM)
    hbm = pl.BlockSpec(memory_space=pltpu.HBM)
    params = pltpu.CompilerParams(vmem_limit_bytes=32 * 1024 * 1024)
    send = pl.pallas_call(
        functools.partial(project_kernel, seq_count, half_count, rest_count),
        out_shape=jax.ShapeDtypeStruct((peers * rows, width), jnp.bfloat16),
        in_specs=[hbm] * 7,
        out_specs=vmem,
        scratch_shapes=[
            pltpu.VMEM((rows, res_total, chan), jnp.bfloat16),
            pltpu.VMEM((1, chan), jnp.float32),
            pltpu.VMEM((1, chan), jnp.float32),
            pltpu.VMEM((hidden, chan), jnp.bfloat16),
            pltpu.VMEM((1, hidden), jnp.float32),
            pltpu.VMEM((hidden, chan), jnp.bfloat16),
            pltpu.VMEM((1, hidden), jnp.float32),
            pltpu.VMEM((rows * res_total, LANES), jnp.float32),
            pltpu.VMEM((half_count * rest_count, rows, row_block * hidden), jnp.float32),
            pltpu.SemaphoreType.DMA((7,)),
        ],
        compiler_params=params,
    )(
        in_hbm(alignment),
        in_hbm(layer_norm_gain.reshape(1, chan)),
        in_hbm(layer_norm_bias.reshape(1, chan)),
        in_hbm(left_projection_weight.T),
        in_hbm(left_bias.reshape(1, hidden)),
        in_hbm(right_projection_weight.T),
        in_hbm(right_bias.reshape(1, hidden)),
    )
    groups = [
        [(b * half_count + h) * rest_count + a for b, a in peer_order(seq_count, rest_count)]
        for h in range(half_count)
    ]
    recv = lax.all_to_all(
        send,
        ("seq", "half", "rest"),
        split_axis=0,
        concat_axis=0,
        tiled=True,
        axis_index_groups=groups,
    )
    sizes = (hidden, row_block, col_block)
    outer_values = pairs * hidden * hidden
    cost = pl.CostEstimate(
        flops=2 * outer_values * (recv.shape[0] + pair_width),
        bytes_accessed=2 * (recv.size + out_weight.size),
        transcendentals=0,
    )
    turned = pltpu.VMEM((recv.shape[0] // LANES, row_block * hidden, LANES), jnp.float32)
    term = jax.ShapeDtypeStruct((pairs, pair_width), jnp.float32)
    theirs, early = pl.pallas_call(
        functools.partial(theirs_kernel, sizes),
        out_shape=[jax.ShapeDtypeStruct((pairs, pair_width), jnp.bfloat16), term],
        in_specs=[vmem] * 2,
        out_specs=[vmem] * 2,
        scratch_shapes=[turned],
        compiler_params=params,
        cost_estimate=cost,
    )(recv, out_weight)
    swap = [
        (h * rest_count + q, (1 - h) * rest_count + partner(q, rest_count))
        for h in range(half_count)
        for q in range(rest_count)
    ]
    came = lax.ppermute(theirs, ("half", "rest"), swap)
    mine = pl.pallas_call(
        functools.partial(mine_kernel, sizes),
        out_shape=term,
        in_specs=[vmem, vmem, vmem, hbm],
        out_specs=vmem,
        scratch_shapes=[
            turned,
            pltpu.VMEM((1, pair_width), jnp.float32),
            pltpu.SemaphoreType.DMA,
        ],
        compiler_params=params,
        cost_estimate=cost,
    )(recv, out_weight, early, in_hbm(out_bias.reshape(1, pair_width)))
    return pl.pallas_call(
        add_kernel,
        out_shape=jax.ShapeDtypeStruct((row_block, col_block, pair_width), jnp.bfloat16),
        in_specs=[vmem] * 2,
        out_specs=vmem,
        scratch_shapes=[pltpu.VMEM((pairs, pair_width), jnp.float32)],
        compiler_params=params,
    )(mine, came)


def solution(mesh):
    seq_count, res_count = mesh.devices.shape
    split = Mesh(mesh.devices.reshape(seq_count, 2, res_count // 2), ("seq", "half", "rest"))
    in_specs = (P(("seq", "half", "rest"), None, None), P(), P(), P(), P(), P(), P(), P(), P())
    out_specs = P(("half", "rest"), "seq", None)
    return jax.shard_map(body, mesh=split, in_specs=in_specs, out_specs=out_specs, check_vma=False)
```

```python
import functools

import jax
import jax.numpy as jnp
from jax import lax
from jax.experimental import pallas as pl
from jax.experimental.pallas import tpu as pltpu
from jax.sharding import Mesh
from jax.sharding import PartitionSpec as P

LANES = 128


def peer_order(seq_count, rest_count):
    chips = range(0, rest_count, 2) if rest_count % 2 == 0 else ()
    peers = [(b, a + core) for a in chips for b in range(seq_count) for core in (1, 0)]
    if not peers:
        peers = [(b, a) for a in range(rest_count) for b in range(seq_count)]
    return peers[-2:-1] + peers[:-2] + peers[-1:]


def partner(at, rest_count):
    return at ^ 1 if rest_count % 2 == 0 else at


def project_kernel(
    seq_count,
    half_count,
    rest_count,
    align_hbm,
    gain_hbm,
    offset_hbm,
    left_w_hbm,
    left_b_hbm,
    right_w_hbm,
    right_b_hbm,
    send_ref,
    align_ref,
    gain_ref,
    offset_ref,
    left_w_ref,
    left_b_ref,
    right_w_ref,
    right_b_ref,
    proj_ref,
    left_ref,
    sems,
):
    copies = [
        pltpu.make_async_copy(source, target, sems.at[n])
        for n, (source, target) in enumerate(
            [
                (align_hbm, align_ref),
                (gain_hbm, gain_ref),
                (offset_hbm, offset_ref),
                (left_w_hbm, left_w_ref),
                (left_b_hbm, left_b_ref),
                (right_w_hbm, right_w_ref),
                (right_b_hbm, right_b_ref),
            ]
        )
    ]
    for copy in copies:
        copy.start()
    for copy in copies:
        copy.wait()
    rows, res_total, chan = align_ref.shape
    hidden = left_w_ref.shape[0]
    copies_of = LANES // (2 * hidden)
    weights = jnp.concatenate([left_w_ref[...], right_w_ref[...]] * copies_of, axis=0)
    scaled = (weights.astype(jnp.float32) * gain_ref[...]).astype(jnp.bfloat16)
    inner = (((1,), (1,)), ((), ()))
    offset = jnp.broadcast_to(offset_ref[...], (8, chan))
    high = offset.astype(jnp.bfloat16)
    low = (offset - high.astype(jnp.float32)).astype(jnp.bfloat16)
    shift = (
        lax.dot_general(high, weights, inner, preferred_element_type=jnp.float32)
        + lax.dot_general(low, weights, inner, preferred_element_type=jnp.float32)
    )[:1] + jnp.concatenate([left_b_ref[...], right_b_ref[...]] * copies_of, axis=1)
    flat, factors = [], []
    for row in range(rows):
        values = align_ref[row].astype(jnp.float32)
        centred = values - jnp.mean(values, axis=-1, keepdims=True)
        spread = jnp.mean(centred * centred, axis=-1, keepdims=True)
        flat.append(centred.astype(jnp.bfloat16))
        factors.append(lax.rsqrt(spread + 1e-05))
    product = lax.dot_general(
        jnp.concatenate(flat, axis=0), scaled, inner, preferred_element_type=jnp.float32
    )
    for row, factor in enumerate(factors):
        place = slice(row * res_total, (row + 1) * res_total)
        proj_ref[place, :] = product[place] * factor + shift
    tiles = [proj_ref[pl.ds(r, rows, stride=res_total), :] for r in range(res_total)]
    moved = {}
    lane_block = lax.broadcasted_iota(jnp.int32, (rows, LANES), 1) // hidden
    per_group = LANES // hidden

    def lined_up(side, residues):
        lines = []
        for at in range(0, len(residues), per_group):
            line = None
            for p, r in enumerate(residues[at : at + per_group]):
                if (p - side) % 2 == 0:
                    tile = tiles[r]
                else:
                    if r not in moved:
                        moved[r] = pltpu.roll(tiles[r], hidden, 1)
                    tile = moved[r]
                line = tile if line is None else jnp.where(lane_block == p, tile, line)
            lines.append(line)
        return jnp.concatenate(lines, axis=1)

    row_block = res_total // (half_count * rest_count)
    col_block = res_total // seq_count
    order = column_order(col_block, per_group)
    for a in range(half_count * rest_count):
        left_ref[a] = lined_up(0, [a * row_block + i for i in range(row_block)])
    right = [lined_up(1, [b * col_block + j for j in order]) for b in range(seq_count)]
    half = lax.axis_index("half")
    own = [left_ref[half * rest_count + a] for a in range(rest_count)]
    other = [left_ref[(1 - half) * rest_count + partner(a, rest_count)] for a in range(rest_count)]
    lefts = [jnp.concatenate([own[a], other[a]], axis=1) for a in range(rest_count)]
    peers = peer_order(seq_count, rest_count)
    split = lefts[0].shape[1]
    group = max(1, 16 // rows)
    packed = {}

    def pack(blocks, picks):
        if picks not in packed:
            block = jnp.concatenate([blocks[at] for _, at in picks], axis=0)
            packed[picks] = block.astype(jnp.bfloat16)
        return packed[picks]

    for start in range(0, len(peers), group):
        block = peers[start : start + group]
        place = pl.ds(start * rows, group * rows)
        send_ref[place, :split] = pack(lefts, tuple(("left", a) for _, a in block))
        send_ref[place, split:] = pack(right, tuple(("right", b) for b, _ in block))


def pair_terms(own, hidden, row_block, col_block, recv_ref, weight_ref):
    seqs = recv_ref.shape[0]
    split = row_block * hidden
    left = recv_ref[:, :split] if own else recv_ref[:, split : 2 * split]
    right = recv_ref[:, 2 * split :]
    turned = left.T.astype(jnp.float32).reshape(row_block, hidden, seqs)
    left = turned.swapaxes(0, 1).reshape(hidden * row_block, seqs).astype(jnp.bfloat16)
    per_group = LANES // hidden
    lane_block = lax.broadcasted_iota(jnp.int32, (2 * row_block, LANES), 1) // hidden
    rows = []
    for g in range(0, col_block // per_group, 2):
        outer = jnp.dot(
            left, right[:, g * LANES : (g + 2) * LANES], preferred_element_type=jnp.float32
        )
        lines = [[] for _ in range(per_group)]
        for c in range(0, hidden, per_group):
            rolled = []
            for k in range(per_group):
                at = (c + k) * row_block
                tile = jnp.concatenate(
                    [
                        outer[at : at + row_block, h * LANES : (h + 1) * LANES]
                        for h in range(2)
                    ],
                    axis=0,
                )
                rolled.append(roll_blocks(tile.astype(jnp.bfloat16), k, hidden))
            for j in range(per_group):
                mixed = rolled[(per_group - 1 - j) % per_group]
                for p in range(per_group - 1):
                    mixed = jnp.where(lane_block == p, rolled[(p - j) % per_group], mixed)
                lines[j].append(roll_blocks(mixed, -j, hidden))
        rows += [jnp.concatenate(line, axis=1) for line in lines]
    flat = jnp.concatenate(rows, axis=0)
    term = jnp.dot(flat, weight_ref[...], preferred_element_type=jnp.float32)
    return term * (1.0 / float(2 * seqs))


def swaps_late():
    return (
        (lax.axis_index("half") == 1)
        & (lax.axis_index("seq") < lax.axis_size("seq") - 1)
        & (lax.axis_index("rest") // 2 % 2 == 1)
    )


def theirs_kernel(sizes, recv_ref, weight_ref, theirs_ref, early_ref):
    @pl.when(swaps_late())
    def _():
        early_ref[...] = pair_terms(True, *sizes, recv_ref, weight_ref)

    theirs_ref[...] = pair_terms(False, *sizes, recv_ref, weight_ref).astype(
        theirs_ref.dtype
    )


def mine_kernel(
    sizes, recv_ref, weight_ref, early_ref, bias_hbm, mine_ref, bias_ref, sem
):
    bias = pltpu.make_async_copy(bias_hbm, bias_ref, sem)
    bias.start()
    late = swaps_late()

    @pl.when(late)
    def _():
        mine_ref[...] = early_ref[...]

    @pl.when(jnp.logical_not(late))
    def _():
        mine_ref[...] = pair_terms(True, *sizes, recv_ref, weight_ref)

    bias.wait()
    mine_ref[...] += bias_ref[...]


def roll_blocks(tile, count, hidden):
    shift = count * hidden % LANES
    return pltpu.roll(tile, shift, 1) if shift else tile


def column_order(col_block, per_group):
    double = 2 * per_group
    return [
        double * (p // double) + 2 * (p % per_group) + (p // per_group) % 2 for p in range(col_block)
    ]


def add_kernel(mine_ref, came_ref, out_ref, term_ref):
    row_block, col_block, _ = out_ref.shape
    term_ref[...] = mine_ref[...] + came_ref[...].astype(jnp.float32)
    for i in range(row_block):
        out_ref[i] = term_ref[pl.ds(i, col_block, stride=row_block), :].astype(jnp.bfloat16)


def in_hbm(array):
    return pltpu.with_memory_space_constraint(array, pltpu.HBM)


def body(
    alignment,
    layer_norm_gain,
    layer_norm_bias,
    left_projection_weight,
    left_bias,
    right_projection_weight,
    right_bias,
    out_weight,
    out_bias,
):
    seq_count = lax.axis_size("seq")
    half_count = lax.axis_size("half")
    rest_count = lax.axis_size("rest")
    rows, res_total, chan = alignment.shape
    hidden = left_projection_weight.shape[1]
    pair_width = out_weight.shape[1]
    row_block = res_total // (half_count * rest_count)
    col_block = res_total // seq_count
    peers = seq_count * rest_count
    width = (half_count * row_block + col_block) * hidden
    pairs = row_block * col_block
    vmem = pl.BlockSpec(memory_space=pltpu.VMEM)
    hbm = pl.BlockSpec(memory_space=pltpu.HBM)
    params = pltpu.CompilerParams(vmem_limit_bytes=32 * 1024 * 1024)
    send = pl.pallas_call(
        functools.partial(project_kernel, seq_count, half_count, rest_count),
        out_shape=jax.ShapeDtypeStruct((peers * rows, width), jnp.bfloat16),
        in_specs=[hbm] * 7,
        out_specs=vmem,
        scratch_shapes=[
            pltpu.VMEM((rows, res_total, chan), jnp.bfloat16),
            pltpu.VMEM((1, chan), jnp.float32),
            pltpu.VMEM((1, chan), jnp.float32),
            pltpu.VMEM((hidden, chan), jnp.bfloat16),
            pltpu.VMEM((1, hidden), jnp.float32),
            pltpu.VMEM((hidden, chan), jnp.bfloat16),
            pltpu.VMEM((1, hidden), jnp.float32),
            pltpu.VMEM((rows * res_total, LANES), jnp.float32),
            pltpu.VMEM((half_count * rest_count, rows, row_block * hidden), jnp.float32),
            pltpu.SemaphoreType.DMA((7,)),
        ],
        compiler_params=params,
    )(
        in_hbm(alignment),
        in_hbm(layer_norm_gain.reshape(1, chan)),
        in_hbm(layer_norm_bias.reshape(1, chan)),
        in_hbm(left_projection_weight.T),
        in_hbm(left_bias.reshape(1, hidden)),
        in_hbm(right_projection_weight.T),
        in_hbm(right_bias.reshape(1, hidden)),
    )
    groups = [
        [(b * half_count + h) * rest_count + a for b, a in peer_order(seq_count, rest_count)]
        for h in range(half_count)
    ]
    recv = lax.all_to_all(
        send,
        ("seq", "half", "rest"),
        split_axis=0,
        concat_axis=0,
        tiled=True,
        axis_index_groups=groups,
    )
    sizes = (hidden, row_block, col_block)
    outer_values = pairs * hidden * hidden
    cost = pl.CostEstimate(
        flops=2 * outer_values * (recv.shape[0] + pair_width),
        bytes_accessed=2 * (recv.size + out_weight.size),
        transcendentals=0,
    )
    term = jax.ShapeDtypeStruct((pairs, pair_width), jnp.float32)
    theirs, early = pl.pallas_call(
        functools.partial(theirs_kernel, sizes),
        out_shape=[jax.ShapeDtypeStruct((pairs, pair_width), jnp.bfloat16), term],
        in_specs=[vmem] * 2,
        out_specs=[vmem] * 2,
        compiler_params=params,
        cost_estimate=cost,
    )(recv, out_weight)
    swap = [
        (h * rest_count + q, (1 - h) * rest_count + partner(q, rest_count))
        for h in range(half_count)
        for q in range(rest_count)
    ]
    came = lax.ppermute(theirs, ("half", "rest"), swap)
    mine = pl.pallas_call(
        functools.partial(mine_kernel, sizes),
        out_shape=term,
        in_specs=[vmem, vmem, vmem, hbm],
        out_specs=vmem,
        scratch_shapes=[
            pltpu.VMEM((1, pair_width), jnp.float32),
            pltpu.SemaphoreType.DMA,
        ],
        compiler_params=params,
        cost_estimate=cost,
    )(recv, out_weight, early, in_hbm(out_bias.reshape(1, pair_width)))
    return pl.pallas_call(
        add_kernel,
        out_shape=jax.ShapeDtypeStruct((row_block, col_block, pair_width), jnp.bfloat16),
        in_specs=[vmem] * 2,
        out_specs=vmem,
        scratch_shapes=[pltpu.VMEM((pairs, pair_width), jnp.float32)],
        compiler_params=params,
    )(mine, came)


def solution(mesh):
    seq_count, res_count = mesh.devices.shape
    split = Mesh(mesh.devices.reshape(seq_count, 2, res_count // 2), ("seq", "half", "rest"))
    in_specs = (P(("seq", "half", "rest"), None, None), P(), P(), P(), P(), P(), P(), P(), P())
    out_specs = P(("half", "rest"), "seq", None)
    return jax.shard_map(body, mesh=split, in_specs=in_specs, out_specs=out_specs, check_vma=False)
```

```python
import functools

import jax
import jax.numpy as jnp
from jax import lax
from jax.experimental import pallas as pl
from jax.experimental.pallas import tpu as pltpu
from jax.sharding import Mesh
from jax.sharding import PartitionSpec as P

LANES = 128


def peer_order(seq_count, rest_count):
    chips = range(0, rest_count, 2) if rest_count % 2 == 0 else ()
    peers = [(b, a + core) for a in chips for b in range(seq_count) for core in (1, 0)]
    if not peers:
        peers = [(b, a) for a in range(rest_count) for b in range(seq_count)]
    return peers[-2:-1] + peers[:-2] + peers[-1:]


def partner(at, rest_count):
    return at ^ 1 if rest_count % 2 == 0 else at


def project_kernel(
    seq_count,
    half_count,
    rest_count,
    align_hbm,
    gain_hbm,
    offset_hbm,
    left_w_hbm,
    left_b_hbm,
    right_w_hbm,
    right_b_hbm,
    send_ref,
    align_ref,
    gain_ref,
    offset_ref,
    left_w_ref,
    left_b_ref,
    right_w_ref,
    right_b_ref,
    proj_ref,
    left_ref,
    sems,
):
    copies = [
        pltpu.make_async_copy(source, target, sems.at[n])
        for n, (source, target) in enumerate(
            [
                (align_hbm, align_ref),
                (gain_hbm, gain_ref),
                (offset_hbm, offset_ref),
                (left_w_hbm, left_w_ref),
                (left_b_hbm, left_b_ref),
                (right_w_hbm, right_w_ref),
                (right_b_hbm, right_b_ref),
            ]
        )
    ]
    for copy in copies:
        copy.start()
    for copy in copies:
        copy.wait()
    rows, res_total, chan = align_ref.shape
    hidden = left_w_ref.shape[0]
    copies_of = LANES // (2 * hidden)
    weights = jnp.concatenate([left_w_ref[...], right_w_ref[...]] * copies_of, axis=0)
    scaled = (weights.astype(jnp.float32) * gain_ref[...]).astype(jnp.bfloat16)
    inner = (((1,), (1,)), ((), ()))
    offset = jnp.broadcast_to(offset_ref[...], (8, chan))
    high = offset.astype(jnp.bfloat16)
    low = (offset - high.astype(jnp.float32)).astype(jnp.bfloat16)
    shift = (
        lax.dot_general(high, weights, inner, preferred_element_type=jnp.float32)
        + lax.dot_general(low, weights, inner, preferred_element_type=jnp.float32)
    )[:1] + jnp.concatenate([left_b_ref[...], right_b_ref[...]] * copies_of, axis=1)
    flat, factors = [], []
    for row in range(rows):
        values = align_ref[row].astype(jnp.float32)
        centred = values - jnp.mean(values, axis=-1, keepdims=True)
        spread = jnp.mean(centred * centred, axis=-1, keepdims=True)
        flat.append(centred.astype(jnp.bfloat16))
        factors.append(lax.rsqrt(spread + 1e-05))
    product = lax.dot_general(
        jnp.concatenate(flat, axis=0), scaled, inner, preferred_element_type=jnp.float32
    )
    for row, factor in enumerate(factors):
        place = slice(row * res_total, (row + 1) * res_total)
        proj_ref[place, :] = product[place] * factor + shift
    tiles = [proj_ref[pl.ds(r, rows, stride=res_total), :] for r in range(res_total)]
    moved = {}
    lane_block = lax.broadcasted_iota(jnp.int32, (rows, LANES), 1) // hidden
    per_group = LANES // hidden

    def lined_up(side, residues):
        lines = []
        for at in range(0, len(residues), per_group):
            line = None
            for p, r in enumerate(residues[at : at + per_group]):
                if (p - side) % 2 == 0:
                    tile = tiles[r]
                else:
                    if r not in moved:
                        moved[r] = pltpu.roll(tiles[r], hidden, 1)
                    tile = moved[r]
                line = tile if line is None else jnp.where(lane_block == p, tile, line)
            lines.append(line)
        return jnp.concatenate(lines, axis=1)

    row_block = res_total // (half_count * rest_count)
    col_block = res_total // seq_count
    order = column_order(col_block, per_group)
    for a in range(half_count * rest_count):
        left_ref[a] = lined_up(0, [a * row_block + i for i in range(row_block)])
    right = [lined_up(1, [b * col_block + j for j in order]) for b in range(seq_count)]
    half = lax.axis_index("half")
    own = [left_ref[half * rest_count + a] for a in range(rest_count)]
    other = [left_ref[(1 - half) * rest_count + partner(a, rest_count)] for a in range(rest_count)]
    lefts = [jnp.concatenate([own[a], other[a]], axis=1) for a in range(rest_count)]
    peers = peer_order(seq_count, rest_count)
    split = lefts[0].shape[1]
    group = max(1, 16 // rows)
    packed = {}

    def pack(blocks, picks):
        if picks not in packed:
            block = jnp.concatenate([blocks[at] for _, at in picks], axis=0)
            packed[picks] = block.astype(jnp.bfloat16)
        return packed[picks]

    for start in range(0, len(peers), group):
        block = peers[start : start + group]
        place = pl.ds(start * rows, group * rows)
        send_ref[place, :split] = pack(lefts, tuple(("left", a) for _, a in block))
        send_ref[place, split:] = pack(right, tuple(("right", b) for b, _ in block))


def pair_terms(own, hidden, row_block, col_block, recv_ref, weight_ref):
    seqs = recv_ref.shape[0]
    split = row_block * hidden
    left = recv_ref[:, :split] if own else recv_ref[:, split : 2 * split]
    right = recv_ref[:, 2 * split :]
    turned = left.T.astype(jnp.float32).reshape(row_block, hidden, seqs)
    left = turned.swapaxes(0, 1).reshape(hidden * row_block, seqs).astype(jnp.bfloat16)
    per_group = LANES // hidden
    lane_block = lax.broadcasted_iota(jnp.int32, (2 * row_block, LANES), 1) // hidden
    rows = []
    for g in range(0, col_block // per_group, 2):
        outer = jnp.dot(
            left, right[:, g * LANES : (g + 2) * LANES], preferred_element_type=jnp.float32
        )
        lines = [[] for _ in range(per_group)]
        for c in range(0, hidden, per_group):
            rolled = []
            for k in range(per_group):
                at = (c + k) * row_block
                tile = jnp.concatenate(
                    [
                        outer[at : at + row_block, h * LANES : (h + 1) * LANES]
                        for h in range(2)
                    ],
                    axis=0,
                )
                rolled.append(roll_blocks(tile.astype(jnp.bfloat16), k, hidden))
            for j in range(per_group):
                mixed = rolled[(per_group - 1 - j) % per_group]
                for p in range(per_group - 1):
                    mixed = jnp.where(lane_block == p, rolled[(p - j) % per_group], mixed)
                lines[j].append(roll_blocks(mixed, -j, hidden))
        rows += [jnp.concatenate(line, axis=1) for line in lines]
    flat = jnp.concatenate(rows, axis=0)
    term = jnp.dot(flat, weight_ref[...], preferred_element_type=jnp.float32)
    return term * (1.0 / float(2 * seqs))


def swaps_late():
    return (
        (lax.axis_index("half") == 1)
        & (lax.axis_index("seq") < lax.axis_size("seq") - 1)
        & (lax.axis_index("rest") // 2 % 2 == 1)
    )


def theirs_kernel(sizes, recv_ref, weight_ref, theirs_ref, early_ref):
    @pl.when(swaps_late())
    def _():
        early_ref[...] = pair_terms(True, *sizes, recv_ref, weight_ref)

    theirs_ref[...] = pair_terms(False, *sizes, recv_ref, weight_ref).astype(
        theirs_ref.dtype
    )


def mine_kernel(
    sizes, recv_ref, weight_ref, early_ref, bias_hbm, mine_ref, bias_ref, sem
):
    bias = pltpu.make_async_copy(bias_hbm, bias_ref, sem)
    bias.start()
    late = swaps_late()

    @pl.when(late)
    def _():
        mine_ref[...] = early_ref[...]

    @pl.when(jnp.logical_not(late))
    def _():
        mine_ref[...] = pair_terms(True, *sizes, recv_ref, weight_ref)

    bias.wait()
    mine_ref[...] += bias_ref[...]


def roll_blocks(tile, count, hidden):
    shift = count * hidden % LANES
    return pltpu.roll(tile, shift, 1) if shift else tile


def column_order(col_block, per_group):
    double = 2 * per_group
    return [
        double * (p // double) + 2 * (p % per_group) + (p // per_group) % 2 for p in range(col_block)
    ]


def add_kernel(mine_ref, came_ref, out_ref):
    row_block, col_block, width = out_ref.shape
    term = mine_ref[...] + came_ref[...].astype(jnp.float32)
    term = term.reshape(col_block, row_block, width).swapaxes(0, 1)
    out_ref[...] = term.astype(jnp.bfloat16)


def in_hbm(array):
    return pltpu.with_memory_space_constraint(array, pltpu.HBM)


def body(
    alignment,
    layer_norm_gain,
    layer_norm_bias,
    left_projection_weight,
    left_bias,
    right_projection_weight,
    right_bias,
    out_weight,
    out_bias,
):
    seq_count = lax.axis_size("seq")
    half_count = lax.axis_size("half")
    rest_count = lax.axis_size("rest")
    rows, res_total, chan = alignment.shape
    hidden = left_projection_weight.shape[1]
    pair_width = out_weight.shape[1]
    row_block = res_total // (half_count * rest_count)
    col_block = res_total // seq_count
    peers = seq_count * rest_count
    width = (half_count * row_block + col_block) * hidden
    pairs = row_block * col_block
    vmem = pl.BlockSpec(memory_space=pltpu.VMEM)
    hbm = pl.BlockSpec(memory_space=pltpu.HBM)
    params = pltpu.CompilerParams(vmem_limit_bytes=32 * 1024 * 1024)
    send = pl.pallas_call(
        functools.partial(project_kernel, seq_count, half_count, rest_count),
        out_shape=jax.ShapeDtypeStruct((peers * rows, width), jnp.bfloat16),
        in_specs=[hbm] * 7,
        out_specs=vmem,
        scratch_shapes=[
            pltpu.VMEM((rows, res_total, chan), jnp.bfloat16),
            pltpu.VMEM((1, chan), jnp.float32),
            pltpu.VMEM((1, chan), jnp.float32),
            pltpu.VMEM((hidden, chan), jnp.bfloat16),
            pltpu.VMEM((1, hidden), jnp.float32),
            pltpu.VMEM((hidden, chan), jnp.bfloat16),
            pltpu.VMEM((1, hidden), jnp.float32),
            pltpu.VMEM((rows * res_total, LANES), jnp.float32),
            pltpu.VMEM((half_count * rest_count, rows, row_block * hidden), jnp.float32),
            pltpu.SemaphoreType.DMA((7,)),
        ],
        compiler_params=params,
    )(
        in_hbm(alignment),
        in_hbm(layer_norm_gain.reshape(1, chan)),
        in_hbm(layer_norm_bias.reshape(1, chan)),
        in_hbm(left_projection_weight.T),
        in_hbm(left_bias.reshape(1, hidden)),
        in_hbm(right_projection_weight.T),
        in_hbm(right_bias.reshape(1, hidden)),
    )
    groups = [
        [(b * half_count + h) * rest_count + a for b, a in peer_order(seq_count, rest_count)]
        for h in range(half_count)
    ]
    recv = lax.all_to_all(
        send,
        ("seq", "half", "rest"),
        split_axis=0,
        concat_axis=0,
        tiled=True,
        axis_index_groups=groups,
    )
    sizes = (hidden, row_block, col_block)
    outer_values = pairs * hidden * hidden
    cost = pl.CostEstimate(
        flops=2 * outer_values * (recv.shape[0] + pair_width),
        bytes_accessed=2 * (recv.size + out_weight.size),
        transcendentals=0,
    )
    term = jax.ShapeDtypeStruct((pairs, pair_width), jnp.float32)
    theirs, early = pl.pallas_call(
        functools.partial(theirs_kernel, sizes),
        out_shape=[jax.ShapeDtypeStruct((pairs, pair_width), jnp.bfloat16), term],
        in_specs=[vmem] * 2,
        out_specs=[vmem] * 2,
        compiler_params=params,
        cost_estimate=cost,
    )(recv, out_weight)
    swap = [
        (h * rest_count + q, (1 - h) * rest_count + partner(q, rest_count))
        for h in range(half_count)
        for q in range(rest_count)
    ]
    came = lax.ppermute(theirs, ("half", "rest"), swap)
    mine = pl.pallas_call(
        functools.partial(mine_kernel, sizes),
        out_shape=term,
        in_specs=[vmem, vmem, vmem, hbm],
        out_specs=vmem,
        scratch_shapes=[
            pltpu.VMEM((1, pair_width), jnp.float32),
            pltpu.SemaphoreType.DMA,
        ],
        compiler_params=params,
        cost_estimate=cost,
    )(recv, out_weight, early, in_hbm(out_bias.reshape(1, pair_width)))
    return pl.pallas_call(
        add_kernel,
        out_shape=jax.ShapeDtypeStruct((row_block, col_block, pair_width), jnp.bfloat16),
        in_specs=[vmem] * 2,
        out_specs=vmem,
        compiler_params=params,
    )(mine, came)


def solution(mesh):
    seq_count, res_count = mesh.devices.shape
    split = Mesh(mesh.devices.reshape(seq_count, 2, res_count // 2), ("seq", "half", "rest"))
    in_specs = (P(("seq", "half", "rest"), None, None), P(), P(), P(), P(), P(), P(), P(), P())
    out_specs = P(("half", "rest"), "seq", None)
    return jax.shard_map(body, mesh=split, in_specs=in_specs, out_specs=out_specs, check_vma=False)
```
